32 devices in a mesh: groups: 2 (over x), rows: 16 (over z, y, core).
Axes of the slice: x: 2, y: 2, z: 4, core: 2. Of those that a mesh axis runs over, the one named last changes fastest.
Arguments:
- token_ids: int32 [1, 256], P(None, 'groups'), parts along dimension 1, may hold values from 0 to 32767
- parents: int32 [1, 8, 32], P(None, 'groups'), parts along dimension 1, may hold values from 0 to 31, as said below
- states: bfloat16 [256, 16, 128, 128], P(('groups', 'rows')), parts along dimension 0, may hold values from -1.75 to 1.75
- embed_table: bfloat16 [32768, 2048], P(None, 'rows'), may hold values from -6 to 6
- qkv_weight: bfloat16 [2048, 3, 2048], P(None, None, 'rows'), may hold values from -0.125 to 0.125
- gate_weight: float32 [16, 128], replicated, may hold values from -6 to 6
- gate_bias: float32 [16], replicated, may hold values from -2 to 3
- norm_gain: float32 [2048], replicated, may hold values from 0.1 to 1.9
- out_weight: bfloat16 [2048, 2048], P(None, 'rows'), may hold values from -0.125 to 0.125
Outputs:
- layer_out: bfloat16 [1, 256, 2048], P(None, 'groups', 'rows'), parts along dimension 1
- final_states: bfloat16 [256, 16, 128, 128], P(('groups', 'rows')), parts along dimension 0
The draws below stay inside these ranges and needn't reach their ends.
There are 2 independent parts, one for each index of `groups`. The reference program is written for one: setup_inputs(seed, part) draws one part's arguments, and reference() takes and returns one part's arrays. A program takes and returns all parts, laid end to end along the dimension named above; an argument that names none is the same for every part. Nothing has to cross between parts.
Inputs may be any that keep to these rules, and one draw needn't show every extreme that they name: The 32 beams of a user fall into 4 aligned blocks of 8. In every step and for every user, at most 2 children of one block have parents in any one other block, and in every step some user has exactly 2 children of one block with parents in another block.
All inputs are finite; a program needn't handle non-finite values.
Results may differ from the reference program's by a relative error of at most 0.0074.
Values may be sent and summed in bfloat16 or wider, within the bound.
No kernel may reach another device: no remote copies, remote signals or barrier semaphores. Data moves between devices by JAX's collectives and lax.ppermute only.
A program may use at most 64 MiB of HBM per device.

```python
import math
import jax
import jax.numpy as jnp
import numpy as np
from jax import lax

HEADS = 16
HEAD = 128
VOCAB = 32768
BEAM = 32
CAP = 2
STEPS = 1
D = 2048
R_ALL = 128
USERS = 4


def draw_parents(key, part):
    key_list = jax.random.split(jax.random.fold_in(key, 11), 6)
    row_count = BEAM // 4
    shape_four = (STEPS, USERS, 4, row_count)
    counts = jax.random.randint(key_list[0], (STEPS, USERS, 4, 3), 0, CAP + 1)
    pick_dev = jax.random.randint(key_list[1], (STEPS, USERS, 1, 1), 0, 4)
    pick_off = jax.random.randint(key_list[2], (STEPS, USERS, 1, 1), 0, 3)
    dev_index = jnp.arange(4, dtype=jnp.int32)[None, None, :, None]
    off_index = jnp.arange(3, dtype=jnp.int32)[None, None, None, :]
    counts = jnp.where((dev_index == pick_dev) & (off_index == pick_off), CAP, counts)
    limits = jnp.cumsum(counts, axis=-1)
    slot_index = jnp.arange(row_count, dtype=jnp.int32)[None, None, None, :]
    offset = jnp.where(slot_index < limits[..., 0:1], 1, jnp.where(slot_index < limits[..., 1:2], 2, jnp.where(slot_index < limits[..., 2:3], 3, 0)))
    scores = jax.random.randint(key_list[3], shape_four, 0, 1 << 20) * row_count + slot_index
    ordering = jnp.argsort(scores, axis=-1, stable=True)
    offset = jnp.take_along_axis(offset, ordering, axis=-1)
    source = jnp.bitwise_xor(dev_index, offset)
    first_draw = jax.random.randint(key_list[4], shape_four, 0, row_count)
    second = jax.random.randint(key_list[5], shape_four, 0, row_count)
    within = jnp.minimum(first_draw, second)
    return (source * row_count + within).reshape(STEPS, USERS, BEAM).astype(jnp.int32)


def place_ends(array, rng, low, top_value):
    place = [jax.random.randint(jax.random.fold_in(rng, axis), (), 0, length) for axis, length in enumerate(array.shape)]
    main_axis = array.shape.index(max(array.shape))
    neighbour = place[:main_axis] + [(place[main_axis] + 1) % array.shape[main_axis]] + place[main_axis + 1:]
    return array.at[tuple(place)].set(low).at[tuple(neighbour)].set(top_value)


def block_levels(key, dims, shards, smallest, largest):
    level, own = 1.0, jax.random.fold_in(key, 6)
    for axis_at, parts in shards:
        steps = jnp.exp(jax.random.uniform(jax.random.fold_in(own, axis_at), (parts,), jnp.float32, smallest / len(shards), largest / len(shards)))
        level = level * jnp.repeat(steps, dims[axis_at] // parts).reshape([-1 if axis == axis_at else 1 for axis in range(len(dims))])
    return level


def cumulative_ranks(number_of, skew):
    loads = [(1 << 20) // math.isqrt(rank ** skew) + 1 for rank in range(1, number_of + 1)]
    scale = 1 + sum(loads) // (1 << 30)
    return np.cumsum(np.array([max(1, weight // scale) for weight in loads]))


def ranked(own_key, extent, amount, lean):
    grid = cumulative_ranks(amount, lean)
    lot = jax.random.randint(jax.random.fold_in(own_key, 1), extent, 0, int(grid[amount - 1]))
    rank = jnp.searchsorted(jnp.asarray(grid, jnp.int32), lot, side="right")
    return jax.random.permutation(jax.random.fold_in(own_key, 2), amount)[rank].astype(jnp.int32)


def scatter_about(stream_key, dims, spread, reach, shards=(), held_as=jnp.bfloat16):
    array = spread * jax.random.normal(stream_key, dims, jnp.float32)
    if shards:
        array = array * block_levels(stream_key, dims, shards, -0.22, 0.18)
    return jnp.clip(array, -reach, reach).astype(held_as)


def setup_inputs(seed: int = 0, part: int = 0) -> dict:
    seeds = jax.random.split(jax.random.key(seed), 10)
    part_splits = jax.random.split(jax.random.fold_in(seeds[9], part), 10)
    token_ids = place_ends(ranked(part_splits[0], (STEPS, R_ALL), VOCAB, 2), jax.random.fold_in(part_splits[0], 3), 0, VOCAB - 1).astype(jnp.int32)
    parents = draw_parents(jax.random.fold_in(jax.random.fold_in(seeds[9], part), 71), part)
    states = scatter_about(part_splits[2], (R_ALL, HEADS, HEAD, HEAD), 0.3, 1.75, ((0, 16),))
    embed_table = scatter_about(seeds[3], (VOCAB, D), 1.0, 6.0, ((1, 16),))
    qkv_weight = scatter_about(seeds[4], (D, 3, D), D ** -0.5, 0.125, ((2, 16),))
    gate_weight = scatter_about(seeds[5], (HEADS, HEAD), 1.0, 6.0, (), jnp.float32)
    gate_bias = jnp.clip(jax.random.uniform(seeds[6], (HEADS,), jnp.float32, -2.0, 3.0), -2.0, 3.0)
    norm_gain = jnp.clip(1.0 + 0.18 * jax.random.normal(seeds[7], (D,), jnp.float32), 0.1, 1.9)
    out_weight = scatter_about(seeds[8], (D, D), D ** -0.5, 0.125, ((1, 16),))
    return {"token_ids": token_ids, "parents": parents, "states": states, "embed_table": embed_table, "qkv_weight": qkv_weight, "gate_weight": gate_weight, "gate_bias": gate_bias, "norm_gain": norm_gain, "out_weight": out_weight}


def reference(token_ids, parents, states, embed_table, qkv_weight, gate_weight, gate_bias, norm_gain, out_weight):
    width = HEADS * HEAD
    row_count = USERS * BEAM
    weight_flat = qkv_weight.reshape(width, 3 * width)
    state_now = states
    outputs = []
    for step_index in range(STEPS):
        inputs = jnp.take(embed_table, token_ids[step_index], axis=0)
        projected = jnp.dot(inputs, weight_flat, preferred_element_type=jnp.float32).astype(jnp.bfloat16)
        projected = projected.reshape(row_count, 3, HEADS, HEAD)
        parent_rows = (jnp.arange(USERS, dtype=jnp.int32)[:, None] * BEAM + parents[step_index]).reshape(row_count)
        prior_state = jnp.take(state_now, parent_rows, axis=0)

        def update(block):
            prior_block, proj_block = block
            queries = proj_block[:, 0].astype(jnp.float32)
            key_float = proj_block[:, 1].astype(jnp.float32)
            values = proj_block[:, 2].astype(jnp.float32)
            gate_logit = lax.optimization_barrier(jnp.sum(key_float * gate_weight, axis=-1)) / math.sqrt(HEAD) + gate_bias
            decay_rate = jax.nn.sigmoid(gate_logit)
            key_unit = key_float * lax.rsqrt(lax.optimization_barrier(jnp.sum(key_float * key_float, axis=-1, keepdims=True)) + 1e-06)
            new_state = decay_rate[:, :, None, None] * prior_block.astype(jnp.float32) + key_unit[:, :, :, None] * values[:, :, None, :]
            new_state = new_state.astype(jnp.bfloat16)
            readout = jnp.einsum('bhd,bhde->bhe', queries, new_state.astype(jnp.float32))
            scaled = readout * lax.rsqrt(lax.optimization_barrier(jnp.mean(readout * readout, axis=-1, keepdims=True)) + 1e-05)
            normed = (scaled.reshape(BEAM, width) * norm_gain).astype(jnp.bfloat16)
            return (new_state, normed)
        new_states, normed = lax.map(update, (prior_state.reshape(USERS, BEAM, HEADS, HEAD, HEAD), projected.reshape(USERS, BEAM, 3, HEADS, HEAD)))
        state_now = new_states.reshape(row_count, HEADS, HEAD, HEAD)
        attention = jnp.dot(normed.reshape(row_count, width), out_weight, preferred_element_type=jnp.float32)
        outputs.append((inputs.astype(jnp.float32) + attention).astype(jnp.bfloat16))
    return (jnp.stack(outputs), state_now)
```

```python
import functools
import math

import jax
import jax.numpy as jnp
from jax import lax
from jax.experimental import pallas as pl
from jax.experimental.pallas import tpu as pltpu
from jax.sharding import PartitionSpec as P

CAP = 2
TILE = 16
VMEM_BYTES = 48 * 1024 * 1024
WHOLE = pl.BlockSpec(memory_space=pltpu.VMEM)
SCALARS = pl.BlockSpec(memory_space=pltpu.SMEM)
PLACED = pl.BlockSpec(memory_space=pl.ANY)


def params():
    return pltpu.CompilerParams(vmem_limit_bytes=VMEM_BYTES)


def xor_permute(block, distance):
    count = lax.axis_size("rows")
    return lax.ppermute(block, "rows", [(i, i ^ distance) for i in range(count)])


def stage_plan(count):
    if count == 1:
        return []
    if count == 2:
        return [[1]]
    if count == 4:
        return [[2], [1]]
    plan = [[6], [4, 8, 12] if count >= 16 else [4]]
    bit = 16
    while bit < count:
        plan.append([bit])
        bit *= 2
    return plan + [[1]]


def plan_order(plan):
    order = [0]
    for stage in plan:
        order = [near ^ far for near in order for far in [0] + stage]
    return order


def gather_all(block, plan):
    gathered, order = block[None], [0]
    for stage in plan:
        gathered = jnp.concatenate([gathered] + [xor_permute(gathered, d) for d in stage], 0)
        order = [near ^ far for far in [0] + stage for near in order]
    return gathered, order


def exchange_all(pieces, plan):
    tail = pieces.shape[1:]
    lengths = tuple(len(stage) + 1 for stage in plan)
    held = pieces.reshape(lengths + tail)
    for axis, stage in enumerate(plan):
        parts = [lax.index_in_dim(held, 0, axis, keepdims=True)]
        for place, distance in enumerate(stage):
            parts.append(xor_permute(lax.index_in_dim(held, place + 1, axis, keepdims=True), distance))
        held = jnp.concatenate(parts, axis)
    return held.reshape((len(pieces),) + tail)


def fetch_kernel(token_ref, send_ref, low_ref, table_ref, states_ref, x_ref, y_ref, d_ref, c_ref, rows_ref, row_sem, state_sem):
    count = token_ref.shape[0]

    def start_row(r, carry):
        first = pl.multiple_of(token_ref[r] // TILE * TILE, TILE)
        pltpu.make_async_copy(
            table_ref.at[pl.ds(first, TILE)],
            rows_ref.at[pl.ds(pl.multiple_of(r * TILE, TILE), TILE)],
            row_sem,
        ).start()
        return carry

    lax.fori_loop(0, count, start_row, 0, unroll=8)
    copies = []
    for partner, out in ((2, y_ref), (3, d_ref), (1, c_ref)):
        for slot in range(CAP):
            place = (partner - 1) * CAP + slot
            copies.append(
                pltpu.make_async_copy(states_ref.at[send_ref[place]], out.at[slot], state_sem.at[place])
            )
            copies[-1].start()
    pltpu.make_async_copy(table_ref.at[pl.ds(0, count * TILE)], rows_ref, row_sem).wait()
    step = math.gcd(count, 128)
    for first in range(0, count, step):
        wanted = lax.broadcasted_iota(jnp.int32, (step, 1), 0) * TILE + low_ref[first : first + step, :]
        chosen = lax.broadcasted_iota(jnp.int32, (step, step * TILE), 1) == wanted
        x_ref[first : first + step, :] = jnp.dot(
            chosen.astype(jnp.float32).astype(jnp.bfloat16),
            rows_ref[first * TILE : (first + step) * TILE, :],
            preferred_element_type=jnp.float32,
        ).astype(jnp.bfloat16)
    for copy in copies:
        copy.wait()


def project_kernel(order, me_ref, x_ref, weight_ref, index_ref, out_ref):
    me = me_ref[0]
    columns = x_ref.shape[2]
    total = None
    for place, distance in enumerate(order):
        first = pl.multiple_of((me ^ distance) * columns, columns)
        term = jnp.dot(x_ref[place], weight_ref[pl.ds(first, columns), :], preferred_element_type=jnp.float32)
        total = term if total is None else total + term
    rounded = total.astype(jnp.bfloat16)
    shape = (index_ref.shape[0], rounded.shape[0])
    chosen = lax.broadcasted_iota(jnp.int32, shape, 1) == index_ref[...]
    out_ref[...] = jnp.dot(
        chosen.astype(jnp.float32).astype(jnp.bfloat16), rounded, preferred_element_type=jnp.float32
    ).astype(jnp.bfloat16)


def head_terms(piece, gate_row, bias, size):
    keys = piece[:, size : 2 * size].astype(jnp.float32)
    values = piece[:, 2 * size :].astype(jnp.float32)
    logit = jnp.sum(keys * gate_row, axis=-1, keepdims=True) / math.sqrt(size) + bias
    decay = 1.0 / (1.0 + jnp.exp(-logit))
    inverse = lax.rsqrt(jnp.sum(keys * keys, axis=-1, keepdims=True) + 1e-06)
    return keys, values, decay, inverse


def readout_kernel(
    own_rows, lane_ref, bias_ref, recv_ref, states_ref, near_ref, place_ref, gate_ref, gain_ref, out_ref, norm_ref
):
    step, block, size = pl.program_id(0), states_ref.shape[1], states_ref.shape[2]
    place = place_ref[...]
    for part in range(block):
        head = step * block + part
        piece = recv_ref[lane_ref[head]]
        keys, values, decay, inverse = head_terms(piece, gate_ref[pl.ds(head, 1), :], bias_ref[head], size)
        queries = piece[:, :size]
        query_float = queries.astype(jnp.float32)
        zero = jnp.zeros_like(query_float)
        prior_part = None
        for ref, first in ((states_ref, 0), (near_ref, own_rows)):
            count = ref.shape[0]
            spread = jnp.concatenate(
                [jnp.where(place == first + p, query_float, zero).astype(jnp.bfloat16) for p in range(count)], 1
            )
            term = jnp.dot(spread, ref[:, part].reshape(count * size, size), preferred_element_type=jnp.float32)
            prior_part = term if prior_part is None else prior_part + term
        overlap = jnp.sum(query_float * keys, axis=-1, keepdims=True) * inverse
        readout = decay * prior_part + overlap * values
        scale = lax.rsqrt(jnp.mean(readout * readout, axis=-1, keepdims=True) + 1e-05)
        norm_ref[head] = readout * scale * gain_ref[pl.ds(head, 1), :]

    @pl.when(step == pl.num_programs(0) - 1)
    def _():
        heads = norm_ref.shape[0]
        halves = []
        for first in (0, heads // 2):
            halves.append(jnp.concatenate([norm_ref[h] for h in range(first, first + heads // 2)], 1))
        foreign = own_rows + 2 * CAP
        out_ref[...] = jnp.concatenate(
            [half[:own_rows] for half in halves] + [half[own_rows:foreign] for half in halves], 0
        ).astype(jnp.bfloat16)


def output_kernel(x_ref, normed_ref, weight_ref, low_ref, high_ref, out_ref):
    half = normed_ref.shape[1]
    shape = (x_ref.shape[0], normed_ref.shape[0])
    total = x_ref[...].astype(jnp.float32)
    for part, index_ref in enumerate((low_ref, high_ref)):
        product = jnp.dot(
            normed_ref[...], weight_ref[part * half : (part + 1) * half, :], preferred_element_type=jnp.float32
        )
        chosen = (lax.broadcasted_iota(jnp.int32, shape, 1) == index_ref[...]).astype(jnp.float32)
        total = total + jnp.dot(
            chosen, product, preferred_element_type=jnp.float32, precision=lax.Precision.HIGHEST
        )
    out_ref[...] = total.astype(jnp.bfloat16)


def near_update_kernel(lane_ref, bias_ref, source_ref, recv_ref, states_ref, near_ref, gate_ref, out_ref):
    own_rows, block, size = states_ref.shape[0], states_ref.shape[1], states_ref.shape[2]
    step = pl.program_id(0)
    for part in range(block):
        head = step * block + part
        piece = recv_ref[lane_ref[head]]
        keys, values, decay, inverse = head_terms(piece, gate_ref[pl.ds(head, 1), :], bias_ref[head], size)
        turned = jnp.transpose(keys * inverse)
        for row in range(own_rows):

            def store(prior, row=row, part=part, turned=turned, values=values, decay=decay):
                fresh = decay[row : row + 1, :] * prior.astype(jnp.float32)
                fresh = fresh + turned[:, row : row + 1] * values[row : row + 1, :]
                out_ref[row, part] = fresh.astype(jnp.bfloat16)

            source = source_ref[row]

            @pl.when((source >= 0) & (source < own_rows))
            def _():
                store(states_ref[jnp.clip(source, 0, own_rows - 1), part])

            @pl.when(source >= own_rows)
            def _():
                store(near_ref[jnp.clip(source - own_rows, 0, near_ref.shape[0] - 1), part])


def far_update_kernel(
    block, lane_ref, bias_ref, child_ref, recv_ref, got_ref, gate_ref, old_ref, out_ref, in_ref, new_ref, in_sem, out_sem
):
    count, heads, size = got_ref.shape[0], got_ref.shape[1], got_ref.shape[2]
    chunks = heads // block

    def load(slot, chunk):
        span = pl.ds(chunk * block, block)
        return pltpu.make_async_copy(got_ref.at[slot, span], in_ref.at[slot, span], in_sem.at[slot, chunk])

    def save(slot, chunk):
        span = pl.ds(chunk * block, block)
        child = jnp.maximum(child_ref[slot], 0)
        return pltpu.make_async_copy(new_ref.at[slot, span], out_ref.at[child, span], out_sem.at[slot, chunk])

    def if_used(slot, action):
        @pl.when(child_ref[slot] >= 0)
        def _():
            action()

    for chunk in range(chunks):
        for slot in range(count):
            if_used(slot, load(slot, chunk).start)
    for chunk in range(chunks):
        for slot in range(count):

            def work(slot=slot, chunk=chunk):
                load(slot, chunk).wait()
                child = child_ref[slot]
                for head in range(chunk * block, (chunk + 1) * block):
                    piece = recv_ref[lane_ref[head]]
                    keys, values, decay, inverse = head_terms(piece, gate_ref[head : head + 1, :], bias_ref[head], size)
                    mine = lax.broadcasted_iota(jnp.int32, (keys.shape[0], 1), 0) == child
                    key_row = jnp.sum(jnp.where(mine, keys * inverse, 0.0), axis=0, keepdims=True)
                    value_row = jnp.sum(jnp.where(mine, values, 0.0), axis=0, keepdims=True)
                    decay_one = jnp.sum(jnp.where(mine, decay, 0.0), axis=0, keepdims=True)
                    turned = jnp.transpose(jnp.broadcast_to(key_row, (8, size)))[:, 0:1]
                    fresh = decay_one * in_ref[slot, head].astype(jnp.float32) + turned * value_row
                    new_ref[slot, head] = fresh.astype(jnp.bfloat16)
                save(slot, chunk).start()

            if_used(slot, work)
    for chunk in range(chunks):
        for slot in range(count):
            if_used(slot, save(slot, chunk).wait)


def per_device(
    token_ids,
    parents,
    states,
    embed_table,
    qkv_weight,
    gate_weight,
    gate_bias,
    norm_gain,
    out_weight,
):
    own_rows, heads, size = states.shape[0], states.shape[1], states.shape[2]
    width = heads * size
    columns = embed_table.shape[1]
    row_total = token_ids.shape[1]
    users, beam = parents.shape[1], parents.shape[2]
    blocks = beam // own_rows
    count = lax.axis_size("rows")
    me = lax.axis_index("rows").astype(jnp.int32)
    user, member = me // blocks, me % blocks
    plan = stage_plan(count)
    slots = own_rows + 4 * CAP
    state_slab = (CAP, heads, size, size)
    bf16, int32 = jnp.bfloat16, jnp.int32

    parent_block = (parents[0] // own_rows).reshape(users, blocks, own_rows)
    parent_row = (parents[0] % own_rows).reshape(users, blocks, own_rows)
    along = jnp.arange(own_rows, dtype=int32)
    same = parent_block[..., :, None] == parent_block[..., None, :]
    rank = jnp.sum((same & (along[None, :] < along[:, None])).astype(int32), axis=-1)
    block_ids = jnp.arange(blocks, dtype=int32)
    rank_ids = jnp.arange(CAP, dtype=int32)
    hit = (parent_block[:, :, None, None, :] == block_ids[:, None, None]) & (
        rank[:, :, None, None, :] == rank_ids[:, None]
    )
    child_at = jnp.sum(jnp.where(hit, along + 1, 0), axis=-1) - 1
    state_at = jnp.sum(jnp.where(hit, parent_row[:, :, None, None, :], 0), axis=-1)

    my_children = lax.dynamic_index_in_dim(child_at, user, 0, keepdims=False)
    my_states = lax.dynamic_index_in_dim(state_at, user, 0, keepdims=False)
    partners = member ^ jnp.arange(1, 4, dtype=int32)
    send = lax.dynamic_index_in_dim(my_states, member, 1, keepdims=False)[partners]

    tokens = token_ids[0]
    local_columns, y_out, d_out, c_out = pl.pallas_call(
        fetch_kernel,
        in_specs=[SCALARS, SCALARS, WHOLE, PLACED, PLACED],
        out_specs=[WHOLE, PLACED, PLACED, PLACED],
        out_shape=[jax.ShapeDtypeStruct((row_total, columns), bf16)] + [jax.ShapeDtypeStruct(state_slab, bf16)] * 3,
        scratch_shapes=[
            pltpu.VMEM((row_total * TILE, columns), bf16),
            pltpu.SemaphoreType.DMA,
            pltpu.SemaphoreType.DMA((3 * CAP,)),
        ],
        compiler_params=params(),
        name="fetch",
    )(tokens, send.reshape(-1), (tokens % TILE)[:, None], embed_table, states)
    y_got = xor_permute(y_out, 2)
    d_got = xor_permute(d_out, 3)
    near_got = xor_permute(c_out, 1)

    device_ids = me ^ jnp.array(plan_order(plan), int32)
    device_user, device_member = device_ids // blocks, device_ids % blocks
    own_list = device_ids[:, None] * own_rows + along
    foreign_lists = []
    for partner in (2, 3):
        child_block = device_member ^ partner
        child = child_at[device_user, child_block, device_member]
        row = (device_user * blocks + child_block)[:, None] * own_rows + child
        foreign_lists.append(jnp.where(child >= 0, row, -1))
    unused = jnp.full((count, 2 * CAP), -1, int32)
    row_list = jnp.concatenate([own_list] + foreign_lists + [unused], 1).reshape(count * slots, 1)

    every_input, order = gather_all(local_columns, plan)
    pieces = pl.pallas_call(
        functools.partial(project_kernel, order),
        in_specs=[SCALARS, WHOLE, WHOLE, WHOLE],
        out_specs=WHOLE,
        out_shape=jax.ShapeDtypeStruct((count * slots, 3 * columns), bf16),
        compiler_params=params(),
        name="project",
    )(me[None], every_input, qkv_weight.reshape(qkv_weight.shape[0], 3 * columns), row_list)
    received = exchange_all(pieces.reshape(count, slots, 3 * columns), plan)
    recv_order = plan_order(plan)
    places = jnp.array([recv_order.index(d) for d in range(count)], int32)
    lanes = places[jnp.arange(count, dtype=int32) ^ me]
    by_head = received
    if columns != size:
        by_head = jnp.take(received, lanes, axis=0).reshape(count, slots, 3, columns).transpose(1, 2, 0, 3)
        by_head = by_head.reshape(slots, 3, heads, size).transpose(2, 0, 1, 3).reshape(heads, slots, 3 * size)
        lanes = jnp.arange(heads, dtype=int32)

    my_parent_block = lax.dynamic_index_in_dim(parent_block, user, 0, keepdims=False)[member]
    my_parent_row = lax.dynamic_index_in_dim(parent_row, user, 0, keepdims=False)[member]
    my_rank = lax.dynamic_index_in_dim(rank, user, 0, keepdims=False)[member]
    away = my_parent_block ^ member
    source = jnp.where(away == 0, my_parent_row, jnp.where(away == 1, own_rows + my_rank, -1))
    foreign_places = []
    for partner in (2, 3):
        child = my_children[member ^ partner, member]
        foreign_places.append(jnp.where(child >= 0, my_states[member ^ partner, member], -1))
    place = jnp.concatenate([source] + foreign_places + [jnp.full((2 * CAP,), -1, int32)])[:, None]

    head_block = math.gcd(heads, 4)
    by_heads = lambda rows: pl.BlockSpec((rows, head_block, size, size), lambda i: (0, i, 0, 0))
    state_bytes = 2 * own_rows * heads * size * size
    normed = pl.pallas_call(
        functools.partial(readout_kernel, own_rows),
        grid=(heads // head_block,),
        in_specs=[SCALARS, SCALARS, WHOLE, by_heads(own_rows), by_heads(CAP), WHOLE, WHOLE, WHOLE],
        out_specs=WHOLE,
        out_shape=jax.ShapeDtypeStruct((2 * (own_rows + 2 * CAP), width // 2), bf16),
        scratch_shapes=[pltpu.VMEM((heads, slots, size), jnp.float32)],
        compiler_params=params(),
        name="readout",
    )(lanes, gate_bias, by_head, states, near_got, place, gate_weight, norm_gain.reshape(heads, size))

    near_done = pl.pallas_call(
        near_update_kernel,
        grid=(heads // head_block,),
        in_specs=[SCALARS, SCALARS, SCALARS, WHOLE, by_heads(own_rows), by_heads(CAP), WHOLE],
        out_specs=by_heads(own_rows),
        out_shape=jax.ShapeDtypeStruct(states.shape, bf16),
        compiler_params=params(),
        cost_estimate=pl.CostEstimate(flops=4 * state_bytes, bytes_accessed=3 * state_bytes, transcendentals=0),
        name="near_update",
    )(lanes, gate_bias, source, by_head, states, near_got, gate_weight)

    def far_update(before, got, children, name):
        chunk = math.gcd(heads, 4)
        return pl.pallas_call(
            functools.partial(far_update_kernel, chunk),
            in_specs=[SCALARS, SCALARS, SCALARS, WHOLE, PLACED, WHOLE, PLACED],
            out_specs=PLACED,
            out_shape=jax.ShapeDtypeStruct(states.shape, bf16),
            scratch_shapes=[
                pltpu.VMEM(state_slab, bf16),
                pltpu.VMEM(state_slab, bf16),
                pltpu.SemaphoreType.DMA((CAP, heads // chunk)),
                pltpu.SemaphoreType.DMA((CAP, heads // chunk)),
            ],
            input_output_aliases={6: 0},
            compiler_params=params(),
            cost_estimate=pl.CostEstimate(flops=state_bytes, bytes_accessed=state_bytes // 2, transcendentals=0),
            name=name,
        )(lanes, gate_bias, children, by_head, got, gate_weight, before)

    y_done = far_update(near_done, y_got, my_children[member, member ^ 2], "y_update")
    final = far_update(y_done, d_got, my_children[member, member ^ 3], "corner_update")

    every_normed, normed_order = gather_all(normed, plan)
    normed_rows = normed.shape[0]
    all_away = parent_block ^ block_ids[None, :, None]
    over_y = all_away >= 2
    user_ids = jnp.arange(users, dtype=int32)[:, None, None]
    holder = user_ids * blocks + jnp.where(over_y, parent_block, block_ids[None, :, None])
    place_of = jnp.array([normed_order.index(d) for d in range(count)], int32)
    base = (place_of[holder ^ me] * normed_rows).reshape(row_total, 1)
    foreign_slot = jnp.where(over_y, (all_away - 2) * CAP + rank, 0).reshape(row_total, 1)
    over_y = over_y.reshape(row_total, 1)
    own_slot = jnp.broadcast_to(along, (users, blocks, own_rows)).reshape(row_total, 1)
    low = base + jnp.where(over_y, 2 * own_rows + foreign_slot, own_slot)
    high = low + jnp.where(over_y, 2 * CAP, own_rows)
    layer_out = pl.pallas_call(
        output_kernel,
        in_specs=[WHOLE] * 5,
        out_specs=WHOLE,
        out_shape=jax.ShapeDtypeStruct((row_total, columns), bf16),
        compiler_params=params(),
        name="output",
    )(local_columns, every_normed.reshape(count * normed_rows, width // 2), out_weight, low, high)
    return (layer_out[None], final)


def solution(mesh):
    placed = (
        P(None, "groups"),
        P(None, "groups", None),
        P(("groups", "rows"), None, None, None),
        P(None, "rows"),
        P(None, None, "rows"),
        P(),
        P(),
        P(),
        P(None, "rows"),
    )
    return jax.shard_map(
        per_device,
        mesh=mesh,
        in_specs=placed,
        out_specs=(P(None, "groups", "rows"), P(("groups", "rows"), None, None, None)),
        check_vma=False,
    )
```

```python
import functools
import math

import jax
import jax.numpy as jnp
from jax import lax
from jax.experimental import pallas as pl
from jax.experimental.pallas import tpu as pltpu
from jax.sharding import PartitionSpec as P

CAP = 2
TILE = 16
VMEM_BYTES = 48 * 1024 * 1024
WHOLE = pl.BlockSpec(memory_space=pltpu.VMEM)
SCALARS = pl.BlockSpec(memory_space=pltpu.SMEM)
PLACED = pl.BlockSpec(memory_space=pl.ANY)


def params():
    return pltpu.CompilerParams(vmem_limit_bytes=VMEM_BYTES)


def xor_permute(block, distance):
    count = lax.axis_size("rows")
    return lax.ppermute(block, "rows", [(i, i ^ distance) for i in range(count)])


def stage_plan(count):
    if count == 1:
        return []
    if count == 2:
        return [[1]]
    if count == 4:
        return [[2], [1]]
    plan = [[6], [4, 8, 12] if count >= 16 else [4]]
    bit = 16
    while bit < count:
        plan.append([bit])
        bit *= 2
    return plan + [[1]]


def plan_order(plan):
    order = [0]
    for stage in plan:
        order = [near ^ far for near in order for far in [0] + stage]
    return order


def gather_all(block, plan):
    held, order = [block], [0]
    for stage in plan:
        held = held + [xor_permute(part, distance) for distance in stage for part in held]
        order = [near ^ far for far in [0] + stage for near in order]
        if len(held) == 2:
            held = [jnp.concatenate(held, 0)]
    return held, order


def exchange_all(pieces, plan):
    tail = pieces.shape[1:]
    lengths = tuple(len(stage) + 1 for stage in plan)
    held = pieces.reshape(lengths + tail)
    for axis, stage in enumerate(plan):
        parts = [lax.index_in_dim(held, 0, axis, keepdims=True)]
        for place, distance in enumerate(stage):
            parts.append(xor_permute(lax.index_in_dim(held, place + 1, axis, keepdims=True), distance))
        held = jnp.concatenate(parts, axis)
    return held.reshape((len(pieces),) + tail)


def column_of(row):
    spread = jnp.broadcast_to(row.astype(jnp.float32), (8, row.shape[1]))
    return jnp.transpose(spread)[:, 0:1]


def chosen_rows(column, width):
    shape = (column.shape[0], width)
    return (lax.broadcasted_iota(jnp.int32, shape, 1).astype(jnp.float32) == column).astype(jnp.float32)


def fetch_kernel(
    blocks, me_ref, parent_ref, token_ref, tokens_ref, table_ref, states_ref, x_ref, y_ref, d_ref, c_ref, rows_ref, row_sem, state_sem
):
    count, own_rows = token_ref.shape[0], states_ref.shape[0]
    user, member = lax.div(me_ref[0], blocks), lax.rem(me_ref[0], blocks)
    copies = []
    for partner, out in ((2, y_ref), (3, d_ref), (1, c_ref)):
        first = (user * blocks + (member ^ partner)) * own_rows
        chosen, found = [jnp.int32(0)] * CAP, jnp.int32(0)
        for child in range(own_rows):
            parent = parent_ref[first + child]
            hit = lax.div(parent, own_rows) == member
            chosen = [jnp.where(hit & (found == j), lax.rem(parent, own_rows), old) for j, old in enumerate(chosen)]
            found = found + hit.astype(jnp.int32)
        for slot in range(CAP):
            place = (partner - 1) * CAP + slot
            copies.append(pltpu.make_async_copy(states_ref.at[chosen[slot]], out.at[slot], state_sem.at[place]))
            copies[-1].start()

    def start_row(r, carry):
        first = pl.multiple_of(lax.div(token_ref[r], TILE) * TILE, TILE)
        pltpu.make_async_copy(
            table_ref.at[pl.ds(first, TILE)],
            rows_ref.at[pl.ds(pl.multiple_of(r * TILE, TILE), TILE)],
            row_sem,
        ).start()
        return carry

    lax.fori_loop(0, count, start_row, 0, unroll=8)
    step = math.gcd(count, 128)
    picks = []
    for first in range(0, count, step):
        low = column_of(lax.rem(tokens_ref[:, first : first + step], TILE))
        wanted = low + lax.broadcasted_iota(jnp.int32, (step, 1), 0).astype(jnp.float32) * TILE
        picks.append(chosen_rows(wanted, step * TILE).astype(jnp.bfloat16))
    pltpu.make_async_copy(table_ref.at[pl.ds(0, count * TILE)], rows_ref, row_sem).wait()
    for first, pick in zip(range(0, count, step), picks):
        x_ref[first : first + step, :] = jnp.dot(
            pick, rows_ref[first * TILE : (first + step) * TILE, :], preferred_element_type=jnp.float32
        ).astype(jnp.bfloat16)
    for copy in copies:
        copy.wait()


def project_kernel(order, parts, me_ref, weight_ref, index_ref, *refs):
    held, out_ref = refs[:parts], refs[parts]
    me, columns = me_ref[0], held[0].shape[1]
    rows = held[0].shape[0] * parts // len(order)
    total = [None] * 3
    for place, distance in enumerate(order):
        ref, within = held[place * parts // len(order)], place % (len(order) // parts)
        block = ref[within * rows : (within + 1) * rows, :]
        first = pl.multiple_of((me ^ distance) * columns, columns)
        for slab in range(3):
            term = jnp.dot(block, weight_ref[slab, pl.ds(first, columns), :], preferred_element_type=jnp.float32)
            total[slab] = term if total[slab] is None else total[slab] + term
    pick = chosen_rows(column_of(index_ref[...]), rows).astype(jnp.bfloat16)
    for slab in range(3):
        out_ref[:, slab * columns : (slab + 1) * columns] = jnp.dot(
            pick, total[slab].astype(jnp.bfloat16), preferred_element_type=jnp.float32
        ).astype(jnp.bfloat16)


def head_terms(piece, gate_row, bias, size):
    keys = piece[:, size : 2 * size].astype(jnp.float32)
    values = piece[:, 2 * size :].astype(jnp.float32)
    logit = jnp.sum(keys * gate_row, axis=-1, keepdims=True) / math.sqrt(size) + bias
    decay = 1.0 / (1.0 + jnp.exp(-logit))
    inverse = lax.rsqrt(jnp.sum(keys * keys, axis=-1, keepdims=True) + 1e-06)
    return keys, values, decay, inverse


def readout_kernel(
    own_rows, lane_ref, bias_ref, recv_ref, states_ref, near_ref, place_ref, gate_ref, gain_ref, out_ref, norm_ref
):
    step, block, size = pl.program_id(0), states_ref.shape[1], states_ref.shape[2]
    place = column_of(place_ref[...])[: recv_ref.shape[1]]
    for part in range(block):
        head = step * block + part
        piece = recv_ref[lane_ref[head]]
        keys, values, decay, inverse = head_terms(piece, gate_ref[pl.ds(head, 1), :], bias_ref[head], size)
        queries = piece[:, :size]
        query_float = queries.astype(jnp.float32)
        zero = jnp.zeros_like(query_float)
        prior_part = None
        for ref, first in ((states_ref, 0), (near_ref, own_rows)):
            count = ref.shape[0]
            spread = jnp.concatenate(
                [jnp.where(place == float(first + p), query_float, zero).astype(jnp.bfloat16) for p in range(count)], 1
            )
            term = jnp.dot(spread, ref[:, part].reshape(count * size, size), preferred_element_type=jnp.float32)
            prior_part = term if prior_part is None else prior_part + term
        overlap = jnp.sum(query_float * keys, axis=-1, keepdims=True) * inverse
        readout = decay * prior_part + overlap * values
        scale = lax.rsqrt(jnp.mean(readout * readout, axis=-1, keepdims=True) + 1e-05)
        norm_ref[head] = readout * scale * gain_ref[pl.ds(head, 1), :]

    @pl.when(step == pl.num_programs(0) - 1)
    def _():
        heads = norm_ref.shape[0]
        halves = []
        for first in (0, heads // 2):
            halves.append(jnp.concatenate([norm_ref[h] for h in range(first, first + heads // 2)], 1))
        foreign = own_rows + 2 * CAP
        out_ref[...] = jnp.concatenate(
            [half[:own_rows] for half in halves] + [half[own_rows:foreign] for half in halves], 0
        ).astype(jnp.bfloat16)


def output_kernel(x_ref, weight_ref, low_ref, high_ref, *refs):
    parts, out_ref = refs[:-1], refs[-1]
    half = parts[0].shape[1]
    total = x_ref[...].astype(jnp.float32)
    for side, index_ref in enumerate((low_ref, high_ref)):
        weight = weight_ref[side * half : (side + 1) * half, :]
        product = jnp.concatenate([jnp.dot(part[...], weight, preferred_element_type=jnp.float32) for part in parts], 0)
        pick = chosen_rows(column_of(index_ref[...]), product.shape[0])
        total = total + jnp.dot(pick, product, preferred_element_type=jnp.float32, precision=lax.Precision.HIGHEST)
    out_ref[...] = total.astype(jnp.bfloat16)


def near_update_kernel(lane_ref, bias_ref, source_ref, recv_ref, states_ref, near_ref, gate_ref, out_ref, turned_ref, terms_ref):
    own_rows, block, size = states_ref.shape[0], states_ref.shape[1], states_ref.shape[2]
    step, slots = pl.program_id(0), recv_ref.shape[1]
    for part in range(block):
        head = step * block + part
        piece = recv_ref[lane_ref[head]]
        keys, _, decay, inverse = head_terms(piece, gate_ref[pl.ds(head, 1), :], bias_ref[head], size)
        turned = jnp.transpose(keys)
        turned_ref[part] = turned.astype(jnp.bfloat16)
        terms_ref[0, part] = jnp.broadcast_to(decay, (slots, size))
        terms_ref[1, part] = jnp.broadcast_to(inverse, (slots, size))
        lane = lax.broadcasted_iota(jnp.int32, (size, slots), 1)
        spread = jnp.concatenate(
            [jnp.where(lane == row, turned, 0.0).astype(jnp.bfloat16) for row in range(own_rows)], 0
        )
        outer = jnp.dot(spread, piece[:, 2 * size :], preferred_element_type=jnp.float32)
        for row in range(own_rows):
            source = source_ref[row]
            prior = jnp.where(
                source >= own_rows,
                near_ref[jnp.clip(source - own_rows, 0, near_ref.shape[0] - 1), part],
                states_ref[jnp.clip(source, 0, own_rows - 1), part],
            )
            fresh = decay[row : row + 1, :] * prior.astype(jnp.float32)
            fresh = fresh + inverse[row : row + 1, :] * outer[row * size : (row + 1) * size, :]
            out_ref[row, part] = fresh.astype(jnp.bfloat16)


def far_update_kernel(
    block, lane_ref, child_ref, recv_ref, turned_ref, terms_ref, got_ref, old_ref, out_ref, in_ref, new_ref, in_sem, out_sem
):
    count, heads, size = got_ref.shape[0], got_ref.shape[1], got_ref.shape[2]
    chunks = heads // block

    def load(slot, chunk):
        span = pl.ds(chunk * block, block)
        return pltpu.make_async_copy(got_ref.at[slot, span], in_ref.at[slot, span], in_sem.at[slot, chunk])

    def save(slot, chunk):
        span = pl.ds(chunk * block, block)
        child = jnp.maximum(child_ref[slot], 0)
        return pltpu.make_async_copy(new_ref.at[slot, span], out_ref.at[child, span], out_sem.at[slot, chunk])

    def if_used(slot, action):
        @pl.when(child_ref[slot] >= 0)
        def _():
            action()

    for chunk in range(chunks):
        for slot in range(count):
            if_used(slot, load(slot, chunk).start)
    for chunk in range(chunks):
        for slot in range(count):

            def work(slot=slot, chunk=chunk):
                load(slot, chunk).wait()
                child = child_ref[slot]
                lane = lax.broadcasted_iota(jnp.int32, (size, turned_ref.shape[2]), 1)
                for head in range(chunk * block, (chunk + 1) * block):
                    turned = turned_ref[head].astype(jnp.float32)
                    key = jnp.where(lane == child, turned, 0.0).astype(jnp.bfloat16)
                    values = recv_ref[lane_ref[head]][:, 2 * size :]
                    outer = jnp.dot(key, values, preferred_element_type=jnp.float32)
                    fresh = terms_ref[0, head, pl.ds(child, 1), :] * in_ref[slot, head].astype(jnp.float32)
                    fresh = fresh + terms_ref[1, head, pl.ds(child, 1), :] * outer
                    new_ref[slot, head] = fresh.astype(jnp.bfloat16)
                save(slot, chunk).start()

            if_used(slot, work)
    for chunk in range(chunks):
        for slot in range(count):
            if_used(slot, save(slot, chunk).wait)


def per_device(
    token_ids,
    parents,
    states,
    embed_table,
    qkv_weight,
    gate_weight,
    gate_bias,
    norm_gain,
    out_weight,
):
    own_rows, heads, size = states.shape[0], states.shape[1], states.shape[2]
    width = heads * size
    columns = embed_table.shape[1]
    row_total = token_ids.shape[1]
    users, beam = parents.shape[1], parents.shape[2]
    blocks = beam // own_rows
    count = lax.axis_size("rows")
    me = lax.axis_index("rows").astype(jnp.int32)
    user, member = me // blocks, me % blocks
    plan = stage_plan(count)
    slots = own_rows + 4 * CAP
    state_slab = (CAP, heads, size, size)
    bf16, int32 = jnp.bfloat16, jnp.int32

    parent_block = (parents[0] // own_rows).reshape(users, blocks, own_rows)
    parent_row = (parents[0] % own_rows).reshape(users, blocks, own_rows)
    along = jnp.arange(own_rows, dtype=int32)
    same = parent_block[..., :, None] == parent_block[..., None, :]
    rank = jnp.sum((same & (along[None, :] < along[:, None])).astype(int32), axis=-1)
    block_ids = jnp.arange(blocks, dtype=int32)
    rank_ids = jnp.arange(CAP, dtype=int32)
    hit = (parent_block[:, :, None, None, :] == block_ids[:, None, None]) & (
        rank[:, :, None, None, :] == rank_ids[:, None]
    )
    child_at = jnp.sum(jnp.where(hit, along + 1, 0), axis=-1) - 1
    state_at = jnp.sum(jnp.where(hit, parent_row[:, :, None, None, :], 0), axis=-1)

    my_children = lax.dynamic_index_in_dim(child_at, user, 0, keepdims=False)
    my_states = lax.dynamic_index_in_dim(state_at, user, 0, keepdims=False)
    local_columns, y_out, d_out, c_out = pl.pallas_call(
        functools.partial(fetch_kernel, blocks),
        in_specs=[SCALARS, SCALARS, SCALARS, WHOLE, PLACED, PLACED],
        out_specs=[WHOLE] * 4,
        out_shape=[jax.ShapeDtypeStruct((row_total, columns), bf16)] + [jax.ShapeDtypeStruct(state_slab, bf16)] * 3,
        scratch_shapes=[
            pltpu.VMEM((row_total * TILE, columns), bf16),
            pltpu.SemaphoreType.DMA,
            pltpu.SemaphoreType.DMA((3 * CAP,)),
        ],
        compiler_params=params(),
        name="fetch",
    )(me[None], parents.reshape(-1), token_ids.reshape(-1), token_ids, embed_table, states)
    y_got = xor_permute(y_out, 2)
    d_got = xor_permute(d_out, 3)
    near_got = xor_permute(c_out, 1)

    device_ids = me ^ jnp.array(plan_order(plan), int32)
    device_user, device_member = device_ids // blocks, device_ids % blocks
    own_list = device_ids[:, None] * own_rows + along
    foreign_lists = []
    for partner in (2, 3):
        child_block = device_member ^ partner
        child = child_at[device_user, child_block, device_member]
        row = (device_user * blocks + child_block)[:, None] * own_rows + child
        foreign_lists.append(jnp.where(child >= 0, row, -1))
    unused = jnp.full((count, 2 * CAP), -1, int32)
    row_list = jnp.concatenate([own_list] + foreign_lists + [unused], 1).reshape(1, count * slots)

    every_input, order = gather_all(local_columns, plan)
    weight = jnp.transpose(qkv_weight, (1, 0, 2))
    pieces = pl.pallas_call(
        functools.partial(project_kernel, order, len(every_input)),
        in_specs=[SCALARS] + [WHOLE] * (2 + len(every_input)),
        out_specs=WHOLE,
        out_shape=jax.ShapeDtypeStruct((count * slots, 3 * columns), bf16),
        compiler_params=params(),
        name="project",
    )(me[None], weight, row_list, *every_input)
    received = exchange_all(pieces.reshape(count, slots, 3 * columns), plan)
    recv_order = plan_order(plan)
    places = jnp.array([recv_order.index(d) for d in range(count)], int32)
    lanes = places[jnp.arange(count, dtype=int32) ^ me]
    by_head = received
    if columns != size:
        by_head = jnp.take(received, lanes, axis=0).reshape(count, slots, 3, columns).transpose(1, 2, 0, 3)
        by_head = by_head.reshape(slots, 3, heads, size).transpose(2, 0, 1, 3).reshape(heads, slots, 3 * size)
        lanes = jnp.arange(heads, dtype=int32)

    my_parent_block = lax.dynamic_index_in_dim(parent_block, user, 0, keepdims=False)[member]
    my_parent_row = lax.dynamic_index_in_dim(parent_row, user, 0, keepdims=False)[member]
    my_rank = lax.dynamic_index_in_dim(rank, user, 0, keepdims=False)[member]
    away = my_parent_block ^ member
    source = jnp.where(away == 0, my_parent_row, jnp.where(away == 1, own_rows + my_rank, -1))
    foreign_places = []
    for partner in (2, 3):
        child = my_children[member ^ partner, member]
        foreign_places.append(jnp.where(child >= 0, my_states[member ^ partner, member], -1))
    idle = jnp.full((128 - own_rows - 2 * CAP,), -1, int32)
    place = jnp.concatenate([source] + foreign_places + [idle])[None]

    head_block = math.gcd(heads, 4)
    by_heads = lambda rows: pl.BlockSpec((rows, head_block, size, size), lambda i: (0, i, 0, 0))
    normed = pl.pallas_call(
        functools.partial(readout_kernel, own_rows),
        grid=(heads // head_block,),
        in_specs=[SCALARS, SCALARS, WHOLE, by_heads(own_rows), by_heads(CAP), WHOLE, WHOLE, WHOLE],
        out_specs=WHOLE,
        out_shape=jax.ShapeDtypeStruct((2 * (own_rows + 2 * CAP), width // 2), bf16),
        scratch_shapes=[pltpu.VMEM((heads, slots, size), jnp.float32)],
        compiler_params=params(),
        name="readout",
    )(lanes, gate_bias, by_head, states, near_got, place, gate_weight, norm_gain.reshape(heads, size))

    turned_shape, terms_shape = (heads, size, slots), (2, heads, slots, size)
    near_done, turned, terms = pl.pallas_call(
        near_update_kernel,
        grid=(heads // head_block,),
        in_specs=[SCALARS, SCALARS, SCALARS, WHOLE, by_heads(own_rows), by_heads(CAP), WHOLE],
        out_specs=[
            by_heads(own_rows),
            pl.BlockSpec((head_block, size, slots), lambda i: (i, 0, 0)),
            pl.BlockSpec((2, head_block, slots, size), lambda i: (0, i, 0, 0)),
        ],
        out_shape=[
            jax.ShapeDtypeStruct(states.shape, bf16),
            jax.ShapeDtypeStruct(turned_shape, bf16),
            jax.ShapeDtypeStruct(terms_shape, jnp.float32),
        ],
        compiler_params=params(),
        name="near_update",
    )(lanes, gate_bias, source, by_head, states, near_got, gate_weight)

    def far_update(before, got, children, name):
        chunk = math.gcd(heads, 4)
        return pl.pallas_call(
            functools.partial(far_update_kernel, chunk),
            in_specs=[SCALARS, SCALARS, WHOLE, WHOLE, WHOLE, PLACED, PLACED],
            out_specs=PLACED,
            out_shape=jax.ShapeDtypeStruct(states.shape, bf16),
            scratch_shapes=[
                pltpu.VMEM(state_slab, bf16),
                pltpu.VMEM(state_slab, bf16),
                pltpu.SemaphoreType.DMA((CAP, heads // chunk)),
                pltpu.SemaphoreType.DMA((CAP, heads // chunk)),
            ],
            input_output_aliases={6: 0},
            compiler_params=params(),
            name=name,
        )(lanes, children, by_head, turned, terms, got, before)

    y_done = far_update(near_done, y_got, my_children[member, member ^ 2], "y_update")
    final = far_update(y_done, d_got, my_children[member, member ^ 3], "corner_update")

    every_normed, normed_order = gather_all(normed, plan)
    normed_rows = normed.shape[0]
    all_away = parent_block ^ block_ids[None, :, None]
    over_y = all_away >= 2
    user_ids = jnp.arange(users, dtype=int32)[:, None, None]
    holder = user_ids * blocks + jnp.where(over_y, parent_block, block_ids[None, :, None])
    place_of = jnp.array([normed_order.index(d) for d in range(count)], int32)
    base = (place_of[holder ^ me] * normed_rows).reshape(1, row_total)
    foreign_slot = jnp.where(over_y, (all_away - 2) * CAP + rank, 0).reshape(1, row_total)
    over_y = over_y.reshape(1, row_total)
    own_slot = jnp.broadcast_to(along, (users, blocks, own_rows)).reshape(1, row_total)
    low = base + jnp.where(over_y, 2 * own_rows + foreign_slot, own_slot)
    high = low + jnp.where(over_y, 2 * CAP, own_rows)
    layer_out = pl.pallas_call(
        output_kernel,
        in_specs=[WHOLE] * (4 + len(every_normed)),
        out_specs=WHOLE,
        out_shape=jax.ShapeDtypeStruct((row_total, columns), bf16),
        compiler_params=params(),
        name="output",
    )(local_columns, out_weight, low, high, *every_normed)
    return (layer_out[None], final)


def solution(mesh):
    placed = (
        P(None, "groups"),
        P(None, "groups", None),
        P(("groups", "rows"), None, None, None),
        P(None, "rows"),
        P(None, None, "rows"),
        P(),
        P(),
        P(),
        P(None, "rows"),
    )
    return jax.shard_map(
        per_device,
        mesh=mesh,
        in_specs=placed,
        out_specs=(P(None, "groups", "rows"), P(("groups", "rows"), None, None, None)),
        check_vma=False,
    )
```

```python
import functools
import math

import jax
import jax.numpy as jnp
from jax import lax
from jax.experimental import pallas as pl
from jax.experimental.pallas import tpu as pltpu
from jax.sharding import PartitionSpec as P

CAP = 2
TILE = 16
VMEM_BYTES = 24 * 1024 * 1024
WHOLE = pl.BlockSpec(memory_space=pltpu.VMEM)
SCALARS = pl.BlockSpec(memory_space=pltpu.SMEM)
PLACED = pl.BlockSpec(memory_space=pl.ANY)


def params():
    return pltpu.CompilerParams(vmem_limit_bytes=VMEM_BYTES)


def in_hbm(array):
    return pltpu.with_memory_space_constraint(array, pltpu.HBM)


def xor_permute(block, distance):
    count = lax.axis_size("rows")
    return lax.ppermute(block, "rows", [(i, i ^ distance) for i in range(count)])


def stage_plan(count):
    if count == 1:
        return []
    if count == 2:
        return [[1]]
    if count == 4:
        return [[2], [1]]
    plan = [[6], [4, 8, 12] if count >= 16 else [4]]
    bit = 16
    while bit < count:
        plan.append([bit])
        bit *= 2
    return plan + [[1]]


def plan_order(plan):
    order = [0]
    for stage in plan:
        order = [near ^ far for near in order for far in [0] + stage]
    return order


def gather_order(plan):
    order = [0]
    for stage in plan:
        order = [near ^ far for far in [0] + stage for near in order]
    return order


def gather_all(block, plan, after=lambda stage, held: held):
    held = [block]
    for number, stage in enumerate(plan):
        held = held + [xor_permute(part, distance) for distance in stage for part in held]
        if len(held) == 2:
            held = [jnp.concatenate(held, 0)]
        held = after(number, held)
    return held


def exchange_all(pieces, plan, after=lambda stage, held: held):
    tail = pieces.shape[1:]
    held = [pieces.reshape(tuple(len(stage) + 1 for stage in plan) + tail)]
    for axis, stage in enumerate(plan):
        slab = lambda part, place: lax.index_in_dim(part, place, axis, keepdims=True)
        fresh = []
        for part in held:
            fresh.append(slab(part, 0))
            fresh += [xor_permute(slab(part, place + 1), distance) for place, distance in enumerate(stage)]
        held = after(axis, [jnp.concatenate(fresh, 0)] if axis == 0 else fresh)
    return [part.reshape((-1,) + tail) for part in held]


def split(number, size):
    if size & (size - 1) == 0:
        return lax.shift_right_logical(number, size.bit_length() - 1), number & (size - 1)
    return lax.div(number, size), lax.rem(number, size)


def place_in(order, distance):
    place, bit = distance & 0, 0
    while 1 << bit < len(order):
        place = place ^ ((lax.shift_right_logical(distance, bit) & 1) * order.index(1 << bit))
        bit += 1
    return place


def row_facts(parent_row, blocks, own_rows):
    lane = lax.broadcasted_iota(jnp.int32, parent_row.shape, 1)
    device, child = split(lane, own_rows)
    parent_block, parent_place = split(parent_row, own_rows)
    rank = jnp.zeros_like(lane)
    for earlier in range(1, own_rows):
        same = (pltpu.roll(parent_block, earlier, 1) == parent_block) & (child >= earlier)
        rank = rank + same.astype(jnp.int32)
    away = parent_block ^ (device & (blocks - 1))
    over = away >= 2
    slot = own_rows + (away - 2) * CAP + rank
    near_place = jnp.where(away == 0, parent_place, own_rows + rank)
    return device, child, over, device ^ away, slot, parent_place, near_place


def column_of(row):
    spread = jnp.broadcast_to(row[0:1].astype(jnp.float32), (8, row.shape[1]))
    return jnp.transpose(spread)[:, 0:1]


def chosen_rows(column, width):
    shape = (column.shape[0], width)
    return (lax.broadcasted_iota(jnp.int32, shape, 1).astype(jnp.float32) == column).astype(jnp.float32)


def matching_children(parent_ref, user, child_block, parent_block, own_rows, none):
    children, parents, found = [jnp.int32(none)] * CAP, [jnp.int32(0)] * CAP, jnp.int32(0)
    for child in range(own_rows):
        block, place = split(parent_ref[0, user, child_block * own_rows + child], own_rows)
        hit = block == parent_block
        for j in range(CAP):
            children[j] = jnp.where(hit & (found == j), child, children[j])
            parents[j] = jnp.where(hit & (found == j), place, parents[j])
        found = found + hit.astype(jnp.int32)
    return children, parents


def fetch_kernel(
    blocks, me_ref, parent_ref, token_ref, tokens_ref, table_ref, states_ref, x_ref, first_ref, rows_ref, row_sem, state_sem
):
    count, own_rows = token_ref.shape[1], states_ref.shape[0]
    user, member = split(me_ref[0], blocks)
    _, chosen = matching_children(parent_ref, user, member ^ 2, member, own_rows, 0)
    state_copy = pltpu.make_async_copy(states_ref.at[chosen[0]], first_ref.at[0], state_sem)
    state_copy.start()

    def start_row(r, carry):
        first = pl.multiple_of(split(token_ref[0, r], TILE)[0] * TILE, TILE)
        pltpu.make_async_copy(
            table_ref.at[pl.ds(first, TILE)],
            rows_ref.at[pl.ds(pl.multiple_of(r * TILE, TILE), TILE)],
            row_sem,
        ).start()
        return carry

    lax.fori_loop(0, count, start_row, 0, unroll=8)
    step = math.gcd(count, 128)
    picks = []
    for first in range(0, count, step):
        low = column_of(split(tokens_ref[:, first : first + step], TILE)[1])
        wanted = low + lax.broadcasted_iota(jnp.int32, (step, 1), 0).astype(jnp.float32) * TILE
        picks.append(chosen_rows(wanted, step * TILE).astype(jnp.bfloat16))
    pltpu.make_async_copy(table_ref.at[pl.ds(0, count * TILE)], rows_ref, row_sem).wait()
    for first, pick in zip(range(0, count, step), picks):
        x_ref[first : first + step, :] = jnp.dot(
            pick, rows_ref[first * TILE : (first + step) * TILE, :], preferred_element_type=jnp.float32
        ).astype(jnp.bfloat16)
    state_copy.wait()


def stage_kernel(
    blocks, slots, send_order, normed_order, me_ref, parent_ref, parents_ref, states_ref,
    second_ref, third_ref, fourth_ref, near_ref, send_pick_ref, place_ref, low_pick_ref, high_pick_ref, hold_ref, in_sem, out_sem,
):
    me, own_rows = me_ref[0], states_ref.shape[0]
    user, member = split(me, blocks)
    wanted = []
    for partner in (2, 3, 1):
        wanted += matching_children(parent_ref, user, member ^ partner, member, own_rows, 0)[1]
    outs = [second_ref.at[0], third_ref.at[0], fourth_ref.at[0], near_ref.at[0], near_ref.at[1]]
    loads, saves = [], []
    for place, (row, out) in enumerate(zip(wanted[1:], outs)):
        loads.append(pltpu.make_async_copy(states_ref.at[row], hold_ref.at[place], in_sem.at[place]))
        saves.append(pltpu.make_async_copy(hold_ref.at[place], out, out_sem.at[place]))
        loads[-1].start()
    device, child, over, holder, slot, parent_place, near_place = row_facts(parents_ref[...], blocks, own_rows)
    rows = parents_ref.shape[1]
    own_target = place_in(send_order, device ^ me) * slots + child
    far_target = jnp.where(over, place_in(send_order, holder ^ me) * slots + slot, -1)
    line = lax.broadcasted_iota(jnp.int32, (len(send_order) * slots, rows), 0)
    send_pick_ref[...] = ((line == own_target[0:1]) | (line == far_target[0:1])).astype(jnp.float32).astype(jnp.bfloat16)
    for load, save in zip(loads, saves):
        load.wait()
        save.start()
    line = lax.broadcasted_iota(jnp.int32, (slots, rows), 0)
    own = (line == jnp.where((device == me) & ~over, child, -1)[0:1]).astype(jnp.float32)
    far = (line == jnp.where((holder == me) & over, slot, -1)[0:1]).astype(jnp.float32)
    place = own * (near_place[0:1] + 1).astype(jnp.float32) + far * (parent_place[0:1] + 1).astype(jnp.float32)
    place_ref[...] = jnp.broadcast_to(jnp.sum(place, axis=1, keepdims=True) - 1.0, place_ref.shape)
    piece = 2 * (own_rows + 2 * CAP)
    low = place_in(normed_order, jnp.where(over, holder, device) ^ me) * piece + jnp.where(over, own_rows + slot, child)
    high = low + jnp.where(over, 2 * CAP, own_rows)
    for index, ref in ((low, low_pick_ref), (high, high_pick_ref)):
        ref[...] = chosen_rows(column_of(index), ref.shape[1]).astype(jnp.bfloat16)
    for save in saves:
        save.wait()


def project_kernel(order, me_ref, weight_ref, pick_ref, *refs):
    held, out_ref = refs[:-1], refs[-1]
    me, columns, parts = me_ref[0], held[0].shape[1], len(held)
    rows = pick_ref.shape[1]
    total = [None] * 3
    for place, distance in enumerate(order):
        ref, within = held[place * parts // len(order)], place % (len(order) // parts)
        block = ref[within * rows : (within + 1) * rows, :]
        first = pl.multiple_of((me ^ distance) * columns, columns)
        for slab in range(3):
            term = jnp.dot(block, weight_ref[slab, pl.ds(first, columns), :], preferred_element_type=jnp.float32)
            total[slab] = term if total[slab] is None else total[slab] + term
    for slab in range(3):
        out_ref[:, slab * columns : (slab + 1) * columns] = jnp.dot(
            pick_ref[...], total[slab].astype(jnp.bfloat16), preferred_element_type=jnp.float32
        ).astype(jnp.bfloat16)


def head_terms(piece, gate_row, bias, size):
    keys = piece[:, size : 2 * size].astype(jnp.float32)
    values = piece[:, 2 * size :].astype(jnp.float32)
    logit = jnp.sum(keys * gate_row, axis=-1, keepdims=True) / math.sqrt(size) + bias
    decay = 1.0 / (1.0 + jnp.exp(-logit))
    inverse = lax.rsqrt(jnp.sum(keys * keys, axis=-1, keepdims=True) + 1e-06)
    return keys, values, decay, inverse


def lane_of(recv_order, me, head):
    return head if recv_order is None else place_in(recv_order, me ^ head)


def readout_kernel(recv_order, me_ref, bias_ref, place_ref, states_ref, near_ref, gate_ref, gain_ref, *refs):
    parts, (out_ref, recv_ref, norm_ref) = refs[:-3], refs[-3:]
    own_rows, block, size = states_ref.shape[0], states_ref.shape[1], states_ref.shape[2]
    step = pl.program_id(0)

    @pl.when(step == 0)
    def _():
        for number, part in enumerate(parts):
            for within in range(part.shape[0]):
                recv_ref[within * len(parts) + number] = part[within]

    place = place_ref[:, 0:1]
    for part in range(block):
        head = step * block + part
        piece = recv_ref[lane_of(recv_order, me_ref[0], head)]
        keys, values, decay, inverse = head_terms(piece, gate_ref[pl.ds(head, 1), :], bias_ref[head], size)
        queries = piece[:, :size].astype(jnp.float32)
        prior_part = None
        for ref, first in ((states_ref, 0), (near_ref, own_rows)):
            count = ref.shape[0]
            spread = jnp.concatenate(
                [jnp.where(place == float(first + p), queries, 0.0).astype(jnp.bfloat16) for p in range(count)], 1
            )
            states = ref[:, part].reshape(count * size, size)
            term = jnp.dot(spread, states, preferred_element_type=jnp.float32)
            prior_part = term if prior_part is None else prior_part + term
        overlap = jnp.sum(queries * keys, axis=-1, keepdims=True) * inverse
        readout = decay * prior_part + overlap * values
        scale = lax.rsqrt(jnp.mean(readout * readout, axis=-1, keepdims=True) + 1e-05)
        norm_ref[head] = readout * scale * gain_ref[pl.ds(head, 1), :]

    @pl.when(step == pl.num_programs(0) - 1)
    def _():
        heads = norm_ref.shape[0]
        halves = []
        for first in (0, heads // 2):
            halves.append(jnp.concatenate([norm_ref[h] for h in range(first, first + heads // 2)], 1))
        foreign = own_rows + 2 * CAP
        out_ref[...] = jnp.concatenate(
            [half[:own_rows] for half in halves] + [half[own_rows:foreign] for half in halves], 0
        ).astype(jnp.bfloat16)


def output_kernel(x_ref, weight_ref, low_pick_ref, high_pick_ref, *refs):
    parts, out_ref = refs[:-1], refs[-1]
    half, columns = parts[0].shape[1], x_ref.shape[1]
    total = x_ref[...].astype(jnp.float32)
    for side, pick_ref in enumerate((low_pick_ref, high_pick_ref)):
        weight = weight_ref[side * half : (side + 1) * half, :]
        rest = jnp.concatenate([jnp.dot(part[...], weight, preferred_element_type=jnp.float32) for part in parts], 0)
        for _ in range(3):
            term = rest.astype(jnp.bfloat16)
            rest = rest - term.astype(jnp.float32)
            total = total + jnp.dot(pick_ref[...], term, preferred_element_type=jnp.float32)
    out_ref[...] = total.astype(jnp.bfloat16)


def main_update_kernel(
    recv_order, blocks, arrived, me_ref, parent_ref, bias_ref, recv_ref, states_ref, near_ref, gate_ref, *refs
):
    far_refs, (out_ref, turned_ref, terms_ref) = refs[: len(arrived)], refs[len(arrived) :]
    own_rows, block, size = states_ref.shape[0], states_ref.shape[1], states_ref.shape[2]
    slots, step = recv_ref.shape[1], pl.program_id(0)
    user, member = split(me_ref[0], blocks)
    sources, found = [], [jnp.int32(0)] * 4
    for row in range(own_rows):
        parent_block, place = split(parent_ref[0, user, member * own_rows + row], own_rows)
        away = parent_block ^ member
        far = [(away == partner) & (found[partner] == rank) for partner, rank in arrived]
        sources.append((place, away == 1, jnp.minimum(found[1], CAP - 1), far))
        found = [count + (away == partner).astype(jnp.int32) for partner, count in enumerate(found)]
    line = lax.broadcasted_iota(jnp.int32, (slots, size), 0)
    for part in range(block):
        head = step * block + part
        piece = recv_ref[lane_of(recv_order, me_ref[0], head)]
        keys, values, decay, inverse = head_terms(piece, gate_ref[pl.ds(head, 1), :], bias_ref[head], size)
        turned = jnp.transpose(keys).astype(jnp.bfloat16)
        turned_ref[part] = turned
        terms_ref[0, part] = jnp.broadcast_to(decay, (slots, size))
        terms_ref[1, part] = jnp.broadcast_to(inverse, (slots, size))
        spread = [jnp.where(line == row, values, 0.0).astype(jnp.bfloat16) for row in range(own_rows)]
        outer = jnp.dot(turned, jnp.concatenate(spread, 1), preferred_element_type=jnp.float32)
        for row in range(own_rows):
            place, is_near, rank, far = sources[row]
            prior = jnp.where(is_near, near_ref[rank, part], states_ref[place, part])
            for ref, is_far in zip(far_refs, far):
                prior = jnp.where(is_far, ref[0, part], prior)
            fresh = decay[row : row + 1, :] * prior.astype(jnp.float32)
            fresh = fresh + inverse[row : row + 1, :] * outer[:, row * size : (row + 1) * size]
            out_ref[row, part] = fresh.astype(jnp.bfloat16)


def last_update_kernel(
    recv_order, block, blocks, own_rows, partner, rank, me_ref, parent_ref, recv_ref, turned_ref, terms_ref, got_ref, old_ref,
    out_ref, new_ref, out_sem,
):
    heads, size = got_ref.shape[1], got_ref.shape[2]
    user, member = split(me_ref[0], blocks)
    child = matching_children(parent_ref, user, member, member ^ partner, own_rows, -1)[0][rank]
    line = lax.broadcasted_iota(jnp.int32, (recv_ref.shape[1], size), 0)

    def save(step):
        span = pl.ds(step * block, block)
        return pltpu.make_async_copy(new_ref.at[span], out_ref.at[jnp.maximum(child, 0), span], out_sem.at[step])

    @pl.when(child >= 0)
    def _():
        def work(step, carry):
            for part in range(block):
                head = step * block + part
                values = recv_ref[lane_of(recv_order, me_ref[0], head)][:, 2 * size :].astype(jnp.float32)
                value = jnp.where(line == child, values, 0.0).astype(jnp.bfloat16)
                outer = jnp.dot(turned_ref[head], value, preferred_element_type=jnp.float32)
                fresh = terms_ref[0, head, pl.ds(child, 1), :] * got_ref[0, head].astype(jnp.float32)
                fresh = fresh + terms_ref[1, head, pl.ds(child, 1), :] * outer
                new_ref[head] = fresh.astype(jnp.bfloat16)
            save(step).start()
            return carry

        lax.fori_loop(0, heads // block, work, 0)
        for step in range(heads // block):
            save(step).wait()


def per_device(
    token_ids,
    parents,
    states,
    embed_table,
    qkv_weight,
    gate_weight,
    gate_bias,
    norm_gain,
    out_weight,
):
    own_rows, heads, size = states.shape[0], states.shape[1], states.shape[2]
    width = heads * size
    columns = embed_table.shape[1]
    row_total = token_ids.shape[1]
    users, beam = parents.shape[1], parents.shape[2]
    blocks = beam // own_rows
    count = lax.axis_size("rows")
    me = lax.axis_index("rows").astype(jnp.int32)
    user, member = me // blocks, me % blocks
    plan = stage_plan(count)
    slots = own_rows + 4 * CAP
    state_slab = (CAP, heads, size, size)
    bf16, int32 = jnp.bfloat16, jnp.int32
    mine = me[None]
    parent_row = jnp.broadcast_to(parents.reshape(1, row_total), (8, row_total))
    head_block = math.gcd(heads, 4)

    one_state = (1, heads, size, size)
    local_columns, first_out = pl.pallas_call(
        functools.partial(fetch_kernel, blocks),
        in_specs=[SCALARS, SCALARS, SCALARS, WHOLE, PLACED, PLACED],
        out_specs=[WHOLE] * 2,
        out_shape=[pltpu.VMEM((row_total, columns), bf16), pltpu.VMEM(one_state, bf16)],
        scratch_shapes=[
            pltpu.VMEM((row_total * TILE, columns), bf16),
            pltpu.SemaphoreType.DMA,
            pltpu.SemaphoreType.DMA,
        ],
        compiler_params=params(),
        name="fetch",
    )(mine, in_hbm(parents), in_hbm(token_ids), in_hbm(token_ids), in_hbm(embed_table), in_hbm(states))

    recv_order, normed_order = plan_order(plan), gather_order(plan)
    piece_rows = 2 * (own_rows + 2 * CAP)
    moved = 2 * CAP + 1
    second_out, third_out, fourth_out, near_out, send_pick, place, low_pick, high_pick = pl.pallas_call(
        functools.partial(stage_kernel, blocks, slots, recv_order, normed_order),
        in_specs=[SCALARS, SCALARS, WHOLE, PLACED],
        out_specs=[PLACED] * 4 + [WHOLE] * 4,
        out_shape=[pltpu.HBM(one_state, bf16)] * 3
        + [
            pltpu.HBM(state_slab, bf16),
            jax.ShapeDtypeStruct((count * slots, row_total), bf16),
            jax.ShapeDtypeStruct((slots, 128), jnp.float32),
            jax.ShapeDtypeStruct((row_total, count * piece_rows), bf16),
            jax.ShapeDtypeStruct((row_total, count * piece_rows), bf16),
        ],
        scratch_shapes=[
            pltpu.VMEM((moved, heads, size, size), bf16),
            pltpu.SemaphoreType.DMA((moved,)),
            pltpu.SemaphoreType.DMA((moved,)),
        ],
        compiler_params=params(),
        name="stage",
    )(mine, in_hbm(parents), parent_row, in_hbm(states))
    sends = [first_out, second_out, third_out, fourth_out]
    arrivals = [(partner, rank) for partner in (2, 3) for rank in range(CAP)]
    gots = [xor_permute(block, partner) for block, (partner, _) in zip(sends, arrivals)]
    near_got = xor_permute(near_out, 1)

    weight = jnp.transpose(qkv_weight, (1, 0, 2))
    tied = {}

    def in_inputs(stage, parts):
        if stage == 0:
            *parts, tied["weight"], tied["pick"] = lax.optimization_barrier((*parts, weight, send_pick))
        if stage == 1:
            *parts, gots[0] = lax.optimization_barrier((*parts, gots[0]))
        return parts

    every_input = gather_all(local_columns, plan, in_inputs)
    pieces = pl.pallas_call(
        functools.partial(project_kernel, normed_order),
        in_specs=[SCALARS] + [WHOLE] * (2 + len(every_input)),
        out_specs=WHOLE,
        out_shape=jax.ShapeDtypeStruct((count * slots, 3 * columns), bf16),
        compiler_params=params(),
        name="project",
    )(mine, tied["weight"], tied["pick"], *every_input)

    def in_exchange(stage, parts):
        if stage == 1:
            *parts, gots[1] = lax.optimization_barrier((*parts, gots[1]))
        return parts

    received = exchange_all(pieces.reshape(count, slots, 3 * columns), plan, in_exchange)
    if columns != size:
        every_piece = jnp.stack(received, 1).reshape(count, slots, 3 * columns)
        places = jnp.array([recv_order.index(d) for d in range(count)], int32)[jnp.arange(count, dtype=int32) ^ me]
        every_piece = jnp.take(every_piece, places, axis=0).reshape(count, slots, 3, columns).transpose(1, 2, 0, 3)
        received = [every_piece.reshape(slots, 3, heads, size).transpose(2, 0, 1, 3).reshape(heads, slots, 3 * size)]
        recv_order = None

    by_heads = lambda rows: pl.BlockSpec((rows, head_block, size, size), lambda i: (0, i, 0, 0))
    normed, by_head = pl.pallas_call(
        functools.partial(readout_kernel, recv_order),
        grid=(heads // head_block,),
        in_specs=[SCALARS] * 2 + [WHOLE, by_heads(own_rows), by_heads(CAP)] + [WHOLE] * (2 + len(received)),
        out_specs=[WHOLE] * 2,
        out_shape=[
            jax.ShapeDtypeStruct((piece_rows, width // 2), bf16),
            jax.ShapeDtypeStruct((heads, slots, 3 * size), bf16),
        ],
        scratch_shapes=[pltpu.VMEM((heads, slots, size), jnp.float32)],
        compiler_params=params(),
        name="readout",
    )(mine, gate_bias, place, in_hbm(states), near_got, gate_weight, norm_gain.reshape(heads, size), *received)

    early = len(arrivals) - 1
    main_done, turned, terms = pl.pallas_call(
        functools.partial(main_update_kernel, recv_order, blocks, arrivals[:early]),
        grid=(heads // head_block,),
        in_specs=[SCALARS] * 3
        + [WHOLE, by_heads(own_rows), by_heads(CAP), WHOLE]
        + [by_heads(1)] * early,
        out_specs=[
            by_heads(own_rows),
            pl.BlockSpec((head_block, size, slots), lambda i: (i, 0, 0)),
            pl.BlockSpec((2, head_block, slots, size), lambda i: (0, i, 0, 0)),
        ],
        out_shape=[
            jax.ShapeDtypeStruct(states.shape, bf16),
            jax.ShapeDtypeStruct((heads, size, slots), bf16),
            jax.ShapeDtypeStruct((2, heads, slots, size), jnp.float32),
        ],
        compiler_params=params(),
        name="main_update",
    )(mine, parents, gate_bias, by_head, in_hbm(states), near_got, gate_weight, *gots[:early])

    def in_normed(stage, parts):
        if stage == 1:
            parts[-1], tied["done"], tied["turned"] = lax.optimization_barrier((parts[-1], main_done, turned))
        return parts

    every_normed = gather_all(normed, plan, in_normed)
    final = pl.pallas_call(
        functools.partial(last_update_kernel, recv_order, head_block, blocks, own_rows, *arrivals[early]),
        in_specs=[SCALARS] * 2 + [WHOLE] * 4 + [PLACED],
        out_specs=PLACED,
        out_shape=jax.ShapeDtypeStruct(states.shape, bf16),
        scratch_shapes=[pltpu.VMEM(one_state[1:], bf16), pltpu.SemaphoreType.DMA((heads // head_block,))],
        input_output_aliases={6: 0},
        compiler_params=params(),
        name="last_update",
    )(mine, parents, by_head, tied["turned"], terms, gots[early], tied["done"])
    layer_out = pl.pallas_call(
        output_kernel,
        in_specs=[WHOLE] * (4 + len(every_normed)),
        out_specs=WHOLE,
        out_shape=jax.ShapeDtypeStruct((row_total, columns), bf16),
        compiler_params=params(),
        name="output",
    )(local_columns, out_weight, low_pick, high_pick, *every_normed)
    return (layer_out[None], final)


def solution(mesh):
    placed = (
        P(None, "groups"),
        P(None, "groups", None),
        P(("groups", "rows"), None, None, None),
        P(None, "rows"),
        P(None, None, "rows"),
        P(),
        P(),
        P(),
        P(None, "rows"),
    )
    return jax.shard_map(
        per_device,
        mesh=mesh,
        in_specs=placed,
        out_specs=(P(None, "groups", "rows"), P(("groups", "rows"), None, None, None)),
        check_vma=False,
    )
```

```python
import functools
import math

import jax
import jax.numpy as jnp
from jax import lax
from jax.experimental import pallas as pl
from jax.experimental.pallas import tpu as pltpu
from jax.sharding import PartitionSpec as P

CAP = 2
TILE = 16
VMEM_BYTES = 24 * 1024 * 1024
WHOLE = pl.BlockSpec(memory_space=pltpu.VMEM)
SCALARS = pl.BlockSpec(memory_space=pltpu.SMEM)
PLACED = pl.BlockSpec(memory_space=pl.ANY)


def params():
    return pltpu.CompilerParams(vmem_limit_bytes=VMEM_BYTES)


def in_hbm(array):
    return pltpu.with_memory_space_constraint(array, pltpu.HBM)


def in_vmem(array):
    return pltpu.with_memory_space_constraint(array, pltpu.VMEM)


def xor_permute(block, distance):
    count = lax.axis_size("rows")
    return lax.ppermute(block, "rows", [(i, i ^ distance) for i in range(count)])


def stage_plan(count):
    if count == 1:
        return []
    if count == 2:
        return [[1]]
    if count == 4:
        return [[2], [1]]
    plan = [[6], [4, 8, 12] if count >= 16 else [4]]
    bit = 16
    while bit < count:
        plan.append([bit])
        bit *= 2
    return plan + [[1]]


def plan_order(plan):
    order = [0]
    for stage in plan:
        order = [near ^ far for near in order for far in [0] + stage]
    return order


def gather_order(plan):
    order = [0]
    for stage in plan:
        order = [near ^ far for far in [0] + stage for near in order]
    return order


def gather_all(block, plan, after=lambda stage, held: held):
    held = [block]
    for number, stage in enumerate(plan):
        held = held + [xor_permute(part, distance) for distance in stage for part in held]
        if len(held) == 2:
            held = [jnp.concatenate(held, 0)]
        held = after(number, held)
    return held


def exchange_plan(plan):
    return plan[-1:] + plan[:-1]


def exchange_all(pieces, plan, before=lambda stage, place, slab: slab, after=lambda stage, held: held):
    tail = pieces.shape[1:]
    held = [pieces.reshape(tuple(len(stage) + 1 for stage in plan) + tail)]
    for axis, stage in enumerate(plan):
        fresh = []
        for part in held:
            slabs = [lax.index_in_dim(part, place, axis, keepdims=True) for place in range(len(stage) + 1)]
            fresh.append(slabs[0])
            fresh += [xor_permute(before(axis, place, slabs[place + 1]), far) for place, far in enumerate(stage)]
        held = after(axis, fresh if axis == len(plan) - 1 else [jnp.concatenate(fresh, axis)])
    return [part.reshape((-1,) + tail) for part in held]


def split(number, size):
    if size & (size - 1) == 0:
        return lax.shift_right_logical(number, size.bit_length() - 1), number & (size - 1)
    return lax.div(number, size), lax.rem(number, size)


def place_in(order, distance):
    place, bit = distance & 0, 0
    while 1 << bit < len(order):
        place = place ^ ((lax.shift_right_logical(distance, bit) & 1) * order.index(1 << bit))
        bit += 1
    return place


def row_facts(parent_row, blocks, own_rows):
    lane = lax.broadcasted_iota(jnp.int32, parent_row.shape, 1)
    device, child = split(lane, own_rows)
    parent_block, parent_place = split(parent_row, own_rows)
    rank = jnp.zeros_like(lane)
    for earlier in range(1, own_rows):
        same = (pltpu.roll(parent_block, earlier, 1) == parent_block) & (child >= earlier)
        rank = rank + same.astype(jnp.int32)
    return device, child, parent_block ^ (device & (blocks - 1)), rank, parent_place


def column_of(row):
    spread = jnp.broadcast_to(row[0:1].astype(jnp.float32), (8, row.shape[1]))
    return jnp.transpose(spread)[:, 0:1]


def chosen_rows(column, width):
    shape = (column.shape[0], width)
    return (lax.broadcasted_iota(jnp.int32, shape, 1).astype(jnp.float32) == column).astype(jnp.float32)


def matching_children(parent_ref, user, child_block, parent_block, own_rows, none):
    children, parents, found = [jnp.int32(none)] * CAP, [jnp.int32(0)] * CAP, jnp.int32(0)
    for child in range(own_rows):
        block, place = split(parent_ref[0, user, child_block * own_rows + child], own_rows)
        hit = block == parent_block
        for j in range(CAP):
            children[j] = jnp.where(hit & (found == j), child, children[j])
            parents[j] = jnp.where(hit & (found == j), place, parents[j])
        found = found + hit.astype(jnp.int32)
    return children, parents


def fetch_kernel(
    blocks, me_ref, parent_ref, token_ref, tokens_ref, table_ref, states_ref, x_ref, first_ref, rows_ref, row_sem, state_sem
):
    count, own_rows = token_ref.shape[1], states_ref.shape[0]
    user, member = split(me_ref[0], blocks)
    _, chosen = matching_children(parent_ref, user, member ^ 2, member, own_rows, 0)
    state_copy = pltpu.make_async_copy(states_ref.at[chosen[0]], first_ref.at[0], state_sem)
    state_copy.start()

    def start_row(r, carry):
        first = pl.multiple_of(split(token_ref[0, r], TILE)[0] * TILE, TILE)
        pltpu.make_async_copy(
            table_ref.at[pl.ds(first, TILE)],
            rows_ref.at[pl.ds(pl.multiple_of(r * TILE, TILE), TILE)],
            row_sem,
        ).start()
        return carry

    lax.fori_loop(0, count, start_row, 0, unroll=8)
    step = math.gcd(count, 128)
    picks = []
    for first in range(0, count, step):
        low = column_of(split(tokens_ref[:, first : first + step], TILE)[1])
        wanted = low + lax.broadcasted_iota(jnp.int32, (step, 1), 0).astype(jnp.float32) * TILE
        picks.append(chosen_rows(wanted, step * TILE).astype(jnp.bfloat16))
    pltpu.make_async_copy(table_ref.at[pl.ds(0, count * TILE)], rows_ref, row_sem).wait()
    for first, pick in zip(range(0, count, step), picks):
        x_ref[first : first + step, :] = jnp.dot(
            pick, rows_ref[first * TILE : (first + step) * TILE, :], preferred_element_type=jnp.float32
        ).astype(jnp.bfloat16)
    state_copy.wait()


def pick_kernel(
    blocks, piece, send_order, me_ref, parent_ref, parents_ref, states_ref, pick_ref, second_ref, sem
):
    me, rows, own_rows = me_ref[0], parents_ref.shape[1], states_ref.shape[0]
    user, member = split(me, blocks)
    chosen = matching_children(parent_ref, user, member ^ 2, member, own_rows, 0)[1][1]
    copy = pltpu.make_async_copy(states_ref.at[chosen], second_ref.at[0], sem)
    copy.start()
    device, child, away, rank, _ = row_facts(parents_ref[...], blocks, own_rows)
    own = place_in(send_order, device ^ me) * piece + child
    far = place_in(send_order, device ^ away ^ me) * piece + 3 * own_rows + rank
    line = lax.broadcasted_iota(jnp.int32, (len(send_order) * piece, rows), 0)
    for slab in range(3):
        far_line = jnp.where(away == 3, far + slab * CAP, -1)
        chosen = (line == own[0:1] + slab * own_rows) | (line == far_line[0:1])
        pick_ref[:, slab * rows : (slab + 1) * rows] = chosen.astype(jnp.float32).astype(jnp.bfloat16)
    copy.wait()


def stage_kernel(
    blocks, normed_order, me_ref, parent_ref, parents_ref, states_ref, *refs
):
    outs, (place_ref, pick_ref, hold_ref, in_sem, out_sem) = refs[:-5], refs[-5:]
    me, own_rows = me_ref[0], states_ref.shape[0]
    user, member = split(me, blocks)
    wanted = []
    for partner in (3, 1):
        wanted += matching_children(parent_ref, user, member ^ partner, member, own_rows, 0)[1]
    targets = [ref.at[slot] for ref in outs for slot in range(ref.shape[0])]
    loads, saves = [], []
    for place, (row, target) in enumerate(zip(wanted, targets)):
        loads.append(pltpu.make_async_copy(states_ref.at[row], hold_ref.at[place], in_sem.at[place]))
        saves.append(pltpu.make_async_copy(hold_ref.at[place], target, out_sem.at[place]))
        loads[-1].start()
    device, child, away, rank, parent_place = row_facts(parents_ref[...], blocks, own_rows)
    line = lax.broadcasted_iota(jnp.int32, (place_ref.shape[0], parents_ref.shape[1]), 0)
    own = (line == jnp.where((device == me) & (away < 3), child, -1)[0:1]).astype(jnp.float32)
    far = (line == jnp.where((device ^ away == me) & (away == 3), own_rows + rank, -1)[0:1]).astype(jnp.float32)
    near_place = jnp.where(away == 0, parent_place, own_rows + (away - 1) * CAP + rank)
    place = own * (near_place[0:1] + 1).astype(jnp.float32) + far * (parent_place[0:1] + 1).astype(jnp.float32)
    place_ref[...] = jnp.broadcast_to(jnp.sum(place, axis=1, keepdims=True) - 1.0, place_ref.shape)
    for load, save in zip(loads, saves):
        load.wait()
        save.start()
    total = len(normed_order) * own_rows
    first = place_in(normed_order, jnp.where(away == 3, device ^ away, device) ^ me) * own_rows
    quarters = own_rows // CAP
    for part in range(1 + quarters):
        if part == 0:
            index = jnp.where(away == 3, -1, first + child)
        else:
            index = jnp.where(away == 3, first + rank * quarters + part - 1, -1)
        pick_ref[:, part * total : (part + 1) * total] = chosen_rows(column_of(index), total).astype(jnp.bfloat16)
    for save in saves:
        save.wait()


def hold_kernel(states_ref, held_ref, sem):
    copies = [pltpu.make_async_copy(states_ref.at[row], held_ref.at[row], sem.at[row]) for row in range(states_ref.shape[0])]
    for copy in copies:
        copy.start()
    for copy in copies:
        copy.wait()


def project_kernel(order, me_ref, weight_ref, pick_ref, *refs):
    held, out_ref = refs[:-1], refs[-1]
    me, columns, parts = me_ref[0], held[0].shape[1], len(held)
    rows = pick_ref.shape[1] // 3
    total = [None] * 3
    for place, distance in enumerate(order):
        ref, within = held[place * parts // len(order)], place % (len(order) // parts)
        block = ref[within * rows : (within + 1) * rows, :]
        first = pl.multiple_of((me ^ distance) * columns, columns)
        for slab in range(3):
            term = jnp.dot(block, weight_ref[slab, pl.ds(first, columns), :], preferred_element_type=jnp.float32)
            total[slab] = term if total[slab] is None else total[slab] + term
    every = jnp.concatenate([part.astype(jnp.bfloat16) for part in total], 0)
    out_ref[...] = jnp.dot(pick_ref[...], every, preferred_element_type=jnp.float32).astype(jnp.bfloat16)


def head_rows(piece, own_rows):
    piece = piece.astype(jnp.float32)
    far = piece[3 * own_rows : 4 * own_rows]
    slabs = []
    for slab in range(3):
        shifted = far if slab == 0 else pltpu.roll(far, own_rows - slab * CAP, 0)
        slabs.append(jnp.concatenate([piece[slab * own_rows : (slab + 1) * own_rows], shifted], 0))
    return slabs


def head_factors(keys, gate_row, bias, size):
    logit = jnp.sum(keys * gate_row, axis=-1, keepdims=True) / math.sqrt(size) + bias
    decay = 1.0 / (1.0 + jnp.exp(-logit))
    return decay, lax.rsqrt(jnp.sum(keys * keys, axis=-1, keepdims=True) + 1e-06)


def lane_of(recv_order, me, head):
    return head if recv_order is None else place_in(recv_order, me ^ head)


def readout_kernel(recv_order, block, near_count, me_ref, bias_ref, place_ref, gate_ref, gain_ref, *refs):
    sources, parts, (out_ref, recv_ref, norm_ref) = refs[:near_count], refs[near_count:-3], refs[-3:]
    own_rows, heads, size = sources[0].shape[0], sources[0].shape[1], sources[0].shape[2]
    slots = place_ref.shape[0]
    for number, part in enumerate(parts):
        for within in range(part.shape[0]):
            recv_ref[within * len(parts) + number] = part[within]
    place = place_ref[:, 0:1]
    joint = math.gcd(block, 2)
    states = sum(ref.shape[0] for ref in sources)

    def work(step, carry):
        for group in range(0, block, joint):
            first_head = step * block + group
            rows = [
                head_rows(recv_ref[lane_of(recv_order, me_ref[0], first_head + n)], own_rows) for n in range(joint)
            ]
            spread = [
                jnp.concatenate([jnp.where(place == float(p), row[0], 0.0).astype(jnp.bfloat16) for p in range(states)], 1)
                for row in rows
            ]
            priors = []
            for n in range(joint):
                one = [ref[:, pl.ds(first_head + n, 1)].reshape(ref.shape[0] * size, size) for ref in sources]
                priors.append(jnp.concatenate(one, 0))
            product = jnp.dot(
                jnp.concatenate(spread, 0), jnp.concatenate(priors, 1), preferred_element_type=jnp.float32
            )
            for n in range(joint):
                head = first_head + n
                queries, keys, values = rows[n]
                decay, inverse = head_factors(keys, gate_ref[pl.ds(head, 1), :], bias_ref[head], size)
                overlap = jnp.sum(queries * keys, axis=-1, keepdims=True) * inverse
                readout = decay * product[n * slots : (n + 1) * slots, n * size : (n + 1) * size] + overlap * values
                scale = lax.rsqrt(jnp.mean(readout * readout, axis=-1, keepdims=True) + 1e-05)
                norm_ref[head] = readout * scale * gain_ref[pl.ds(head, 1), :]
        return carry

    lax.fori_loop(0, heads // block, work, 0)
    quarters = own_rows // CAP
    share = heads // quarters
    own = [norm_ref[h][:own_rows] for h in range(heads)]
    far = []
    for rank in range(CAP):
        for quarter in range(quarters):
            line = slice(own_rows + rank, own_rows + rank + 1)
            far.append(jnp.concatenate([norm_ref[h][line] for h in range(quarter * share, (quarter + 1) * share)], 1))
    out_ref[...] = jnp.concatenate(own + [jnp.concatenate(far, 0)], 1).astype(jnp.bfloat16)


def output_kernel(own_rows, x_ref, weight_ref, pick_ref, *refs):
    parts, out_ref = refs[:-1], refs[-1]
    width, columns = weight_ref.shape[0], x_ref.shape[1]
    quarters = own_rows // CAP
    share = width // quarters
    gathered = jnp.concatenate([part[...] for part in parts], 0)
    own = jnp.dot(gathered[:, :width], weight_ref[...], preferred_element_type=jnp.float32)
    weight = jnp.concatenate([weight_ref[q * share : (q + 1) * share, :] for q in range(quarters)], 1)
    far = jnp.dot(gathered[:, width:], weight, preferred_element_type=jnp.float32)
    rest = jnp.concatenate([own] + [far[:, q * columns : (q + 1) * columns] for q in range(quarters)], 0)
    total = x_ref[...].astype(jnp.float32)
    for _ in range(3):
        term = rest.astype(jnp.bfloat16)
        rest = rest - term.astype(jnp.float32)
        total = total + jnp.dot(pick_ref[...], term, preferred_element_type=jnp.float32)
    out_ref[...] = total.astype(jnp.bfloat16)


def near_update_kernel(
    recv_order, block, blocks, me_ref, parent_ref, bias_ref, recv_ref, gate_ref, states_ref, *refs
):
    near_refs, (out_ref, turned_ref, values_ref, terms_ref, new_ref, out_sem) = refs[:CAP], refs[CAP:]
    own_rows, heads, size = states_ref.shape[0], states_ref.shape[1], states_ref.shape[2]
    slots = values_ref.shape[1]
    user, member = split(me_ref[0], blocks)

    def prepare(step, carry):
        for part in range(block):
            head = step * block + part
            _, keys, values = head_rows(recv_ref[lane_of(recv_order, me_ref[0], head)], own_rows)
            decay, inverse = head_factors(keys, gate_ref[pl.ds(head, 1), :], bias_ref[head], size)
            turned_ref[head] = jnp.transpose(keys).astype(jnp.bfloat16)
            values_ref[head] = values
            terms_ref[0, head] = jnp.broadcast_to(decay, (slots, size))
            terms_ref[1, head] = jnp.broadcast_to(inverse, (slots, size))
        return carry

    lax.fori_loop(0, heads // block, prepare, 0)
    line = lax.broadcasted_iota(jnp.int32, (slots, size), 0)

    def save(row):
        return pltpu.make_async_copy(new_ref.at[row], out_ref.at[row], out_sem.at[row])

    def facts(row):
        parent_block, place = split(parent_ref[0, user, member * own_rows + row], own_rows)
        return parent_block ^ member, place

    def update(row, prior_of):
        for head in range(heads):
            value = jnp.where(line == row, values_ref[head], 0.0).astype(jnp.bfloat16)
            outer = jnp.dot(turned_ref[head], value, preferred_element_type=jnp.float32)
            fresh = terms_ref[0, head, pl.ds(row, 1), :] * prior_of(head).astype(jnp.float32)
            fresh = fresh + terms_ref[1, head, pl.ds(row, 1), :] * outer
            new_ref[row, head] = fresh.astype(jnp.bfloat16)
        save(row).start()

    def work(row, found):
        away, place = facts(row)

        @pl.when(away == 0)
        def _():
            update(row, lambda head: states_ref[place, head])

        for rank, ref in enumerate(near_refs):

            @pl.when((away == 1) & (found == rank))
            def _():
                update(row, lambda head: ref[0, head])

        return found + (away == 1).astype(jnp.int32)

    lax.fori_loop(0, own_rows, work, jnp.int32(0))

    def finish(row, carry):
        @pl.when(facts(row)[0] < 2)
        def _():
            save(row).wait()

        return carry

    lax.fori_loop(0, own_rows, finish, 0)


def far_update_kernel(block, blocks, own_rows, entries, me_ref, parent_ref, turned_ref, values_ref, terms_ref, *refs):
    gots, (_, out_ref, new_ref, out_sem) = refs[:-4], refs[-4:]
    heads, size = gots[0].shape[1], gots[0].shape[2]
    user, member = split(me_ref[0], blocks)
    children = [
        matching_children(parent_ref, user, member, member ^ partner, own_rows, -1)[0][rank] for _, _, partner, rank in entries
    ]
    line = lax.broadcasted_iota(jnp.int32, (values_ref.shape[1], size), 0)

    def save(entry, step):
        span = pl.ds(step * block, block)
        target = out_ref.at[jnp.maximum(children[entry], 0), span]
        return pltpu.make_async_copy(new_ref.at[entry, span], target, out_sem.at[entry, step])

    for entry, (array, within, _, _) in enumerate(entries):
        got_ref, child = gots[array], children[entry]

        @pl.when(child >= 0)
        def _():
            for step in range(heads // block):
                for head in range(step * block, (step + 1) * block):
                    value = jnp.where(line == child, values_ref[head], 0.0).astype(jnp.bfloat16)
                    outer = jnp.dot(turned_ref[head], value, preferred_element_type=jnp.float32)
                    fresh = terms_ref[0, head, pl.ds(child, 1), :] * got_ref[within, head].astype(jnp.float32)
                    fresh = fresh + terms_ref[1, head, pl.ds(child, 1), :] * outer
                    new_ref[entry, head] = fresh.astype(jnp.bfloat16)
                save(entry, step).start()

    for entry in range(len(entries)):

        @pl.when(children[entry] >= 0)
        def _():
            for step in range(heads // block):
                save(entry, step).wait()


def per_device(
    token_ids,
    parents,
    states,
    embed_table,
    qkv_weight,
    gate_weight,
    gate_bias,
    norm_gain,
    out_weight,
):
    own_rows, heads, size = states.shape[0], states.shape[1], states.shape[2]
    width = heads * size
    columns = embed_table.shape[1]
    row_total = token_ids.shape[1]
    users, beam = parents.shape[1], parents.shape[2]
    blocks = beam // own_rows
    count = lax.axis_size("rows")
    me = lax.axis_index("rows").astype(jnp.int32)
    user, member = me // blocks, me % blocks
    plan = stage_plan(count)
    steps = exchange_plan(plan)
    recv_order, normed_order = plan_order(steps), gather_order(plan)
    slots, piece = 2 * own_rows, 4 * own_rows
    one_state, two_states = (1, heads, size, size), (CAP, heads, size, size)
    normed_columns = width + CAP * width // own_rows
    bf16, int32 = jnp.bfloat16, jnp.int32
    mine = me[None]
    parent_row = jnp.broadcast_to(parents.reshape(1, row_total), (8, row_total))
    head_block = math.gcd(heads, 4)

    local_columns, first_out = pl.pallas_call(
        functools.partial(fetch_kernel, blocks),
        in_specs=[SCALARS, SCALARS, SCALARS, WHOLE, PLACED, PLACED],
        out_specs=[WHOLE] * 2,
        out_shape=[pltpu.VMEM((row_total, columns), bf16), pltpu.VMEM(one_state, bf16)],
        scratch_shapes=[
            pltpu.VMEM((row_total * TILE, columns), bf16),
            pltpu.SemaphoreType.DMA,
            pltpu.SemaphoreType.DMA,
        ],
        compiler_params=params(),
        name="fetch",
    )(mine, in_hbm(parents), in_hbm(token_ids), in_hbm(token_ids), in_hbm(embed_table), in_hbm(states))
    first_got = xor_permute(first_out, 2)

    send_pick, second_out = pl.pallas_call(
        functools.partial(pick_kernel, blocks, piece, recv_order),
        in_specs=[SCALARS, SCALARS, WHOLE, PLACED],
        out_specs=[WHOLE] * 2,
        out_shape=[jax.ShapeDtypeStruct((count * piece, 3 * row_total), bf16), pltpu.VMEM(one_state, bf16)],
        scratch_shapes=[pltpu.SemaphoreType.DMA],
        compiler_params=params(),
        name="pick",
    )(mine, in_hbm(parents), parent_row, in_hbm(states))
    second_got = xor_permute(second_out, 2)

    corner_out, *near_outs, place, out_pick = pl.pallas_call(
        functools.partial(stage_kernel, blocks, normed_order),
        in_specs=[SCALARS, SCALARS, WHOLE, PLACED],
        out_specs=[PLACED] * (1 + CAP) + [WHOLE] * 2,
        out_shape=[pltpu.HBM(two_states, bf16)]
        + [pltpu.HBM(one_state, bf16)] * CAP
        + [
            jax.ShapeDtypeStruct((slots, 128), jnp.float32),
            jax.ShapeDtypeStruct((row_total, (1 + own_rows // CAP) * row_total), bf16),
        ],
        scratch_shapes=[
            pltpu.VMEM((2 * CAP, heads, size, size), bf16),
            pltpu.SemaphoreType.DMA((2 * CAP,)),
            pltpu.SemaphoreType.DMA((2 * CAP,)),
        ],
        compiler_params=params(),
        name="stage",
    )(mine, in_hbm(parents), parent_row, in_hbm(states))
    corner_got = xor_permute(corner_out, 3)
    near_gots = [xor_permute(block, 1) for block in near_outs]

    held = pl.pallas_call(
        hold_kernel,
        in_specs=[PLACED],
        out_specs=WHOLE,
        out_shape=pltpu.VMEM(states.shape, bf16),
        scratch_shapes=[pltpu.SemaphoreType.DMA((own_rows,))],
        compiler_params=params(),
        name="hold",
    )(in_hbm(states))

    weight = jnp.transpose(qkv_weight, (1, 0, 2))
    tied = {}

    def in_inputs(stage, parts):
        if stage == 0:
            *parts, tied["weight"], tied["pick"] = lax.optimization_barrier((*parts, weight, send_pick))
        if stage == 1:
            *parts, tied["first"], tied["place"] = lax.optimization_barrier((*parts, first_got, place))
        return parts

    every_input = gather_all(local_columns, plan, in_inputs)
    pieces = pl.pallas_call(
        functools.partial(project_kernel, normed_order),
        in_specs=[SCALARS] + [WHOLE] * (2 + len(every_input)),
        out_specs=WHOLE,
        out_shape=jax.ShapeDtypeStruct((count * piece, columns), bf16),
        compiler_params=params(),
        name="project",
    )(mine, tied["weight"], tied["pick"], *every_input)

    def before_exchange(stage, place, slab):
        if stage == 2 and place == 0:
            slab, tied["second"] = lax.optimization_barrier((slab, second_got))
        return slab

    def in_exchange(stage, parts):
        if stage == 1:
            *parts, tied["near"], tied["nearer"] = lax.optimization_barrier((*parts, *near_gots))
        return parts

    received = exchange_all(pieces.reshape(count, piece, columns), steps, before_exchange, in_exchange)
    if columns != size:
        every_piece = jnp.stack(received, 1).reshape(count, piece, columns)
        places = jnp.array([recv_order.index(d) for d in range(count)], int32)[jnp.arange(count, dtype=int32) ^ me]
        every_piece = jnp.take(every_piece, places, axis=0).transpose(1, 0, 2).reshape(piece, heads, size)
        received = [every_piece.transpose(1, 0, 2)]
        recv_order = None

    held, near_gots = in_vmem(held), [tied["near"], tied["nearer"]]
    sources = [held, *near_gots, tied["first"], tied["second"]]
    normed, by_head = pl.pallas_call(
        functools.partial(readout_kernel, recv_order, head_block, len(sources)),
        in_specs=[SCALARS] * 2 + [WHOLE] * (3 + len(sources) + len(received)),
        out_specs=[WHOLE] * 2,
        out_shape=[
            jax.ShapeDtypeStruct((own_rows, normed_columns), bf16),
            jax.ShapeDtypeStruct((heads, piece, size), bf16),
        ],
        scratch_shapes=[pltpu.VMEM((heads, slots, size), jnp.float32)],
        compiler_params=params(),
        name="readout",
    )(mine, gate_bias, tied["place"], gate_weight, norm_gain.reshape(heads, size), *sources, *received)

    near_done, turned, values, terms = pl.pallas_call(
        functools.partial(near_update_kernel, recv_order, head_block, blocks),
        in_specs=[SCALARS] * 3 + [WHOLE] * (3 + CAP),
        out_specs=[PLACED] + [WHOLE] * 3,
        out_shape=[
            pltpu.HBM(states.shape, bf16),
            jax.ShapeDtypeStruct((heads, size, slots), bf16),
            jax.ShapeDtypeStruct((heads, slots, size), jnp.float32),
            jax.ShapeDtypeStruct((2, heads, slots, size), jnp.float32),
        ],
        scratch_shapes=[pltpu.VMEM(states.shape, bf16), pltpu.SemaphoreType.DMA((own_rows,))],
        compiler_params=params(),
        name="near_update",
    )(mine, parents, gate_bias, by_head, gate_weight, held, *near_gots)

    def far_update(before, gots, entries, name):
        return pl.pallas_call(
            functools.partial(far_update_kernel, head_block, blocks, own_rows, entries),
            in_specs=[SCALARS] * 2 + [WHOLE] * (3 + len(gots)) + [PLACED],
            out_specs=PLACED,
            out_shape=jax.ShapeDtypeStruct(states.shape, bf16),
            scratch_shapes=[
                pltpu.VMEM((len(entries),) + one_state[1:], bf16),
                pltpu.SemaphoreType.DMA((len(entries), heads // head_block)),
            ],
            input_output_aliases={5 + len(gots): 0},
            compiler_params=params(),
            name=name,
        )(mine, parents, tied["turned"], values, terms, *gots, before)

    def in_normed(stage, parts):
        if stage == 0:
            *parts, tied["rows"], tied["turned"] = lax.optimization_barrier((*parts, near_done, turned))
        if stage == 1:
            entries = [(rank, 0, 2, rank) for rank in range(CAP)]
            far_done = far_update(tied["rows"], [tied["first"], tied["second"]], entries, "far_update")
            ends = (parts[-1], far_done, corner_got)
            parts[-1], tied["done"], tied["corner"] = lax.optimization_barrier(ends)
        return parts

    every_normed = gather_all(normed, plan, in_normed)
    final = far_update(tied["done"], [tied["corner"]], [(0, rank, 3, rank) for rank in range(CAP)], "last_update")
    layer_out = pl.pallas_call(
        functools.partial(output_kernel, own_rows),
        in_specs=[WHOLE] * (3 + len(every_normed)),
        out_specs=WHOLE,
        out_shape=jax.ShapeDtypeStruct((row_total, columns), bf16),
        compiler_params=params(),
        name="output",
    )(local_columns, out_weight, out_pick, *every_normed)
    return (layer_out[None], final)


def solution(mesh):
    placed = (
        P(None, "groups"),
        P(None, "groups", None),
        P(("groups", "rows"), None, None, None),
        P(None, "rows"),
        P(None, None, "rows"),
        P(),
        P(),
        P(),
        P(None, "rows"),
    )
    return jax.shard_map(
        per_device,
        mesh=mesh,
        in_specs=placed,
        out_specs=(P(None, "groups", "rows"), P(("groups", "rows"), None, None, None)),
        check_vma=False,
    )
```

```python
import functools
import math

import jax
import jax.numpy as jnp
from jax import lax
from jax.experimental import pallas as pl
from jax.experimental.pallas import tpu as pltpu
from jax.sharding import PartitionSpec as P

CAP = 2
FARS = 2 * CAP - 1
TILE = 16
VMEM_BYTES = 24 * 1024 * 1024
WHOLE = pl.BlockSpec(memory_space=pltpu.VMEM)
SCALARS = pl.BlockSpec(memory_space=pltpu.SMEM)
PLACED = pl.BlockSpec(memory_space=pl.ANY)


def params():
    return pltpu.CompilerParams(vmem_limit_bytes=VMEM_BYTES)


def in_hbm(array):
    return pltpu.with_memory_space_constraint(array, pltpu.HBM)


def in_vmem(array):
    return pltpu.with_memory_space_constraint(array, pltpu.VMEM)


def xor_permute(block, distance):
    count = lax.axis_size("rows")
    return lax.ppermute(block, "rows", [(i, i ^ distance) for i in range(count)])


def stage_plan(count):
    if count == 1:
        return []
    if count == 2:
        return [[1]]
    if count == 4:
        return [[2], [1]]
    plan = [[6], [4, 8, 12] if count >= 16 else [4]]
    bit = 16
    while bit < count:
        plan.append([bit])
        bit *= 2
    return plan + [[1]]


def plan_order(plan):
    order = [0]
    for stage in plan:
        order = [near ^ far for near in order for far in [0] + stage]
    return order


def gather_order(plan):
    order = [0]
    for stage in plan:
        order = [near ^ far for far in [0] + stage for near in order]
    return order


def gather_all(block, plan, after=lambda stage, held: held):
    held = [block]
    for number, stage in enumerate(plan):
        held = held + [xor_permute(part, distance) for distance in stage for part in held]
        if len(held) == 2:
            held = [jnp.concatenate(held, 0)]
        held = after(number, held)
    return held


def exchange_plan(plan):
    return plan[-1:] + plan[:-1]


def exchange_all(pieces, plan, after=lambda stage, held: held):
    tail = pieces.shape[1:]
    held = [pieces.reshape(tuple(len(stage) + 1 for stage in plan) + tail)]
    for axis, stage in enumerate(plan):
        fresh = []
        for part in held:
            slabs = [lax.index_in_dim(part, place, axis, keepdims=True) for place in range(len(stage) + 1)]
            fresh.append(slabs[0])
            fresh += [xor_permute(slab, distance) for slab, distance in zip(slabs[1:], stage)]
        held = after(axis, fresh if axis == len(plan) - 1 else [jnp.concatenate(fresh, axis)])
    return [part.reshape((-1,) + tail) for part in held]


def split(number, size):
    if size & (size - 1) == 0:
        return lax.shift_right_logical(number, size.bit_length() - 1), number & (size - 1)
    return lax.div(number, size), lax.rem(number, size)


def place_in(order, distance):
    place, bit = distance & 0, 0
    while 1 << bit < len(order):
        place = place ^ ((lax.shift_right_logical(distance, bit) & 1) * order.index(1 << bit))
        bit += 1
    return place


def row_facts(parent_row, blocks, own_rows):
    lane = lax.broadcasted_iota(jnp.int32, parent_row.shape, 1)
    device, child = split(lane, own_rows)
    parent_block, parent_place = split(parent_row, own_rows)
    rank = jnp.zeros_like(lane)
    for earlier in range(1, own_rows):
        same = (pltpu.roll(parent_block, earlier, 1) == parent_block) & (child >= earlier)
        rank = rank + same.astype(jnp.int32)
    return device, child, parent_block ^ (device & (blocks - 1)), rank, parent_place


def far_number(away, rank):
    return (away == 3) | ((away == 2) & (rank > 0)), jnp.where(away == 3, rank, CAP + rank - 1)


def column_of(row):
    spread = jnp.broadcast_to(row[0:1].astype(jnp.float32), (8, row.shape[1]))
    return jnp.transpose(spread)[:, 0:1]


def chosen_rows(column, width):
    shape = (column.shape[0], width)
    return (lax.broadcasted_iota(jnp.int32, shape, 1).astype(jnp.float32) == column).astype(jnp.float32)


def matching_children(parent_ref, user, child_block, parent_block, own_rows, none):
    children, parents, found = [jnp.int32(none)] * CAP, [jnp.int32(0)] * CAP, jnp.int32(0)
    for child in range(own_rows):
        block, place = split(parent_ref[0, user, child_block * own_rows + child], own_rows)
        hit = block == parent_block
        for j in range(CAP):
            children[j] = jnp.where(hit & (found == j), child, children[j])
            parents[j] = jnp.where(hit & (found == j), place, parents[j])
        found = found + hit.astype(jnp.int32)
    return children, parents


def fetch_kernel(
    blocks, me_ref, parent_ref, token_ref, tokens_ref, table_ref, states_ref, x_ref, first_ref, rows_ref, row_sem, state_sem
):
    count, own_rows = token_ref.shape[1], states_ref.shape[0]
    user, member = split(me_ref[0], blocks)
    _, chosen = matching_children(parent_ref, user, member ^ 2, member, own_rows, 0)
    state_copy = pltpu.make_async_copy(states_ref.at[chosen[0]], first_ref.at[0], state_sem)
    state_copy.start()

    def start_row(r, carry):
        first = pl.multiple_of(split(token_ref[0, r], TILE)[0] * TILE, TILE)
        pltpu.make_async_copy(
            table_ref.at[pl.ds(first, TILE)],
            rows_ref.at[pl.ds(pl.multiple_of(r * TILE, TILE), TILE)],
            row_sem,
        ).start()
        return carry

    lax.fori_loop(0, count, start_row, 0, unroll=8)
    step = math.gcd(count, 128)
    picks = []
    for first in range(0, count, step):
        low = column_of(split(tokens_ref[:, first : first + step], TILE)[1])
        wanted = low + lax.broadcasted_iota(jnp.int32, (step, 1), 0).astype(jnp.float32) * TILE
        picks.append(chosen_rows(wanted, step * TILE).astype(jnp.bfloat16))
    pltpu.make_async_copy(table_ref.at[pl.ds(0, count * TILE)], rows_ref, row_sem).wait()
    for first, pick in zip(range(0, count, step), picks):
        x_ref[first : first + step, :] = jnp.dot(
            pick, rows_ref[first * TILE : (first + step) * TILE, :], preferred_element_type=jnp.float32
        ).astype(jnp.bfloat16)
    state_copy.wait()


def pick_kernel(blocks, piece, send_order, me_ref, parent_ref, parents_ref, states_ref, pick_ref, corner_ref, sem):
    me, rows, own_rows = me_ref[0], parents_ref.shape[1], states_ref.shape[0]
    user, member = split(me, blocks)
    copies = []
    for slot, row in enumerate(matching_children(parent_ref, user, member ^ 3, member, own_rows, 0)[1]):
        copies.append(pltpu.make_async_copy(states_ref.at[row], corner_ref.at[slot], sem.at[slot]))
        copies[-1].start()
    device, child, away, rank, _ = row_facts(parents_ref[...], blocks, own_rows)
    is_far, number = far_number(away, rank)
    own = place_in(send_order, device ^ me) * piece + child
    far = place_in(send_order, device ^ away ^ me) * piece + 3 * own_rows + number
    line = lax.broadcasted_iota(jnp.int32, (len(send_order) * piece, rows), 0)
    for slab in range(3):
        far_line = jnp.where(is_far, far + slab * FARS, -1)
        chosen = (line == own[0:1] + slab * own_rows) | (line == far_line[0:1])
        pick_ref[:, slab * rows : (slab + 1) * rows] = chosen.astype(jnp.float32).astype(jnp.bfloat16)
    for copy in copies:
        copy.wait()


def stage_kernel(blocks, normed_order, me_ref, parent_ref, parents_ref, states_ref, *refs):
    outs, (place_ref, pick_ref, hold_ref, in_sem, out_sem) = refs[:-5], refs[-5:]
    me, own_rows = me_ref[0], states_ref.shape[0]
    user, member = split(me, blocks)
    wanted = matching_children(parent_ref, user, member ^ 1, member, own_rows, 0)[1]
    wanted += matching_children(parent_ref, user, member ^ 2, member, own_rows, 0)[1][1:]
    loads, saves = [], []
    for place, (row, out) in enumerate(zip(wanted, outs)):
        loads.append(pltpu.make_async_copy(states_ref.at[row], hold_ref.at[place], in_sem.at[place]))
        saves.append(pltpu.make_async_copy(hold_ref.at[place], out.at[0], out_sem.at[place]))
        loads[-1].start()
    device, child, away, rank, parent_place = row_facts(parents_ref[...], blocks, own_rows)
    is_far, number = far_number(away, rank)
    line = lax.broadcasted_iota(jnp.int32, (place_ref.shape[0], parents_ref.shape[1]), 0)
    own = (line == jnp.where((device == me) & ~is_far, child, -1)[0:1]).astype(jnp.float32)
    far = (line == jnp.where((device ^ away == me) & is_far, own_rows + number, -1)[0:1]).astype(jnp.float32)
    came = own_rows + jnp.where(away == 1, rank, CAP + rank)
    own_place = jnp.where(away == 0, parent_place, came)
    place = own * (own_place[0:1] + 1).astype(jnp.float32) + far * (parent_place[0:1] + 1).astype(jnp.float32)
    place_ref[...] = jnp.broadcast_to(jnp.sum(place, axis=1, keepdims=True) - 1.0, place_ref.shape)
    for load, save in zip(loads, saves):
        load.wait()
        save.start()
    count = len(normed_order)
    holder = place_in(normed_order, jnp.where(is_far, device ^ away, device) ^ me)
    index = jnp.where(is_far, count * own_rows + number * count + holder, holder * own_rows + child)
    pick_ref[...] = chosen_rows(column_of(index), pick_ref.shape[1]).astype(jnp.bfloat16)
    for save in saves:
        save.wait()


def hold_kernel(states_ref, held_ref, sem):
    copies = [pltpu.make_async_copy(states_ref.at[row], held_ref.at[row], sem.at[row]) for row in range(states_ref.shape[0])]
    for copy in copies:
        copy.start()
    for copy in copies:
        copy.wait()


def project_kernel(order, me_ref, weight_ref, pick_ref, *refs):
    held, out_ref = refs[:-1], refs[-1]
    me, columns, parts = me_ref[0], held[0].shape[1], len(held)
    rows = pick_ref.shape[1] // 3
    total = [None] * 3
    for place, distance in enumerate(order):
        ref, within = held[place * parts // len(order)], place % (len(order) // parts)
        block = ref[within * rows : (within + 1) * rows, :]
        first = pl.multiple_of((me ^ distance) * columns, columns)
        for slab in range(3):
            term = jnp.dot(block, weight_ref[slab, pl.ds(first, columns), :], preferred_element_type=jnp.float32)
            total[slab] = term if total[slab] is None else total[slab] + term
    every = jnp.concatenate([part.astype(jnp.bfloat16) for part in total], 0)
    out_ref[...] = jnp.dot(pick_ref[...], every, preferred_element_type=jnp.float32).astype(jnp.bfloat16)


def head_rows(piece, own_rows):
    piece = piece.astype(jnp.float32)
    far = piece[3 * own_rows :]
    slabs = []
    for slab in range(3):
        shifted = far if slab == 0 else pltpu.roll(far, far.shape[0] - slab * FARS, 0)
        slabs.append(jnp.concatenate([piece[slab * own_rows : (slab + 1) * own_rows], shifted[:own_rows]], 0))
    return slabs


def head_factors(keys, gate_row, bias, size):
    logit = jnp.sum(keys * gate_row, axis=-1, keepdims=True) / math.sqrt(size) + bias
    decay = 1.0 / (1.0 + jnp.exp(-logit))
    return decay, lax.rsqrt(jnp.sum(keys * keys, axis=-1, keepdims=True) + 1e-06)


def lane_of(recv_order, me, head):
    return head if recv_order is None else place_in(recv_order, me ^ head)


def readout_kernel(recv_order, block, near_count, me_ref, bias_ref, place_ref, gate_ref, gain_ref, *refs):
    sources, parts, (out_ref, recv_ref, norm_ref) = refs[:near_count], refs[near_count:-3], refs[-3:]
    own_rows, heads, size = sources[0].shape[0], sources[0].shape[1], sources[0].shape[2]
    slots = place_ref.shape[0]
    for number, part in enumerate(parts):
        for within in range(part.shape[0]):
            recv_ref[within * len(parts) + number] = part[within]
    place = place_ref[:, 0:1]
    joint = math.gcd(block, 2)
    states = sum(ref.shape[0] for ref in sources)

    def work(step, carry):
        for group in range(0, block, joint):
            first_head = step * block + group
            rows = [
                head_rows(recv_ref[lane_of(recv_order, me_ref[0], first_head + n)], own_rows) for n in range(joint)
            ]
            spread = [
                jnp.concatenate([jnp.where(place == float(p), row[0], 0.0).astype(jnp.bfloat16) for p in range(states)], 1)
                for row in rows
            ]
            priors = []
            for n in range(joint):
                one = [ref[:, pl.ds(first_head + n, 1)].reshape(ref.shape[0] * size, size) for ref in sources]
                priors.append(jnp.concatenate(one, 0))
            product = jnp.dot(
                jnp.concatenate(spread, 0), jnp.concatenate(priors, 1), preferred_element_type=jnp.float32
            )
            for n in range(joint):
                head = first_head + n
                queries, keys, values = rows[n]
                decay, inverse = head_factors(keys, gate_ref[pl.ds(head, 1), :], bias_ref[head], size)
                overlap = jnp.sum(queries * keys, axis=-1, keepdims=True) * inverse
                readout = decay * product[n * slots : (n + 1) * slots, n * size : (n + 1) * size] + overlap * values
                scale = lax.rsqrt(jnp.mean(readout * readout, axis=-1, keepdims=True) + 1e-05)
                norm_ref[head] = readout * scale * gain_ref[pl.ds(head, 1), :]
        return carry

    lax.fori_loop(0, heads // block, work, 0)
    share = heads // own_rows
    columns = [norm_ref[h][:own_rows] for h in range(heads)]
    for number in range(own_rows, own_rows + FARS):
        lines = []
        for line in range(own_rows):
            span = range(line * share, (line + 1) * share)
            lines.append(jnp.concatenate([norm_ref[h][number : number + 1] for h in span], 1))
        columns.append(jnp.concatenate(lines, 0))
    out_ref[...] = jnp.concatenate(columns, 1).astype(jnp.bfloat16)


def output_kernel(own_rows, x_ref, weight_ref, pick_ref, *refs):
    parts, (out_ref, far_ref) = refs[:-2], refs[-2:]
    width = weight_ref.shape[0]
    share = width // own_rows
    gathered = jnp.concatenate([part[...] for part in parts], 0)
    count = gathered.shape[0] // own_rows
    lanes = far_ref.shape[2]
    for block in range(far_ref.shape[0]):
        far_ref[block] = gathered[:, width + block * lanes : width + (block + 1) * lanes].astype(jnp.float32)
    rows = [gathered[:, :width]]
    blocks = share // lanes
    for number in range(FARS):
        spans = range(number * blocks, (number + 1) * blocks)
        lines = [far_ref[block, pl.ds(line, count, stride=own_rows), :] for line in range(own_rows) for block in spans]
        rows.append(jnp.concatenate(lines, 1).astype(jnp.bfloat16))
    rest = jnp.dot(jnp.concatenate(rows, 0), weight_ref[...], preferred_element_type=jnp.float32)
    total = x_ref[...].astype(jnp.float32)
    for _ in range(3):
        term = rest.astype(jnp.bfloat16)
        rest = rest - term.astype(jnp.float32)
        total = total + jnp.dot(pick_ref[...], term, preferred_element_type=jnp.float32)
    out_ref[...] = total.astype(jnp.bfloat16)


def near_update_kernel(
    recv_order, block, blocks, me_ref, parent_ref, bias_ref, recv_ref, gate_ref, states_ref, *refs
):
    near_refs, (out_ref, turned_ref, values_ref, terms_ref, new_ref, out_sem) = refs[:CAP], refs[CAP:]
    own_rows, heads, size = states_ref.shape[0], states_ref.shape[1], states_ref.shape[2]
    slots = values_ref.shape[1]
    user, member = split(me_ref[0], blocks)

    def prepare(step, carry):
        for part in range(block):
            head = step * block + part
            _, keys, values = head_rows(recv_ref[lane_of(recv_order, me_ref[0], head)], own_rows)
            decay, inverse = head_factors(keys, gate_ref[pl.ds(head, 1), :], bias_ref[head], size)
            turned_ref[head] = jnp.transpose(keys).astype(jnp.bfloat16)
            values_ref[head] = values
            terms_ref[0, head] = jnp.broadcast_to(decay, (slots, size))
            terms_ref[1, head] = jnp.broadcast_to(inverse, (slots, size))
        return carry

    lax.fori_loop(0, heads // block, prepare, 0)
    line = lax.broadcasted_iota(jnp.int32, (slots, size), 0)

    def save(row):
        return pltpu.make_async_copy(new_ref.at[row], out_ref.at[row], out_sem.at[row])

    def facts(row):
        parent_block, place = split(parent_ref[0, user, member * own_rows + row], own_rows)
        return parent_block ^ member, place

    def update(row, prior_of):
        for head in range(heads):
            value = jnp.where(line == row, values_ref[head], 0.0).astype(jnp.bfloat16)
            outer = jnp.dot(turned_ref[head], value, preferred_element_type=jnp.float32)
            fresh = terms_ref[0, head, pl.ds(row, 1), :] * prior_of(head).astype(jnp.float32)
            fresh = fresh + terms_ref[1, head, pl.ds(row, 1), :] * outer
            new_ref[row, head] = fresh.astype(jnp.bfloat16)
        save(row).start()

    def work(row, found):
        away, place = facts(row)

        @pl.when(away == 0)
        def _():
            update(row, lambda head: states_ref[place, head])

        for rank, ref in enumerate(near_refs):

            @pl.when((away == 1) & (found == rank))
            def _():
                update(row, lambda head: ref[0, head])

        return found + (away == 1).astype(jnp.int32)

    lax.fori_loop(0, own_rows, work, jnp.int32(0))

    def finish(row, carry):
        @pl.when(facts(row)[0] < 2)
        def _():
            save(row).wait()

        return carry

    lax.fori_loop(0, own_rows, finish, 0)


def far_update_kernel(block, blocks, own_rows, entries, me_ref, parent_ref, turned_ref, values_ref, terms_ref, *refs):
    gots, (_, out_ref, new_ref, out_sem) = refs[:-4], refs[-4:]
    heads, size = gots[0].shape[1], gots[0].shape[2]
    user, member = split(me_ref[0], blocks)
    children = [
        matching_children(parent_ref, user, member, member ^ partner, own_rows, -1)[0][rank] for _, _, partner, rank in entries
    ]
    line = lax.broadcasted_iota(jnp.int32, (values_ref.shape[1], size), 0)

    def save(entry, step):
        span = pl.ds(step * block, block)
        target = out_ref.at[jnp.maximum(children[entry], 0), span]
        return pltpu.make_async_copy(new_ref.at[entry, span], target, out_sem.at[entry, step])

    for entry, (array, within, _, _) in enumerate(entries):
        got_ref, child = gots[array], children[entry]

        @pl.when(child >= 0)
        def _():
            for step in range(heads // block):
                for head in range(step * block, (step + 1) * block):
                    value = jnp.where(line == child, values_ref[head], 0.0).astype(jnp.bfloat16)
                    outer = jnp.dot(turned_ref[head], value, preferred_element_type=jnp.float32)
                    fresh = terms_ref[0, head, pl.ds(child, 1), :] * got_ref[within, head].astype(jnp.float32)
                    fresh = fresh + terms_ref[1, head, pl.ds(child, 1), :] * outer
                    new_ref[entry, head] = fresh.astype(jnp.bfloat16)
                save(entry, step).start()

    for entry in range(len(entries)):

        @pl.when(children[entry] >= 0)
        def _():
            for step in range(heads // block):
                save(entry, step).wait()


def per_device(
    token_ids,
    parents,
    states,
    embed_table,
    qkv_weight,
    gate_weight,
    gate_bias,
    norm_gain,
    out_weight,
):
    own_rows, heads, size = states.shape[0], states.shape[1], states.shape[2]
    width = heads * size
    columns = embed_table.shape[1]
    row_total = token_ids.shape[1]
    users, beam = parents.shape[1], parents.shape[2]
    blocks = beam // own_rows
    count = lax.axis_size("rows")
    me = lax.axis_index("rows").astype(jnp.int32)
    user, member = me // blocks, me % blocks
    plan = stage_plan(count)
    steps = exchange_plan(plan)
    recv_order, normed_order = plan_order(steps), gather_order(plan)
    slots, piece = 2 * own_rows, 5 * own_rows
    one_state, two_states = (1, heads, size, size), (CAP, heads, size, size)
    normed_columns = width + FARS * width // own_rows
    bf16, int32 = jnp.bfloat16, jnp.int32
    mine = me[None]
    parent_row = jnp.broadcast_to(parents.reshape(1, row_total), (8, row_total))
    head_block = math.gcd(heads, 4)

    local_columns, first_out = pl.pallas_call(
        functools.partial(fetch_kernel, blocks),
        in_specs=[SCALARS, SCALARS, SCALARS, WHOLE, PLACED, PLACED],
        out_specs=[WHOLE] * 2,
        out_shape=[pltpu.VMEM((row_total, columns), bf16), pltpu.VMEM(one_state, bf16)],
        scratch_shapes=[
            pltpu.VMEM((row_total * TILE, columns), bf16),
            pltpu.SemaphoreType.DMA,
            pltpu.SemaphoreType.DMA,
        ],
        compiler_params=params(),
        name="fetch",
    )(mine, in_hbm(parents), in_hbm(token_ids), in_hbm(token_ids), in_hbm(embed_table), in_hbm(states))
    first_got = xor_permute(first_out, 2)

    send_pick, corner_out = pl.pallas_call(
        functools.partial(pick_kernel, blocks, piece, recv_order),
        in_specs=[SCALARS, SCALARS, WHOLE, PLACED],
        out_specs=[WHOLE] * 2,
        out_shape=[jax.ShapeDtypeStruct((count * piece, 3 * row_total), bf16), pltpu.VMEM(two_states, bf16)],
        scratch_shapes=[pltpu.SemaphoreType.DMA((CAP,))],
        compiler_params=params(),
        name="pick",
    )(mine, in_hbm(parents), parent_row, in_hbm(states))
    corner_got = xor_permute(corner_out, 3)

    *near_outs, last_out, place, out_pick = pl.pallas_call(
        functools.partial(stage_kernel, blocks, normed_order),
        in_specs=[SCALARS, SCALARS, WHOLE, PLACED],
        out_specs=[PLACED] * (CAP + 1) + [WHOLE] * 2,
        out_shape=[pltpu.HBM(one_state, bf16)] * (CAP + 1)
        + [
            jax.ShapeDtypeStruct((slots, 128), jnp.float32),
            jax.ShapeDtypeStruct((row_total, row_total + FARS * count), bf16),
        ],
        scratch_shapes=[
            pltpu.VMEM((CAP + 1, heads, size, size), bf16),
            pltpu.SemaphoreType.DMA((CAP + 1,)),
            pltpu.SemaphoreType.DMA((CAP + 1,)),
        ],
        compiler_params=params(),
        name="stage",
    )(mine, in_hbm(parents), parent_row, in_hbm(states))
    near_gots = [xor_permute(block, 1) for block in near_outs]
    last_got = xor_permute(last_out, 2)

    held = pl.pallas_call(
        hold_kernel,
        in_specs=[PLACED],
        out_specs=WHOLE,
        out_shape=pltpu.VMEM(states.shape, bf16),
        scratch_shapes=[pltpu.SemaphoreType.DMA((own_rows,))],
        compiler_params=params(),
        name="hold",
    )(in_hbm(states))

    weight = jnp.transpose(qkv_weight, (1, 0, 2))
    tied = {}

    def in_inputs(stage, parts):
        if stage == 0:
            *parts, tied["weight"], tied["pick"] = lax.optimization_barrier((*parts, weight, send_pick))
        if stage == 1:
            *parts, tied["first"], tied["place"] = lax.optimization_barrier((*parts, first_got, place))
        return parts

    every_input = gather_all(local_columns, plan, in_inputs)
    pieces = pl.pallas_call(
        functools.partial(project_kernel, normed_order),
        in_specs=[SCALARS] + [WHOLE] * (2 + len(every_input)),
        out_specs=WHOLE,
        out_shape=jax.ShapeDtypeStruct((count * piece, columns), bf16),
        compiler_params=params(),
        name="project",
    )(mine, tied["weight"], tied["pick"], *every_input)

    def in_exchange(stage, parts):
        if stage == 1:
            *parts, tied["near"], tied["nearer"] = lax.optimization_barrier((*parts, *near_gots))
        return parts

    received = exchange_all(pieces.reshape(count, piece, columns), steps, in_exchange)
    if columns != size:
        every_piece = jnp.stack(received, 1).reshape(count, piece, columns)
        places = jnp.array([recv_order.index(d) for d in range(count)], int32)[jnp.arange(count, dtype=int32) ^ me]
        every_piece = jnp.take(every_piece, places, axis=0).transpose(1, 0, 2).reshape(piece, heads, size)
        received = [every_piece.transpose(1, 0, 2)]
        recv_order = None

    held, near_gots = in_vmem(held), [tied["near"], tied["nearer"]]
    sources = [held, *near_gots, tied["first"]]
    normed, by_head = pl.pallas_call(
        functools.partial(readout_kernel, recv_order, head_block, len(sources)),
        in_specs=[SCALARS] * 2 + [WHOLE] * (3 + len(sources) + len(received)),
        out_specs=[WHOLE] * 2,
        out_shape=[
            jax.ShapeDtypeStruct((own_rows, normed_columns), bf16),
            jax.ShapeDtypeStruct((heads, piece, size), bf16),
        ],
        scratch_shapes=[pltpu.VMEM((heads, slots, size), jnp.float32)],
        compiler_params=params(),
        name="readout",
    )(mine, gate_bias, tied["place"], gate_weight, norm_gain.reshape(heads, size), *sources, *received)

    near_done, turned, values, terms = pl.pallas_call(
        functools.partial(near_update_kernel, recv_order, head_block, blocks),
        in_specs=[SCALARS] * 3 + [WHOLE] * (3 + CAP),
        out_specs=[PLACED] + [WHOLE] * 3,
        out_shape=[
            pltpu.HBM(states.shape, bf16),
            jax.ShapeDtypeStruct((heads, size, slots), bf16),
            jax.ShapeDtypeStruct((heads, slots, size), jnp.float32),
            jax.ShapeDtypeStruct((2, heads, slots, size), jnp.float32),
        ],
        scratch_shapes=[pltpu.VMEM(states.shape, bf16), pltpu.SemaphoreType.DMA((own_rows,))],
        compiler_params=params(),
        name="near_update",
    )(mine, parents, gate_bias, by_head, gate_weight, held, *near_gots)

    def far_update(before, gots, entries, name):
        return pl.pallas_call(
            functools.partial(far_update_kernel, head_block, blocks, own_rows, entries),
            in_specs=[SCALARS] * 2 + [WHOLE] * (3 + len(gots)) + [PLACED],
            out_specs=PLACED,
            out_shape=jax.ShapeDtypeStruct(states.shape, bf16),
            scratch_shapes=[
                pltpu.VMEM((len(entries),) + one_state[1:], bf16),
                pltpu.SemaphoreType.DMA((len(entries), heads // head_block)),
            ],
            input_output_aliases={5 + len(gots): 0},
            compiler_params=params(),
            name=name,
        )(mine, parents, tied["turned"], values, terms, *gots, before)

    def in_normed(stage, parts):
        if stage == 0:
            *parts, tied["rows"], tied["turned"] = lax.optimization_barrier((*parts, near_done, turned))
        if stage == 1:
            entries = [(0, 0, 2, 0)] + [(1, rank, 3, rank) for rank in range(CAP)]
            far_done = far_update(tied["rows"], [tied["first"], corner_got], entries, "far_update")
            parts[-1], tied["done"] = lax.optimization_barrier((parts[-1], far_done))
        return parts

    every_normed = gather_all(normed, plan, in_normed)
    layer_out = pl.pallas_call(
        functools.partial(output_kernel, own_rows),
        in_specs=[WHOLE] * (3 + len(every_normed)),
        out_specs=WHOLE,
        out_shape=jax.ShapeDtypeStruct((row_total, columns), bf16),
        scratch_shapes=[pltpu.VMEM(((normed_columns - width) // size, row_total, size), jnp.float32)],
        compiler_params=params(),
        name="output",
    )(local_columns, out_weight, out_pick, *every_normed)
    layer_out, last_got = lax.optimization_barrier((layer_out, last_got))
    final = far_update(tied["done"], [last_got], [(0, 0, 2, 1)], "last_update")
    return (layer_out[None], final)


def solution(mesh):
    placed = (
        P(None, "groups"),
        P(None, "groups", None),
        P(("groups", "rows"), None, None, None),
        P(None, "rows"),
        P(None, None, "rows"),
        P(),
        P(),
        P(),
        P(None, "rows"),
    )
    return jax.shard_map(
        per_device,
        mesh=mesh,
        in_specs=placed,
        out_specs=(P(None, "groups", "rows"), P(("groups", "rows"), None, None, None)),
        check_vma=False,
    )
```

```python
import functools
import math

import jax
import jax.numpy as jnp
from jax import lax
from jax.experimental import pallas as pl
from jax.experimental.pallas import tpu as pltpu
from jax.sharding import PartitionSpec as P

CAP = 2
FARS = 2 * CAP - 1
TILE = 16
VMEM_BYTES = 24 * 1024 * 1024
WHOLE = pl.BlockSpec(memory_space=pltpu.VMEM)
SCALARS = pl.BlockSpec(memory_space=pltpu.SMEM)
PLACED = pl.BlockSpec(memory_space=pl.ANY)


def params():
    return pltpu.CompilerParams(vmem_limit_bytes=VMEM_BYTES)


def in_hbm(array):
    return pltpu.with_memory_space_constraint(array, pltpu.HBM)


def in_vmem(array):
    return pltpu.with_memory_space_constraint(array, pltpu.VMEM)


def xor_permute(block, distance):
    count = lax.axis_size("rows")
    return lax.ppermute(block, "rows", [(i, i ^ distance) for i in range(count)])


def stage_plan(count):
    if count == 1:
        return []
    if count == 2:
        return [[1]]
    if count == 4:
        return [[2], [1]]
    plan = [[6], [4, 8, 12] if count >= 16 else [4]]
    bit = 16
    while bit < count:
        plan.append([bit])
        bit *= 2
    return plan + [[1]]


def plan_order(plan):
    order = [0]
    for stage in plan:
        order = [near ^ far for near in order for far in [0] + stage]
    return order


def gather_order(plan):
    order = [0]
    for stage in plan:
        order = [near ^ far for far in [0] + stage for near in order]
    return order


def gather_all(block, plan, after=lambda stage, held: held):
    held = [block]
    for number, stage in enumerate(plan):
        held = held + [xor_permute(part, distance) for distance in stage for part in held]
        if len(held) == 2:
            held = [jnp.concatenate(held, 0)]
        held = after(number, held)
    return held


def exchange_plan(plan):
    return plan[-1:] + plan[:-1]


def exchange_all(pieces, plan, after=lambda stage, held: held):
    tail = pieces.shape[1:]
    held = [pieces.reshape(tuple(len(stage) + 1 for stage in plan) + tail)]
    for axis, stage in enumerate(plan):
        fresh = []
        for part in held:
            slabs = [lax.index_in_dim(part, place, axis, keepdims=True) for place in range(len(stage) + 1)]
            fresh.append(slabs[0])
            fresh += [xor_permute(slab, distance) for slab, distance in zip(slabs[1:], stage)]
        held = after(axis, fresh if axis == len(plan) - 1 else [jnp.concatenate(fresh, axis)])
    return [part.reshape((-1,) + tail) for part in held]


def split(number, size):
    if size & (size - 1) == 0:
        return lax.shift_right_logical(number, size.bit_length() - 1), number & (size - 1)
    return lax.div(number, size), lax.rem(number, size)


def place_in(order, distance):
    place, bit = distance & 0, 0
    while 1 << bit < len(order):
        place = place ^ ((lax.shift_right_logical(distance, bit) & 1) * order.index(1 << bit))
        bit += 1
    return place


def row_facts(parent_row, blocks, own_rows):
    lane = lax.broadcasted_iota(jnp.int32, parent_row.shape, 1)
    device, child = split(lane, own_rows)
    parent_block, parent_place = split(parent_row, own_rows)
    rank = jnp.zeros_like(lane)
    for earlier in range(1, own_rows):
        same = (pltpu.roll(parent_block, earlier, 1) == parent_block) & (child >= earlier)
        rank = rank + same.astype(jnp.int32)
    return device, child, parent_block ^ (device & (blocks - 1)), rank, parent_place


def far_number(away, rank):
    return (away == 3) | ((away == 2) & (rank > 0)), jnp.where(away == 3, rank, CAP + rank - 1)


def column_of(row):
    spread = jnp.broadcast_to(row[0:1].astype(jnp.float32), (8, row.shape[1]))
    return jnp.transpose(spread)[:, 0:1]


def chosen_rows(column, width):
    shape = (column.shape[0], width)
    return (lax.broadcasted_iota(jnp.int32, shape, 1).astype(jnp.float32) == column).astype(jnp.float32)


def matching_children(parent_ref, user, child_block, parent_block, own_rows, none):
    children, parents, found = [jnp.int32(none)] * CAP, [jnp.int32(0)] * CAP, jnp.int32(0)
    for child in range(own_rows):
        block, place = split(parent_ref[0, user, child_block * own_rows + child], own_rows)
        hit = block == parent_block
        for j in range(CAP):
            children[j] = jnp.where(hit & (found == j), child, children[j])
            parents[j] = jnp.where(hit & (found == j), place, parents[j])
        found = found + hit.astype(jnp.int32)
    return children, parents


def fetch_kernel(
    blocks, me_ref, parent_ref, token_ref, tokens_ref, table_ref, states_ref, x_ref, y_ref, rows_ref, row_sem, state_sem
):
    count, own_rows, heads = token_ref.shape[1], states_ref.shape[0], states_ref.shape[1]
    user, member = split(me_ref[0], blocks)

    def start_row(r, carry):
        first = pl.multiple_of(split(token_ref[0, r], TILE)[0] * TILE, TILE)
        pltpu.make_async_copy(
            table_ref.at[pl.ds(first, TILE)],
            rows_ref.at[pl.ds(pl.multiple_of(r * TILE, TILE), TILE)],
            row_sem,
        ).start()
        return carry

    lax.fori_loop(0, count, start_row, 0, unroll=8)
    copies = []
    wanted = matching_children(parent_ref, user, member ^ 2, member, own_rows, 0)[1]
    extra = y_ref.shape[0] - heads
    for part, (row, first, size) in enumerate(((wanted[0], 0, heads // 2), (wanted[0], heads // 2, heads // 2), (wanted[1], 0, extra))):
        span, target = pl.ds(first, size), y_ref.at[pl.ds(part * (heads // 2), size)]
        copies.append(pltpu.make_async_copy(states_ref.at[row, span], target, state_sem.at[part]))
        copies[-1].start()
    step = math.gcd(count, 128)
    picks = []
    for first in range(0, count, step):
        low = column_of(split(tokens_ref[:, first : first + step], TILE)[1])
        wanted = low + lax.broadcasted_iota(jnp.int32, (step, 1), 0).astype(jnp.float32) * TILE
        picks.append(chosen_rows(wanted, step * TILE).astype(jnp.bfloat16))
    pltpu.make_async_copy(table_ref.at[pl.ds(0, count * TILE)], rows_ref, row_sem).wait()
    for first, pick in zip(range(0, count, step), picks):
        x_ref[first : first + step, :] = jnp.dot(
            pick, rows_ref[first * TILE : (first + step) * TILE, :], preferred_element_type=jnp.float32
        ).astype(jnp.bfloat16)
    for copy in copies:
        copy.wait()


def pick_kernel(blocks, piece, send_order, me_ref, parent_ref, parents_ref, states_ref, pick_ref, corner_ref, sem):
    me, rows, own_rows = me_ref[0], parents_ref.shape[1], states_ref.shape[0]
    user, member = split(me, blocks)
    copies = []
    for slot, row in enumerate(matching_children(parent_ref, user, member ^ 3, member, own_rows, 0)[1]):
        copies.append(pltpu.make_async_copy(states_ref.at[row], corner_ref.at[slot], sem.at[slot]))
        copies[-1].start()
    device, child, away, rank, _ = row_facts(parents_ref[...], blocks, own_rows)
    is_far, number = far_number(away, rank)
    own = place_in(send_order, device ^ me) * piece + child
    far = place_in(send_order, device ^ away ^ me) * piece + 3 * own_rows + number
    line = lax.broadcasted_iota(jnp.int32, (len(send_order) * piece, rows), 0)
    for slab in range(3):
        far_line = jnp.where(is_far, far + slab * FARS, -1)
        chosen = (line == own[0:1] + slab * own_rows) | (line == far_line[0:1])
        pick_ref[:, slab * rows : (slab + 1) * rows] = chosen.astype(jnp.float32).astype(jnp.bfloat16)
    for copy in copies:
        copy.wait()


def stage_kernel(blocks, normed_order, me_ref, parent_ref, parents_ref, states_ref, *refs):
    outs, (place_ref, pick_ref, hold_ref, in_sem, out_sem) = refs[:-5], refs[-5:]
    me, own_rows = me_ref[0], states_ref.shape[0]
    user, member = split(me, blocks)
    wanted = matching_children(parent_ref, user, member ^ 1, member, own_rows, 0)[1]
    wanted += matching_children(parent_ref, user, member ^ 2, member, own_rows, 0)[1][1:]
    heads = states_ref.shape[1]
    loads, saves = [], []
    for place, (row, out) in enumerate(zip(wanted, outs)):
        span, kept = pl.ds(heads - out.shape[0], out.shape[0]), pl.ds(0, out.shape[0])
        loads.append(pltpu.make_async_copy(states_ref.at[row, span], hold_ref.at[place, kept], in_sem.at[place]))
        saves.append(pltpu.make_async_copy(hold_ref.at[place, kept], out, out_sem.at[place]))
        loads[-1].start()
    device, child, away, rank, parent_place = row_facts(parents_ref[...], blocks, own_rows)
    is_far, number = far_number(away, rank)
    line = lax.broadcasted_iota(jnp.int32, (place_ref.shape[0], parents_ref.shape[1]), 0)
    own = (line == jnp.where((device == me) & ~is_far, child, -1)[0:1]).astype(jnp.float32)
    far = (line == jnp.where((device ^ away == me) & is_far, own_rows + number, -1)[0:1]).astype(jnp.float32)
    came = own_rows + jnp.where(away == 1, rank, CAP + rank)
    own_place = jnp.where(away == 0, parent_place, came)
    place = own * (own_place[0:1] + 1).astype(jnp.float32) + far * (parent_place[0:1] + 1).astype(jnp.float32)
    place_ref[...] = jnp.broadcast_to(jnp.sum(place, axis=1, keepdims=True) - 1.0, place_ref.shape)
    for load, save in zip(loads, saves):
        load.wait()
        save.start()
    count = len(normed_order)
    holder = place_in(normed_order, jnp.where(is_far, device ^ away, device) ^ me)
    index = jnp.where(is_far, count * own_rows + number * count + holder, holder * own_rows + child)
    pick_ref[...] = chosen_rows(column_of(index), pick_ref.shape[1]).astype(jnp.bfloat16)
    for save in saves:
        save.wait()


def hold_kernel(states_ref, held_ref, sem):
    copies = [pltpu.make_async_copy(states_ref.at[row], held_ref.at[row], sem.at[row]) for row in range(states_ref.shape[0])]
    for copy in copies:
        copy.start()
    for copy in copies:
        copy.wait()


def project_kernel(order, me_ref, weight_ref, pick_ref, *refs):
    held, out_ref = refs[:-1], refs[-1]
    me, columns, parts = me_ref[0], held[0].shape[1], len(held)
    rows = pick_ref.shape[1] // 3
    total = [None] * 3
    for place, distance in enumerate(order):
        ref, within = held[place * parts // len(order)], place % (len(order) // parts)
        block = ref[within * rows : (within + 1) * rows, :]
        first = pl.multiple_of((me ^ distance) * columns, columns)
        for slab in range(3):
            term = jnp.dot(block, weight_ref[slab, pl.ds(first, columns), :], preferred_element_type=jnp.float32)
            total[slab] = term if total[slab] is None else total[slab] + term
    every = jnp.concatenate([part.astype(jnp.bfloat16) for part in total], 0)
    out_ref[...] = jnp.dot(pick_ref[...], every, preferred_element_type=jnp.float32).astype(jnp.bfloat16)


def head_rows(piece, own_rows):
    piece = piece.astype(jnp.float32)
    far = piece[3 * own_rows :]
    slabs = []
    for slab in range(3):
        shifted = far if slab == 0 else pltpu.roll(far, far.shape[0] - slab * FARS, 0)
        slabs.append(jnp.concatenate([piece[slab * own_rows : (slab + 1) * own_rows], shifted[:own_rows]], 0))
    return slabs


def head_factors(keys, gate_row, bias, size):
    logit = jnp.sum(keys * gate_row, axis=-1, keepdims=True) / math.sqrt(size) + bias
    decay = 1.0 / (1.0 + jnp.exp(-logit))
    return decay, lax.rsqrt(jnp.sum(keys * keys, axis=-1, keepdims=True) + 1e-06)


def lane_of(recv_order, me, head):
    return head if recv_order is None else place_in(recv_order, me ^ head)


def readout_kernel(recv_order, block, near_count, me_ref, bias_ref, place_ref, gate_ref, gain_ref, *refs):
    sources, parts, (out_ref, recv_ref, norm_ref) = refs[:near_count], refs[near_count:-3], refs[-3:]
    own_rows, heads, size = sources[0].shape[0], sources[0].shape[1], sources[0].shape[2]
    slots = place_ref.shape[0]
    for number, part in enumerate(parts):
        for within in range(part.shape[0]):
            recv_ref[within * len(parts) + number] = part[within]
    place = place_ref[:, 0:1]
    joint = math.gcd(block, 2)
    states = sum(ref.shape[0] if len(ref.shape) == 4 else 1 for ref in sources)

    def work(step, carry):
        for group in range(0, block, joint):
            first_head = step * block + group
            rows = [
                head_rows(recv_ref[lane_of(recv_order, me_ref[0], first_head + n)], own_rows) for n in range(joint)
            ]
            spread = [
                jnp.concatenate([jnp.where(place == float(p), row[0], 0.0).astype(jnp.bfloat16) for p in range(states)], 1)
                for row in rows
            ]
            priors = []
            for n in range(joint):
                head = first_head + n
                one = [
                    ref[:, pl.ds(head, 1)].reshape(ref.shape[0] * size, size) if len(ref.shape) == 4 else ref[head]
                    for ref in sources
                ]
                priors.append(jnp.concatenate(one, 0))
            product = jnp.dot(
                jnp.concatenate(spread, 0), jnp.concatenate(priors, 1), preferred_element_type=jnp.float32
            )
            for n in range(joint):
                head = first_head + n
                queries, keys, values = rows[n]
                decay, inverse = head_factors(keys, gate_ref[pl.ds(head, 1), :], bias_ref[head], size)
                overlap = jnp.sum(queries * keys, axis=-1, keepdims=True) * inverse
                readout = decay * product[n * slots : (n + 1) * slots, n * size : (n + 1) * size] + overlap * values
                scale = lax.rsqrt(jnp.mean(readout * readout, axis=-1, keepdims=True) + 1e-05)
                norm_ref[head] = readout * scale * gain_ref[pl.ds(head, 1), :]
        return carry

    lax.fori_loop(0, heads // block, work, 0)
    share = heads // own_rows
    columns = [norm_ref[h][:own_rows] for h in range(heads)]
    for number in range(own_rows, own_rows + FARS):
        lines = []
        for line in range(own_rows):
            span = range(line * share, (line + 1) * share)
            lines.append(jnp.concatenate([norm_ref[h][number : number + 1] for h in span], 1))
        columns.append(jnp.concatenate(lines, 0))
    out_ref[...] = jnp.concatenate(columns, 1).astype(jnp.bfloat16)


def output_kernel(own_rows, x_ref, weight_ref, pick_ref, *refs):
    parts, (out_ref, far_ref) = refs[:-2], refs[-2:]
    width = weight_ref.shape[0]
    share = width // own_rows
    gathered = jnp.concatenate([part[...] for part in parts], 0)
    count = gathered.shape[0] // own_rows
    lanes = far_ref.shape[2]
    for block in range(far_ref.shape[0]):
        far_ref[block] = gathered[:, width + block * lanes : width + (block + 1) * lanes].astype(jnp.float32)
    rows = [gathered[:, :width]]
    blocks = share // lanes
    for number in range(FARS):
        spans = range(number * blocks, (number + 1) * blocks)
        lines = [far_ref[block, pl.ds(line, count, stride=own_rows), :] for line in range(own_rows) for block in spans]
        rows.append(jnp.concatenate(lines, 1).astype(jnp.bfloat16))
    rest = jnp.dot(jnp.concatenate(rows, 0), weight_ref[...], preferred_element_type=jnp.float32)
    total = x_ref[...].astype(jnp.float32)
    for _ in range(3):
        term = rest.astype(jnp.bfloat16)
        rest = rest - term.astype(jnp.float32)
        total = total + jnp.dot(pick_ref[...], term, preferred_element_type=jnp.float32)
    out_ref[...] = total.astype(jnp.bfloat16)


def near_update_kernel(
    recv_order, block, blocks, me_ref, parent_ref, bias_ref, recv_ref, gate_ref, states_ref, *refs
):
    near_refs, (out_ref, turned_ref, values_ref, terms_ref, new_ref, out_sem) = refs[:CAP], refs[CAP:]
    own_rows, heads, size = states_ref.shape[0], states_ref.shape[1], states_ref.shape[2]
    slots = values_ref.shape[1]
    user, member = split(me_ref[0], blocks)

    def prepare(step, carry):
        for part in range(block):
            head = step * block + part
            _, keys, values = head_rows(recv_ref[lane_of(recv_order, me_ref[0], head)], own_rows)
            decay, inverse = head_factors(keys, gate_ref[pl.ds(head, 1), :], bias_ref[head], size)
            turned_ref[head] = jnp.transpose(keys).astype(jnp.bfloat16)
            values_ref[head] = values
            terms_ref[0, head] = jnp.broadcast_to(decay, (slots, size))
            terms_ref[1, head] = jnp.broadcast_to(inverse, (slots, size))
        return carry

    lax.fori_loop(0, heads // block, prepare, 0)
    line = lax.broadcasted_iota(jnp.int32, (slots, size), 0)

    def save(row):
        return pltpu.make_async_copy(new_ref.at[row], out_ref.at[row], out_sem.at[row])

    def facts(row):
        parent_block, place = split(parent_ref[0, user, member * own_rows + row], own_rows)
        return parent_block ^ member, place

    def update(row, prior_of):
        for head in range(heads):
            value = jnp.where(line == row, values_ref[head], 0.0).astype(jnp.bfloat16)
            outer = jnp.dot(turned_ref[head], value, preferred_element_type=jnp.float32)
            fresh = terms_ref[0, head, pl.ds(row, 1), :] * prior_of(head).astype(jnp.float32)
            fresh = fresh + terms_ref[1, head, pl.ds(row, 1), :] * outer
            new_ref[row, head] = fresh.astype(jnp.bfloat16)
        save(row).start()

    def work(row, found):
        away, place = facts(row)

        @pl.when(away == 0)
        def _():
            update(row, lambda head: states_ref[place, head])

        for rank, ref in enumerate(near_refs):

            @pl.when((away == 1) & (found == rank))
            def _():
                update(row, lambda head: ref[head])

        return found + (away == 1).astype(jnp.int32)

    lax.fori_loop(0, own_rows, work, jnp.int32(0))

    def finish(row, carry):
        @pl.when(facts(row)[0] < 2)
        def _():
            save(row).wait()

        return carry

    lax.fori_loop(0, own_rows, finish, 0)


def far_update_kernel(block, blocks, own_rows, entries, me_ref, parent_ref, turned_ref, values_ref, terms_ref, *refs):
    gots, (_, out_ref, new_ref, out_sem) = refs[:-4], refs[-4:]
    user, member = split(me_ref[0], blocks)
    children = [
        matching_children(parent_ref, user, member, member ^ partner, own_rows, -1)[0][rank] for partner, rank, *_ in entries
    ]
    line = lax.broadcasted_iota(jnp.int32, values_ref.shape[1:], 0)

    def save(entry, head):
        target = out_ref.at[jnp.maximum(children[entry], 0), pl.ds(head, block)]
        return pltpu.make_async_copy(new_ref.at[entry, pl.ds(head, block)], target, out_sem.at[entry, head // block])

    for entry, (_, _, array, start, heads) in enumerate(entries):
        got_ref, child = gots[array], children[entry]

        @pl.when(child >= 0)
        def _():
            for head in heads:
                value = jnp.where(line == child, values_ref[head], 0.0).astype(jnp.bfloat16)
                outer = jnp.dot(turned_ref[head], value, preferred_element_type=jnp.float32)
                prior = got_ref[start + head - heads[0]].astype(jnp.float32)
                fresh = terms_ref[0, head, pl.ds(child, 1), :] * prior
                fresh = fresh + terms_ref[1, head, pl.ds(child, 1), :] * outer
                new_ref[entry, head] = fresh.astype(jnp.bfloat16)
                if (head + 1) % block == 0:
                    save(entry, head + 1 - block).start()

    for entry, (_, _, _, _, heads) in enumerate(entries):

        @pl.when(children[entry] >= 0)
        def _():
            for head in heads[::block]:
                save(entry, head).wait()


def per_device(
    token_ids,
    parents,
    states,
    embed_table,
    qkv_weight,
    gate_weight,
    gate_bias,
    norm_gain,
    out_weight,
):
    own_rows, heads, size = states.shape[0], states.shape[1], states.shape[2]
    width = heads * size
    columns = embed_table.shape[1]
    row_total = token_ids.shape[1]
    users, beam = parents.shape[1], parents.shape[2]
    blocks = beam // own_rows
    count = lax.axis_size("rows")
    me = lax.axis_index("rows").astype(jnp.int32)
    user, member = me // blocks, me % blocks
    plan = stage_plan(count)
    steps = exchange_plan(plan)
    recv_order, normed_order = plan_order(steps), gather_order(plan)
    slots, piece = 2 * own_rows, 5 * own_rows
    one_state, two_states = (heads, size, size), (CAP, heads, size, size)
    normed_columns = width + FARS * width // own_rows
    bf16, int32 = jnp.bfloat16, jnp.int32
    mine = me[None]
    parent_row = jnp.broadcast_to(parents.reshape(1, row_total), (8, row_total))
    head_block = math.gcd(heads, 4)
    extra = heads // 4

    local_columns, first_out = pl.pallas_call(
        functools.partial(fetch_kernel, blocks),
        in_specs=[SCALARS, SCALARS, SCALARS, WHOLE, PLACED, PLACED],
        out_specs=[WHOLE] * 2,
        out_shape=[pltpu.VMEM((row_total, columns), bf16), pltpu.VMEM((heads + extra, size, size), bf16)],
        scratch_shapes=[
            pltpu.VMEM((row_total * TILE, columns), bf16),
            pltpu.SemaphoreType.DMA,
            pltpu.SemaphoreType.DMA((3,)),
        ],
        compiler_params=params(),
        name="fetch",
    )(mine, in_hbm(parents), in_hbm(token_ids), in_hbm(token_ids), in_hbm(embed_table), in_hbm(states))
    first_got = xor_permute(first_out, 2)

    send_pick, corner_out = pl.pallas_call(
        functools.partial(pick_kernel, blocks, piece, recv_order),
        in_specs=[SCALARS, SCALARS, WHOLE, PLACED],
        out_specs=[WHOLE] * 2,
        out_shape=[jax.ShapeDtypeStruct((count * piece, 3 * row_total), bf16), pltpu.VMEM(two_states, bf16)],
        scratch_shapes=[pltpu.SemaphoreType.DMA((CAP,))],
        compiler_params=params(),
        name="pick",
    )(mine, in_hbm(parents), parent_row, in_hbm(states))
    corner_got = xor_permute(corner_out, 3)

    *near_outs, last_out, place, out_pick = pl.pallas_call(
        functools.partial(stage_kernel, blocks, normed_order),
        in_specs=[SCALARS, SCALARS, WHOLE, PLACED],
        out_specs=[PLACED] * (CAP + 1) + [WHOLE] * 2,
        out_shape=[pltpu.HBM(one_state, bf16)] * CAP
        + [pltpu.HBM((heads - extra, size, size), bf16)]
        + [
            jax.ShapeDtypeStruct((slots, 128), jnp.float32),
            jax.ShapeDtypeStruct((row_total, row_total + FARS * count), bf16),
        ],
        scratch_shapes=[
            pltpu.VMEM((CAP + 1, heads, size, size), bf16),
            pltpu.SemaphoreType.DMA((CAP + 1,)),
            pltpu.SemaphoreType.DMA((CAP + 1,)),
        ],
        compiler_params=params(),
        name="stage",
    )(mine, in_hbm(parents), parent_row, in_hbm(states))
    near_gots = [xor_permute(block, 1) for block in near_outs]
    last_got = xor_permute(last_out, 2)

    held = pl.pallas_call(
        hold_kernel,
        in_specs=[PLACED],
        out_specs=WHOLE,
        out_shape=pltpu.VMEM(states.shape, bf16),
        scratch_shapes=[pltpu.SemaphoreType.DMA((own_rows,))],
        compiler_params=params(),
        name="hold",
    )(in_hbm(states))

    weight = jnp.transpose(qkv_weight, (1, 0, 2))
    tied = {}

    def in_inputs(stage, parts):
        if stage == 0:
            *parts, tied["weight"], tied["pick"] = lax.optimization_barrier((*parts, weight, send_pick))
        if stage == 1:
            *parts, tied["place"] = lax.optimization_barrier((*parts, place))
        if stage == len(plan) - 1:
            *parts, tied["first"] = lax.optimization_barrier((*parts, first_got))
        return parts

    every_input = gather_all(local_columns, plan, in_inputs)
    pieces = pl.pallas_call(
        functools.partial(project_kernel, normed_order),
        in_specs=[SCALARS] + [WHOLE] * (2 + len(every_input)),
        out_specs=WHOLE,
        out_shape=jax.ShapeDtypeStruct((count * piece, columns), bf16),
        compiler_params=params(),
        name="project",
    )(mine, tied["weight"], tied["pick"], *every_input)

    def in_exchange(stage, parts):
        if stage == 1:
            *parts, tied["near"], tied["nearer"] = lax.optimization_barrier((*parts, *near_gots))
        return parts

    received = exchange_all(pieces.reshape(count, piece, columns), steps, in_exchange)
    if columns != size:
        every_piece = jnp.stack(received, 1).reshape(count, piece, columns)
        places = jnp.array([recv_order.index(d) for d in range(count)], int32)[jnp.arange(count, dtype=int32) ^ me]
        every_piece = jnp.take(every_piece, places, axis=0).transpose(1, 0, 2).reshape(piece, heads, size)
        received = [every_piece.transpose(1, 0, 2)]
        recv_order = None

    held, near_gots = in_vmem(held), [tied["near"], tied["nearer"]]
    sources = [held, *near_gots, tied["first"]]
    normed, by_head = pl.pallas_call(
        functools.partial(readout_kernel, recv_order, head_block, len(sources)),
        in_specs=[SCALARS] * 2 + [WHOLE] * (3 + len(sources) + len(received)),
        out_specs=[WHOLE] * 2,
        out_shape=[
            jax.ShapeDtypeStruct((own_rows, normed_columns), bf16),
            jax.ShapeDtypeStruct((heads, piece, size), bf16),
        ],
        scratch_shapes=[pltpu.VMEM((heads, slots, size), jnp.float32)],
        compiler_params=params(),
        name="readout",
    )(mine, gate_bias, tied["place"], gate_weight, norm_gain.reshape(heads, size), *sources, *received)

    near_done, turned, values, terms = pl.pallas_call(
        functools.partial(near_update_kernel, recv_order, head_block, blocks),
        in_specs=[SCALARS] * 3 + [WHOLE] * (3 + CAP),
        out_specs=[PLACED] + [WHOLE] * 3,
        out_shape=[
            pltpu.HBM(states.shape, bf16),
            jax.ShapeDtypeStruct((heads, size, slots), bf16),
            jax.ShapeDtypeStruct((heads, slots, size), jnp.float32),
            jax.ShapeDtypeStruct((2, heads, slots, size), jnp.float32),
        ],
        scratch_shapes=[pltpu.VMEM(states.shape, bf16), pltpu.SemaphoreType.DMA((own_rows,))],
        compiler_params=params(),
        name="near_update",
    )(mine, parents, gate_bias, by_head, gate_weight, held, *near_gots)

    far_block = math.gcd(extra, 4)

    def far_update(before, gots, entries, name):
        return pl.pallas_call(
            functools.partial(far_update_kernel, far_block, blocks, own_rows, entries),
            in_specs=[SCALARS] * 2 + [WHOLE] * (3 + len(gots)) + [PLACED],
            out_specs=PLACED,
            out_shape=jax.ShapeDtypeStruct(states.shape, bf16),
            scratch_shapes=[
                pltpu.VMEM((len(entries),) + one_state, bf16),
                pltpu.SemaphoreType.DMA((len(entries), heads // far_block)),
            ],
            input_output_aliases={5 + len(gots): 0},
            compiler_params=params(),
            name=name,
        )(mine, parents, tied["turned"], values, terms, *gots, before)

    def in_normed(stage, parts):
        if stage == 0:
            *parts, tied["rows"], tied["turned"] = lax.optimization_barrier((*parts, near_done, turned))
        if stage == 1:
            every = range(heads)
            entries = [(2, 0, 0, 0, every), (2, 1, 0, heads, every[:extra])]
            entries += [(3, rank, 1, rank * heads, every) for rank in range(CAP)]
            gots = [tied["first"], corner_got.reshape(CAP * heads, size, size)]
            far_done = far_update(tied["rows"], gots, entries, "far_update")
            *parts, tied["done"] = lax.optimization_barrier((*parts, far_done))
        return parts

    every_normed = gather_all(normed, plan, in_normed)
    layer_out = pl.pallas_call(
        functools.partial(output_kernel, own_rows),
        in_specs=[WHOLE] * (3 + len(every_normed)),
        out_specs=WHOLE,
        out_shape=jax.ShapeDtypeStruct((row_total, columns), bf16),
        scratch_shapes=[pltpu.VMEM(((normed_columns - width) // size, row_total, size), jnp.float32)],
        compiler_params=params(),
        name="output",
    )(local_columns, out_weight, out_pick, *every_normed)
    layer_out, last_got = lax.optimization_barrier((layer_out, last_got))
    final = far_update(tied["done"], [last_got], [(2, 1, 0, 0, range(extra, heads))], "last_update")
    return (layer_out[None], final)


def solution(mesh):
    placed = (
        P(None, "groups"),
        P(None, "groups", None),
        P(("groups", "rows"), None, None, None),
        P(None, "rows"),
        P(None, None, "rows"),
        P(),
        P(),
        P(),
        P(None, "rows"),
    )
    return jax.shard_map(
        per_device,
        mesh=mesh,
        in_specs=placed,
        out_specs=(P(None, "groups", "rows"), P(("groups", "rows"), None, None, None)),
        check_vma=False,
    )
```

```python
import functools
import math

import jax
import jax.numpy as jnp
from jax import lax
from jax.experimental import pallas as pl
from jax.experimental.pallas import tpu as pltpu
from jax.sharding import PartitionSpec as P

CAP = 2
FARS = 2 * CAP - 1
TILE = 16
VMEM_BYTES = 24 * 1024 * 1024
WHOLE = pl.BlockSpec(memory_space=pltpu.VMEM)
SCALARS = pl.BlockSpec(memory_space=pltpu.SMEM)
PLACED = pl.BlockSpec(memory_space=pl.ANY)


def params():
    return pltpu.CompilerParams(vmem_limit_bytes=VMEM_BYTES)


def in_hbm(array):
    return pltpu.with_memory_space_constraint(array, pltpu.HBM)


def in_vmem(array):
    return pltpu.with_memory_space_constraint(array, pltpu.VMEM)


def xor_permute(block, distance):
    count = lax.axis_size("rows")
    return lax.ppermute(block, "rows", [(i, i ^ distance) for i in range(count)])


def stage_plan(count):
    if count == 1:
        return []
    if count == 2:
        return [[1]]
    if count == 4:
        return [[2], [1]]
    plan = [[6], [12, 8, 4] if count >= 16 else [4]]
    bit = 16
    while bit < count:
        plan.append([bit])
        bit *= 2
    return plan + [[1]]


def plan_order(plan):
    order = [0]
    for stage in plan:
        order = [near ^ far for near in order for far in [0] + stage]
    return order


def gather_order(plan):
    order = [0]
    for stage in plan:
        order = [near ^ far for far in [0] + stage for near in order]
    return order


def gather_all(block, plan, after=lambda stage, held: held):
    held = [block]
    for number, stage in enumerate(plan):
        held = held + [xor_permute(part, distance) for distance in stage for part in held]
        if len(held) == 2:
            held = [jnp.concatenate(held, 0)]
        held = after(number, held)
    return held


def exchange_plan(plan):
    return plan[-1:] + plan[:-1]


def exchange_all(pieces, plan, after=lambda stage, held: held):
    tail = pieces.shape[1:]
    held = [pieces.reshape(tuple(len(stage) + 1 for stage in plan) + tail)]
    for axis, stage in enumerate(plan):
        fresh = []
        for part in held:
            slabs = [lax.index_in_dim(part, place, axis, keepdims=True) for place in range(len(stage) + 1)]
            fresh.append(slabs[0])
            fresh += [xor_permute(slab, distance) for slab, distance in zip(slabs[1:], stage)]
        held = after(axis, fresh if axis == len(plan) - 1 else [jnp.concatenate(fresh, axis)])
    return [part.reshape((-1,) + tail) for part in held]


def split(number, size):
    if size & (size - 1) == 0:
        return lax.shift_right_logical(number, size.bit_length() - 1), number & (size - 1)
    return lax.div(number, size), lax.rem(number, size)


def place_in(order, distance):
    place, bit = distance & 0, 0
    while 1 << bit < len(order):
        place = place ^ ((lax.shift_right_logical(distance, bit) & 1) * order.index(1 << bit))
        bit += 1
    return place


def row_facts(parent_row, blocks, own_rows):
    lane = lax.broadcasted_iota(jnp.int32, parent_row.shape, 1)
    device, child = split(lane, own_rows)
    parent_block, parent_place = split(parent_row, own_rows)
    rank = jnp.zeros_like(lane)
    for earlier in range(1, own_rows):
        same = (pltpu.roll(parent_block, earlier, 1) == parent_block) & (child >= earlier)
        rank = rank + same.astype(jnp.int32)
    return device, child, parent_block ^ (device & (blocks - 1)), rank, parent_place


def far_number(away, rank):
    return (away == 3) | ((away == 2) & (rank > 0)), jnp.where(away == 3, rank, CAP + rank - 1)


def column_of(row):
    spread = jnp.broadcast_to(row[0:1].astype(jnp.float32), (8, row.shape[1]))
    return jnp.transpose(spread)[:, 0:1]


def chosen_rows(column, width):
    shape = (column.shape[0], width)
    return (lax.broadcasted_iota(jnp.int32, shape, 1).astype(jnp.float32) == column).astype(jnp.float32)


def matching_children(parent_ref, user, child_block, parent_block, own_rows, none):
    children, parents, found = [jnp.int32(none)] * CAP, [jnp.int32(0)] * CAP, jnp.int32(0)
    for child in range(own_rows):
        block, place = split(parent_ref[0, user, child_block * own_rows + child], own_rows)
        hit = block == parent_block
        for j in range(CAP):
            children[j] = jnp.where(hit & (found == j), child, children[j])
            parents[j] = jnp.where(hit & (found == j), place, parents[j])
        found = found + hit.astype(jnp.int32)
    return children, parents


def fetch_kernel(
    blocks, me_ref, parent_ref, token_ref, tokens_ref, table_ref, states_ref, x_ref, y_ref, rows_ref, row_sem, state_sem
):
    count, own_rows, heads = token_ref.shape[1], states_ref.shape[0], states_ref.shape[1]
    user, member = split(me_ref[0], blocks)

    def start_row(r, carry):
        first = pl.multiple_of(split(token_ref[0, r], TILE)[0] * TILE, TILE)
        pltpu.make_async_copy(
            table_ref.at[pl.ds(first, TILE)],
            rows_ref.at[pl.ds(pl.multiple_of(r * TILE, TILE), TILE)],
            row_sem,
        ).start()
        return carry

    lax.fori_loop(0, count, start_row, 0, unroll=8)
    copies = []
    wanted = matching_children(parent_ref, user, member ^ 2, member, own_rows, 0)[1]
    extra = y_ref.shape[0] - heads
    for part, (row, first, size) in enumerate(((wanted[0], 0, heads // 2), (wanted[0], heads // 2, heads // 2), (wanted[1], 0, extra))):
        span, target = pl.ds(first, size), y_ref.at[pl.ds(part * (heads // 2), size)]
        copies.append(pltpu.make_async_copy(states_ref.at[row, span], target, state_sem.at[part]))
        copies[-1].start()
    step = math.gcd(count, 128)
    picks = []
    for first in range(0, count, step):
        low = column_of(split(tokens_ref[:, first : first + step], TILE)[1])
        wanted = low + lax.broadcasted_iota(jnp.int32, (step, 1), 0).astype(jnp.float32) * TILE
        picks.append(chosen_rows(wanted, step * TILE).astype(jnp.bfloat16))
    pltpu.make_async_copy(table_ref.at[pl.ds(0, count * TILE)], rows_ref, row_sem).wait()
    for first, pick in zip(range(0, count, step), picks):
        x_ref[first : first + step, :] = jnp.dot(
            pick, rows_ref[first * TILE : (first + step) * TILE, :], preferred_element_type=jnp.float32
        ).astype(jnp.bfloat16)
    for copy in copies:
        copy.wait()


def pick_kernel(blocks, piece, send_order, me_ref, parent_ref, parents_ref, states_ref, pick_ref, corner_ref, sem):
    me, rows, own_rows = me_ref[0], parents_ref.shape[1], states_ref.shape[0]
    user, member = split(me, blocks)
    copies = []
    for slot, row in enumerate(matching_children(parent_ref, user, member ^ 3, member, own_rows, 0)[1]):
        copies.append(pltpu.make_async_copy(states_ref.at[row], corner_ref.at[slot], sem.at[slot]))
        copies[-1].start()
    device, child, away, rank, _ = row_facts(parents_ref[...], blocks, own_rows)
    is_far, number = far_number(away, rank)
    own = place_in(send_order, device ^ me) * piece + child
    far = place_in(send_order, device ^ away ^ me) * piece + 3 * own_rows + number
    line = lax.broadcasted_iota(jnp.int32, (len(send_order) * piece, rows), 0)
    for slab in range(3):
        far_line = jnp.where(is_far, far + slab * FARS, -1)
        chosen = (line == own[0:1] + slab * own_rows) | (line == far_line[0:1])
        pick_ref[:, slab * rows : (slab + 1) * rows] = chosen.astype(jnp.float32).astype(jnp.bfloat16)
    for copy in copies:
        copy.wait()


def stage_kernel(blocks, normed_order, me_ref, parent_ref, parents_ref, states_ref, *refs):
    outs, (place_ref, pick_ref, hold_ref, in_sem, out_sem) = refs[:-5], refs[-5:]
    me, own_rows = me_ref[0], states_ref.shape[0]
    user, member = split(me, blocks)
    wanted = matching_children(parent_ref, user, member ^ 1, member, own_rows, 0)[1]
    wanted += matching_children(parent_ref, user, member ^ 2, member, own_rows, 0)[1][1:]
    heads = states_ref.shape[1]
    loads, saves = [], []
    for place, (row, out) in enumerate(zip(wanted, outs)):
        span, kept = pl.ds(heads - out.shape[0], out.shape[0]), pl.ds(0, out.shape[0])
        loads.append(pltpu.make_async_copy(states_ref.at[row, span], hold_ref.at[place, kept], in_sem.at[place]))
        saves.append(pltpu.make_async_copy(hold_ref.at[place, kept], out, out_sem.at[place]))
        loads[-1].start()
    device, child, away, rank, parent_place = row_facts(parents_ref[...], blocks, own_rows)
    is_far, number = far_number(away, rank)
    line = lax.broadcasted_iota(jnp.int32, (place_ref.shape[0], parents_ref.shape[1]), 0)
    own = (line == jnp.where((device == me) & ~is_far, child, -1)[0:1]).astype(jnp.float32)
    far = (line == jnp.where((device ^ away == me) & is_far, own_rows + number, -1)[0:1]).astype(jnp.float32)
    came = own_rows + jnp.where(away == 1, rank, CAP + rank)
    own_place = jnp.where(away == 0, parent_place, came)
    place = own * (own_place[0:1] + 1).astype(jnp.float32) + far * (parent_place[0:1] + 1).astype(jnp.float32)
    place_ref[...] = jnp.broadcast_to(jnp.sum(place, axis=1, keepdims=True) - 1.0, place_ref.shape)
    for load, save in zip(loads, saves):
        load.wait()
        save.start()
    count = len(normed_order)
    holder = place_in(normed_order, jnp.where(is_far, device ^ away, device) ^ me)
    index = jnp.where(is_far, count * own_rows + number * count + holder, holder * own_rows + child)
    pick_ref[...] = chosen_rows(column_of(index), pick_ref.shape[1]).astype(jnp.bfloat16)
    for save in saves:
        save.wait()


def hold_kernel(states_ref, held_ref, sem):
    copies = [pltpu.make_async_copy(states_ref.at[row], held_ref.at[row], sem.at[row]) for row in range(states_ref.shape[0])]
    for copy in copies:
        copy.start()
    for copy in copies:
        copy.wait()


def project_kernel(order, me_ref, weight_ref, pick_ref, *refs):
    held, out_ref = refs[:-1], refs[-1]
    me, columns, parts = me_ref[0], held[0].shape[1], len(held)
    rows = pick_ref.shape[1] // 3
    total = [None] * 3

    def block_at(place):
        ref, within = held[place * parts // len(order)], place % (len(order) // parts)
        return ref[within * rows : (within + 1) * rows, :]

    odd = (me & 1) == 1
    for place in range(len(order) // 2):
        here, other = block_at(place), block_at(order.index(order[place] ^ 1))
        flip = odd if order[place] & 1 == 0 else ~odd
        pair = jnp.concatenate([jnp.where(flip, other, here), jnp.where(flip, here, other)], 1)
        first = pl.multiple_of(((me ^ order[place]) >> 1) * (2 * columns), 2 * columns)
        for slab in range(3):
            term = jnp.dot(pair, weight_ref[slab, pl.ds(first, 2 * columns), :], preferred_element_type=jnp.float32)
            total[slab] = term if total[slab] is None else total[slab] + term
    every = jnp.concatenate([part.astype(jnp.bfloat16) for part in total], 0)
    out_ref[...] = jnp.dot(pick_ref[...], every, preferred_element_type=jnp.float32).astype(jnp.bfloat16)


def head_rows(piece, own_rows):
    piece = piece.astype(jnp.float32)
    far = piece[3 * own_rows :]
    slabs = []
    for slab in range(3):
        shifted = far if slab == 0 else pltpu.roll(far, far.shape[0] - slab * FARS, 0)
        slabs.append(jnp.concatenate([piece[slab * own_rows : (slab + 1) * own_rows], shifted[:own_rows]], 0))
    return slabs


def head_factors(keys, gate_row, bias, size):
    logit = jnp.sum(keys * gate_row, axis=-1, keepdims=True) / math.sqrt(size) + bias
    decay = 1.0 / (1.0 + jnp.exp(-logit))
    return decay, lax.rsqrt(jnp.sum(keys * keys, axis=-1, keepdims=True) + 1e-06)


def lane_of(recv_order, me, head):
    return head if recv_order is None else place_in(recv_order, me ^ head)


def readout_kernel(recv_order, block, near_count, me_ref, bias_ref, place_ref, gate_ref, gain_ref, *refs):
    sources, parts, (out_ref, recv_ref, norm_ref) = refs[:near_count], refs[near_count:-3], refs[-3:]
    own_rows, heads, size = sources[0].shape[0], sources[0].shape[1], sources[0].shape[2]
    slots = place_ref.shape[0]
    for number, part in enumerate(parts):
        for within in range(part.shape[0]):
            recv_ref[within * len(parts) + number] = part[within]
    place = place_ref[:, 0:1]
    joint = math.gcd(block, 2)
    states = sum(ref.shape[0] if len(ref.shape) == 4 else 1 for ref in sources)

    def work(step, carry):
        for group in range(0, block, joint):
            first_head = step * block + group
            rows = [
                head_rows(recv_ref[lane_of(recv_order, me_ref[0], first_head + n)], own_rows) for n in range(joint)
            ]
            spread = [
                jnp.concatenate([jnp.where(place == float(p), row[0], 0.0).astype(jnp.bfloat16) for p in range(states)], 1)
                for row in rows
            ]
            priors = []
            for n in range(joint):
                head = first_head + n
                one = [
                    ref[:, pl.ds(head, 1)].reshape(ref.shape[0] * size, size) if len(ref.shape) == 4 else ref[head]
                    for ref in sources
                ]
                priors.append(jnp.concatenate(one, 0))
            product = jnp.dot(
                jnp.concatenate(spread, 0), jnp.concatenate(priors, 1), preferred_element_type=jnp.float32
            )
            for n in range(joint):
                head = first_head + n
                queries, keys, values = rows[n]
                decay, inverse = head_factors(keys, gate_ref[pl.ds(head, 1), :], bias_ref[head], size)
                overlap = jnp.sum(queries * keys, axis=-1, keepdims=True) * inverse
                readout = decay * product[n * slots : (n + 1) * slots, n * size : (n + 1) * size] + overlap * values
                scale = lax.rsqrt(jnp.mean(readout * readout, axis=-1, keepdims=True) + 1e-05)
                norm_ref[head] = readout * scale * gain_ref[pl.ds(head, 1), :]
        return carry

    lax.fori_loop(0, heads // block, work, 0)
    share = heads // own_rows
    columns = [norm_ref[h][:own_rows] for h in range(heads)]
    for number in range(own_rows, own_rows + FARS):
        lines = []
        for line in range(own_rows):
            span = range(line * share, (line + 1) * share)
            lines.append(jnp.concatenate([norm_ref[h][number : number + 1] for h in span], 1))
        columns.append(jnp.concatenate(lines, 0))
    out_ref[...] = jnp.concatenate(columns, 1).astype(jnp.bfloat16)


def output_kernel(own_rows, x_ref, weight_ref, pick_ref, *refs):
    parts, (out_ref, far_ref) = refs[:-2], refs[-2:]
    width = weight_ref.shape[0]
    share = width // own_rows
    gathered = jnp.concatenate([part[...] for part in parts], 0)
    count = gathered.shape[0] // own_rows
    lanes = far_ref.shape[2]
    for block in range(far_ref.shape[0]):
        far_ref[block] = gathered[:, width + block * lanes : width + (block + 1) * lanes].astype(jnp.float32)
    rows = [gathered[:, :width]]
    blocks = share // lanes
    for number in range(FARS):
        spans = range(number * blocks, (number + 1) * blocks)
        lines = [far_ref[block, pl.ds(line, count, stride=own_rows), :] for line in range(own_rows) for block in spans]
        rows.append(jnp.concatenate(lines, 1).astype(jnp.bfloat16))
    rest = jnp.dot(jnp.concatenate(rows, 0), weight_ref[...], preferred_element_type=jnp.float32)
    total = x_ref[...].astype(jnp.float32)
    for _ in range(3):
        term = rest.astype(jnp.bfloat16)
        rest = rest - term.astype(jnp.float32)
        total = total + jnp.dot(pick_ref[...], term, preferred_element_type=jnp.float32)
    out_ref[...] = total.astype(jnp.bfloat16)


def near_update_kernel(
    recv_order, block, blocks, me_ref, parent_ref, bias_ref, recv_ref, gate_ref, states_ref,
    out_ref, turned_ref, values_ref, terms_ref, new_ref, out_sem,
):
    own_rows, heads, size = states_ref.shape[0], states_ref.shape[1], states_ref.shape[2]
    slots = values_ref.shape[1]
    user, member = split(me_ref[0], blocks)

    def prepare(step, carry):
        for part in range(block):
            head = step * block + part
            _, keys, values = head_rows(recv_ref[lane_of(recv_order, me_ref[0], head)], own_rows)
            decay, inverse = head_factors(keys, gate_ref[pl.ds(head, 1), :], bias_ref[head], size)
            turned_ref[head] = jnp.transpose(keys).astype(jnp.bfloat16)
            values_ref[head] = values
            terms_ref[0, head] = jnp.broadcast_to(decay, (slots, size))
            terms_ref[1, head] = jnp.broadcast_to(inverse, (slots, size))
        return carry

    lax.fori_loop(0, heads // block, prepare, 0)
    line = lax.broadcasted_iota(jnp.int32, (slots, size), 0)

    def save(row):
        return pltpu.make_async_copy(new_ref.at[row], out_ref.at[row], out_sem.at[row])

    def facts(row):
        parent_block, place = split(parent_ref[0, user, member * own_rows + row], own_rows)
        return parent_block ^ member, place

    def update(row, prior_of):
        for head in range(heads):
            value = jnp.where(line == row, values_ref[head], 0.0).astype(jnp.bfloat16)
            outer = jnp.dot(turned_ref[head], value, preferred_element_type=jnp.float32)
            fresh = terms_ref[0, head, pl.ds(row, 1), :] * prior_of(head).astype(jnp.float32)
            fresh = fresh + terms_ref[1, head, pl.ds(row, 1), :] * outer
            new_ref[row, head] = fresh.astype(jnp.bfloat16)
        save(row).start()

    def work(row, carry):
        away, place = facts(row)

        @pl.when(away == 0)
        def _():
            update(row, lambda head: states_ref[place, head])

        return carry

    lax.fori_loop(0, own_rows, work, 0)

    def finish(row, carry):
        @pl.when(facts(row)[0] == 0)
        def _():
            save(row).wait()

        return carry

    lax.fori_loop(0, own_rows, finish, 0)


def far_update_kernel(block, blocks, own_rows, entries, me_ref, parent_ref, turned_ref, values_ref, terms_ref, *refs):
    gots, (_, out_ref, new_ref, out_sem) = refs[:-4], refs[-4:]
    user, member = split(me_ref[0], blocks)
    children = [
        matching_children(parent_ref, user, member, member ^ partner, own_rows, -1)[0][rank] for partner, rank, *_ in entries
    ]
    line = lax.broadcasted_iota(jnp.int32, values_ref.shape[1:], 0)

    def save(entry, head):
        target = out_ref.at[jnp.maximum(children[entry], 0), pl.ds(head, block)]
        return pltpu.make_async_copy(new_ref.at[entry, pl.ds(head, block)], target, out_sem.at[entry, head // block])

    for entry, (_, _, array, start, heads) in enumerate(entries):
        got_ref, child = gots[array], children[entry]

        @pl.when(child >= 0)
        def _():
            for head in heads:
                value = jnp.where(line == child, values_ref[head], 0.0).astype(jnp.bfloat16)
                outer = jnp.dot(turned_ref[head], value, preferred_element_type=jnp.float32)
                prior = got_ref[start + head - heads[0]].astype(jnp.float32)
                fresh = terms_ref[0, head, pl.ds(child, 1), :] * prior
                fresh = fresh + terms_ref[1, head, pl.ds(child, 1), :] * outer
                new_ref[entry, head] = fresh.astype(jnp.bfloat16)
                if (head + 1) % block == 0:
                    save(entry, head + 1 - block).start()

    for entry, (_, _, _, _, heads) in enumerate(entries):

        @pl.when(children[entry] >= 0)
        def _():
            for head in heads[::block]:
                save(entry, head).wait()


def per_device(
    token_ids,
    parents,
    states,
    embed_table,
    qkv_weight,
    gate_weight,
    gate_bias,
    norm_gain,
    out_weight,
):
    own_rows, heads, size = states.shape[0], states.shape[1], states.shape[2]
    width = heads * size
    columns = embed_table.shape[1]
    row_total = token_ids.shape[1]
    users, beam = parents.shape[1], parents.shape[2]
    blocks = beam // own_rows
    count = lax.axis_size("rows")
    me = lax.axis_index("rows").astype(jnp.int32)
    user, member = me // blocks, me % blocks
    plan = stage_plan(count)
    steps = exchange_plan(plan)
    recv_order, normed_order = plan_order(steps), gather_order(plan)
    slots, piece = 2 * own_rows, 5 * own_rows
    one_state, two_states = (heads, size, size), (CAP, heads, size, size)
    normed_columns = width + FARS * width // own_rows
    bf16, int32 = jnp.bfloat16, jnp.int32
    mine = me[None]
    parent_row = jnp.broadcast_to(parents.reshape(1, row_total), (8, row_total))
    head_block = math.gcd(heads, 4)
    extra = heads // 4

    local_columns, first_out = pl.pallas_call(
        functools.partial(fetch_kernel, blocks),
        in_specs=[SCALARS, SCALARS, SCALARS, WHOLE, PLACED, PLACED],
        out_specs=[WHOLE] * 2,
        out_shape=[pltpu.VMEM((row_total, columns), bf16), pltpu.VMEM((heads + extra, size, size), bf16)],
        scratch_shapes=[
            pltpu.VMEM((row_total * TILE, columns), bf16),
            pltpu.SemaphoreType.DMA,
            pltpu.SemaphoreType.DMA((3,)),
        ],
        compiler_params=params(),
        name="fetch",
    )(mine, in_hbm(parents), in_hbm(token_ids), in_hbm(token_ids), in_hbm(embed_table), in_hbm(states))
    first_got = xor_permute(first_out, 2)

    send_pick, corner_out = pl.pallas_call(
        functools.partial(pick_kernel, blocks, piece, recv_order),
        in_specs=[SCALARS, SCALARS, WHOLE, PLACED],
        out_specs=[WHOLE] * 2,
        out_shape=[jax.ShapeDtypeStruct((count * piece, 3 * row_total), bf16), pltpu.VMEM(two_states, bf16)],
        scratch_shapes=[pltpu.SemaphoreType.DMA((CAP,))],
        compiler_params=params(),
        name="pick",
    )(mine, in_hbm(parents), parent_row, in_hbm(states))
    corner_got = xor_permute(corner_out, 3)

    *near_outs, last_out, place, out_pick = pl.pallas_call(
        functools.partial(stage_kernel, blocks, normed_order),
        in_specs=[SCALARS, SCALARS, WHOLE, PLACED],
        out_specs=[PLACED] * (CAP + 1) + [WHOLE] * 2,
        out_shape=[pltpu.HBM(one_state, bf16)] * CAP
        + [pltpu.HBM((heads - extra, size, size), bf16)]
        + [
            jax.ShapeDtypeStruct((slots, 128), jnp.float32),
            jax.ShapeDtypeStruct((row_total, row_total + FARS * count), bf16),
        ],
        scratch_shapes=[
            pltpu.VMEM((CAP + 1, heads, size, size), bf16),
            pltpu.SemaphoreType.DMA((CAP + 1,)),
            pltpu.SemaphoreType.DMA((CAP + 1,)),
        ],
        compiler_params=params(),
        name="stage",
    )(mine, in_hbm(parents), parent_row, in_hbm(states))
    near_gots = [xor_permute(block, 1) for block in near_outs]
    last_got = xor_permute(last_out, 2)

    held = pl.pallas_call(
        hold_kernel,
        in_specs=[PLACED],
        out_specs=WHOLE,
        out_shape=pltpu.VMEM(states.shape, bf16),
        scratch_shapes=[pltpu.SemaphoreType.DMA((own_rows,))],
        compiler_params=params(),
        name="hold",
    )(in_hbm(states))

    weight = jnp.transpose(qkv_weight, (1, 0, 2))
    tied = {}

    def in_inputs(stage, parts):
        if stage == 0:
            *parts, tied["weight"], tied["pick"] = lax.optimization_barrier((*parts, weight, send_pick))
        if stage == 1:
            *parts, tied["place"] = lax.optimization_barrier((*parts, place))
        if stage == len(plan) - 1:
            *parts, tied["first"] = lax.optimization_barrier((*parts, first_got))
        return parts

    every_input = gather_all(local_columns, plan, in_inputs)
    pieces = pl.pallas_call(
        functools.partial(project_kernel, normed_order),
        in_specs=[SCALARS] + [WHOLE] * (2 + len(every_input)),
        out_specs=WHOLE,
        out_shape=jax.ShapeDtypeStruct((count * piece, columns), bf16),
        compiler_params=params(),
        name="project",
    )(mine, tied["weight"], tied["pick"], *every_input)

    def in_exchange(stage, parts):
        if stage == 1:
            *parts, tied["near"], tied["nearer"] = lax.optimization_barrier((*parts, *near_gots))
        return parts

    received = exchange_all(pieces.reshape(count, piece, columns), steps, in_exchange)
    if columns != size:
        every_piece = jnp.stack(received, 1).reshape(count, piece, columns)
        places = jnp.array([recv_order.index(d) for d in range(count)], int32)[jnp.arange(count, dtype=int32) ^ me]
        every_piece = jnp.take(every_piece, places, axis=0).transpose(1, 0, 2).reshape(piece, heads, size)
        received = [every_piece.transpose(1, 0, 2)]
        recv_order = None

    held, near_gots = in_vmem(held), [tied["near"], tied["nearer"]]
    sources = [held, *near_gots, tied["first"]]
    normed, by_head = pl.pallas_call(
        functools.partial(readout_kernel, recv_order, math.gcd(heads, 8), len(sources)),
        in_specs=[SCALARS] * 2 + [WHOLE] * (3 + len(sources) + len(received)),
        out_specs=[WHOLE] * 2,
        out_shape=[
            jax.ShapeDtypeStruct((own_rows, normed_columns), bf16),
            jax.ShapeDtypeStruct((heads, piece, size), bf16),
        ],
        scratch_shapes=[pltpu.VMEM((heads, slots, size), jnp.float32)],
        compiler_params=params(),
        name="readout",
    )(mine, gate_bias, tied["place"], gate_weight, norm_gain.reshape(heads, size), *sources, *received)

    near_done, turned, values, terms = pl.pallas_call(
        functools.partial(near_update_kernel, recv_order, head_block, blocks),
        in_specs=[SCALARS] * 3 + [WHOLE] * 3,
        out_specs=[PLACED] + [WHOLE] * 3,
        out_shape=[
            pltpu.HBM(states.shape, bf16),
            jax.ShapeDtypeStruct((heads, size, slots), bf16),
            jax.ShapeDtypeStruct((heads, slots, size), jnp.float32),
            jax.ShapeDtypeStruct((2, heads, slots, size), jnp.float32),
        ],
        scratch_shapes=[pltpu.VMEM(states.shape, bf16), pltpu.SemaphoreType.DMA((own_rows,))],
        compiler_params=params(),
        name="near_update",
    )(mine, parents, gate_bias, by_head, gate_weight, held)

    far_block = math.gcd(extra, 4)

    def far_update(before, gots, entries, name):
        return pl.pallas_call(
            functools.partial(far_update_kernel, far_block, blocks, own_rows, entries),
            in_specs=[SCALARS] * 2 + [WHOLE] * (3 + len(gots)) + [PLACED],
            out_specs=PLACED,
            out_shape=jax.ShapeDtypeStruct(states.shape, bf16),
            scratch_shapes=[
                pltpu.VMEM((len(entries),) + one_state, bf16),
                pltpu.SemaphoreType.DMA((len(entries), heads // far_block)),
            ],
            input_output_aliases={5 + len(gots): 0},
            compiler_params=params(),
            name=name,
        )(mine, parents, tied["turned"], values, terms, *gots, before)

    def in_normed(stage, parts):
        if stage == 0:
            *parts, tied["rows"], tied["turned"] = lax.optimization_barrier((*parts, near_done, turned))
        if stage == 1:
            every = range(heads)
            entries = [(2, 0, 0, 0, every), (2, 1, 0, heads, every[:extra])]
            entries += [(3, rank, 1, rank * heads, every) for rank in range(CAP)]
            gots = [tied["first"], corner_got.reshape(CAP * heads, size, size)]
            entries += [(1, rank, 2 + rank, 0, every) for rank in range(CAP)]
            far_done = far_update(tied["rows"], gots + near_gots, entries, "far_update")
            *parts, tied["done"] = lax.optimization_barrier((*parts, far_done))
        return parts

    every_normed = gather_all(normed, plan, in_normed)
    layer_out = pl.pallas_call(
        functools.partial(output_kernel, own_rows),
        in_specs=[WHOLE] * (3 + len(every_normed)),
        out_specs=WHOLE,
        out_shape=jax.ShapeDtypeStruct((row_total, columns), bf16),
        scratch_shapes=[pltpu.VMEM(((normed_columns - width) // size, row_total, size), jnp.float32)],
        compiler_params=params(),
        name="output",
    )(local_columns, out_weight, out_pick, *every_normed)
    layer_out, last_got = lax.optimization_barrier((layer_out, last_got))
    final = far_update(tied["done"], [last_got], [(2, 1, 0, 0, range(extra, heads))], "last_update")
    return (layer_out[None], final)


def solution(mesh):
    placed = (
        P(None, "groups"),
        P(None, "groups", None),
        P(("groups", "rows"), None, None, None),
        P(None, "rows"),
        P(None, None, "rows"),
        P(),
        P(),
        P(),
        P(None, "rows"),
    )
    return jax.shard_map(
        per_device,
        mesh=mesh,
        in_specs=placed,
        out_specs=(P(None, "groups", "rows"), P(("groups", "rows"), None, None, None)),
        check_vma=False,
    )
```

```python
import functools
import math

import jax
import jax.numpy as jnp
from jax import lax
from jax.experimental import pallas as pl
from jax.experimental.pallas import tpu as pltpu
from jax.sharding import PartitionSpec as P

CAP = 2
FARS = 2 * CAP - 1
TILE = 16
VMEM_BYTES = 24 * 1024 * 1024
WHOLE = pl.BlockSpec(memory_space=pltpu.VMEM)
SCALARS = pl.BlockSpec(memory_space=pltpu.SMEM)
PLACED = pl.BlockSpec(memory_space=pl.ANY)


def params():
    return pltpu.CompilerParams(vmem_limit_bytes=VMEM_BYTES)


def in_hbm(array):
    return pltpu.with_memory_space_constraint(array, pltpu.HBM)


def in_vmem(array):
    return pltpu.with_memory_space_constraint(array, pltpu.VMEM)


def xor_permute(block, distance):
    count = lax.axis_size("rows")
    return lax.ppermute(block, "rows", [(i, i ^ distance) for i in range(count)])


def stage_plan(count):
    if count == 1:
        return []
    if count == 2:
        return [[1]]
    if count == 4:
        return [[2], [1]]
    plan = [[6], [12, 8, 4] if count >= 16 else [4]]
    bit = 16
    while bit < count:
        plan.append([bit])
        bit *= 2
    return plan + [[1]]


def plan_order(plan):
    order = [0]
    for stage in plan:
        order = [near ^ far for near in order for far in [0] + stage]
    return order


def gather_order(plan):
    order = [0]
    for stage in plan:
        order = [near ^ far for far in [0] + stage for near in order]
    return order


def gather_all(block, plan, after=lambda stage, held: held):
    held = [block]
    for number, stage in enumerate(plan):
        held = held + [xor_permute(part, distance) for distance in stage for part in held]
        if len(held) == 2:
            held = [jnp.concatenate(held, 0)]
        held = after(number, held)
    return held


def exchange_plan(plan):
    return plan[-1:] + plan[:-1]


def exchange_all(pieces, plan, after=lambda stage, held: held):
    tail = pieces.shape[1:]
    held = [pieces.reshape(tuple(len(stage) + 1 for stage in plan) + tail)]
    for axis, stage in enumerate(plan):
        fresh = []
        for part in held:
            slabs = [lax.index_in_dim(part, place, axis, keepdims=True) for place in range(len(stage) + 1)]
            fresh.append(slabs[0])
            fresh += [xor_permute(slab, distance) for slab, distance in zip(slabs[1:], stage)]
        held = after(axis, fresh if axis == len(plan) - 1 else [jnp.concatenate(fresh, axis)])
    return [part.reshape((-1,) + tail) for part in held]


def split(number, size):
    if size & (size - 1) == 0:
        return lax.shift_right_logical(number, size.bit_length() - 1), number & (size - 1)
    return lax.div(number, size), lax.rem(number, size)


def place_in(order, distance):
    place, bit = distance & 0, 0
    while 1 << bit < len(order):
        place = place ^ ((lax.shift_right_logical(distance, bit) & 1) * order.index(1 << bit))
        bit += 1
    return place


def row_facts(parent_row, blocks, own_rows):
    lane = lax.broadcasted_iota(jnp.int32, parent_row.shape, 1)
    device, child = split(lane, own_rows)
    parent_block, parent_place = split(parent_row, own_rows)
    rank = jnp.zeros_like(lane)
    for earlier in range(1, own_rows):
        same = (pltpu.roll(parent_block, earlier, 1) == parent_block) & (child >= earlier)
        rank = rank + same.astype(jnp.int32)
    return device, child, parent_block ^ (device & (blocks - 1)), rank, parent_place


def far_number(away, rank):
    return (away == 3) | ((away == 2) & (rank > 0)), jnp.where(away == 3, rank, CAP + rank - 1)


def column_of(row):
    spread = jnp.broadcast_to(row[0:1].astype(jnp.float32), (8, row.shape[1]))
    return jnp.transpose(spread)[:, 0:1]


def chosen_rows(column, width):
    shape = (column.shape[0], width)
    return (lax.broadcasted_iota(jnp.int32, shape, 1).astype(jnp.float32) == column).astype(jnp.float32)


def matching_children(parent_ref, user, child_block, parent_block, own_rows, none):
    children, parents, found = [jnp.int32(none)] * CAP, [jnp.int32(0)] * CAP, jnp.int32(0)
    for child in range(own_rows):
        block, place = split(parent_ref[0, user, child_block * own_rows + child], own_rows)
        hit = block == parent_block
        for j in range(CAP):
            children[j] = jnp.where(hit & (found == j), child, children[j])
            parents[j] = jnp.where(hit & (found == j), place, parents[j])
        found = found + hit.astype(jnp.int32)
    return children, parents


def fetch_kernel(
    blocks, me_ref, parent_ref, token_ref, tokens_ref, table_ref, states_ref, x_ref, y_ref, rows_ref, row_sem, state_sem
):
    count, own_rows, heads = token_ref.shape[1], states_ref.shape[0], states_ref.shape[1]
    user, member = split(me_ref[0], blocks)

    def start_row(r, carry):
        first = pl.multiple_of(split(token_ref[0, r], TILE)[0] * TILE, TILE)
        pltpu.make_async_copy(
            table_ref.at[pl.ds(first, TILE)],
            rows_ref.at[pl.ds(pl.multiple_of(r * TILE, TILE), TILE)],
            row_sem,
        ).start()
        return carry

    lax.fori_loop(0, count, start_row, 0, unroll=8)
    copies = []
    wanted = matching_children(parent_ref, user, member ^ 2, member, own_rows, 0)[1]
    extra = y_ref.shape[0] - heads
    for part, (row, first, size) in enumerate(((wanted[0], 0, heads // 2), (wanted[0], heads // 2, heads // 2), (wanted[1], 0, extra))):
        span, target = pl.ds(first, size), y_ref.at[pl.ds(part * (heads // 2), size)]
        copies.append(pltpu.make_async_copy(states_ref.at[row, span], target, state_sem.at[part]))
        copies[-1].start()
    step = math.gcd(count, 128)
    picks = []
    for first in range(0, count, step):
        low = column_of(split(tokens_ref[:, first : first + step], TILE)[1])
        wanted = low + lax.broadcasted_iota(jnp.int32, (step, 1), 0).astype(jnp.float32) * TILE
        picks.append(chosen_rows(wanted, step * TILE).astype(jnp.bfloat16))
    pltpu.make_async_copy(table_ref.at[pl.ds(0, count * TILE)], rows_ref, row_sem).wait()
    for first, pick in zip(range(0, count, step), picks):
        x_ref[first : first + step, :] = jnp.dot(
            pick, rows_ref[first * TILE : (first + step) * TILE, :], preferred_element_type=jnp.float32
        ).astype(jnp.bfloat16)
    for copy in copies:
        copy.wait()


def pick_kernel(blocks, piece, send_order, me_ref, parent_ref, parents_ref, states_ref, pick_ref, corner_ref, sem):
    me, rows, own_rows = me_ref[0], parents_ref.shape[1], states_ref.shape[0]
    user, member = split(me, blocks)
    copies = []
    for slot, row in enumerate(matching_children(parent_ref, user, member ^ 3, member, own_rows, 0)[1]):
        copies.append(pltpu.make_async_copy(states_ref.at[row], corner_ref.at[slot], sem.at[slot]))
        copies[-1].start()
    device, child, away, rank, _ = row_facts(parents_ref[...], blocks, own_rows)
    is_far, number = far_number(away, rank)
    own = place_in(send_order, device ^ me) * piece + child
    far = place_in(send_order, device ^ away ^ me) * piece + 3 * own_rows + number
    line = lax.broadcasted_iota(jnp.int32, (len(send_order) * piece, rows), 0)
    for slab in range(3):
        far_line = jnp.where(is_far, far + slab * FARS, -1)
        chosen = (line == own[0:1] + slab * own_rows) | (line == far_line[0:1])
        pick_ref[:, slab * rows : (slab + 1) * rows] = chosen.astype(jnp.float32).astype(jnp.bfloat16)
    for copy in copies:
        copy.wait()


def stage_kernel(blocks, normed_order, me_ref, parent_ref, parents_ref, states_ref, *refs):
    outs, (place_ref, pick_ref, hold_ref, in_sem, out_sem) = refs[:-5], refs[-5:]
    me, own_rows = me_ref[0], states_ref.shape[0]
    user, member = split(me, blocks)
    wanted = matching_children(parent_ref, user, member ^ 1, member, own_rows, 0)[1]
    wanted += matching_children(parent_ref, user, member ^ 2, member, own_rows, 0)[1][1:]
    heads = states_ref.shape[1]
    loads, saves = [], []
    for place, (row, out) in enumerate(zip(wanted, outs)):
        span, kept = pl.ds(heads - out.shape[0], out.shape[0]), pl.ds(0, out.shape[0])
        loads.append(pltpu.make_async_copy(states_ref.at[row, span], hold_ref.at[place, kept], in_sem.at[place]))
        saves.append(pltpu.make_async_copy(hold_ref.at[place, kept], out, out_sem.at[place]))
        loads[-1].start()
    device, child, away, rank, parent_place = row_facts(parents_ref[...], blocks, own_rows)
    is_far, number = far_number(away, rank)
    line = lax.broadcasted_iota(jnp.int32, (place_ref.shape[0], parents_ref.shape[1]), 0)
    own = (line == jnp.where((device == me) & ~is_far, child, -1)[0:1]).astype(jnp.float32)
    far = (line == jnp.where((device ^ away == me) & is_far, own_rows + number, -1)[0:1]).astype(jnp.float32)
    came = own_rows + jnp.where(away == 1, rank, CAP + rank)
    own_place = jnp.where(away == 0, parent_place, came)
    place = own * (own_place[0:1] + 1).astype(jnp.float32) + far * (parent_place[0:1] + 1).astype(jnp.float32)
    place_ref[...] = jnp.broadcast_to(jnp.sum(place, axis=1, keepdims=True) - 1.0, place_ref.shape)
    for load, save in zip(loads, saves):
        load.wait()
        save.start()
    count = len(normed_order)
    holder = place_in(normed_order, jnp.where(is_far, device ^ away, device) ^ me)
    index = jnp.where(is_far, count * own_rows + number * count + holder, holder * own_rows + child)
    pick_ref[...] = chosen_rows(column_of(index), pick_ref.shape[1]).astype(jnp.bfloat16)
    for save in saves:
        save.wait()


def hold_kernel(states_ref, held_ref, sem):
    copies = [pltpu.make_async_copy(states_ref.at[row], held_ref.at[row], sem.at[row]) for row in range(states_ref.shape[0])]
    for copy in copies:
        copy.start()
    for copy in copies:
        copy.wait()


def project_kernel(order, me_ref, weight_ref, pick_ref, *refs):
    held, out_ref = refs[:-1], refs[-1]
    me, columns, parts = me_ref[0], held[0].shape[1], len(held)
    rows = pick_ref.shape[1] // 3
    total = [None] * 3

    def block_at(place):
        ref, within = held[place * parts // len(order)], place % (len(order) // parts)
        return ref[within * rows : (within + 1) * rows, :]

    odd = (me & 1) == 1
    for place in range(len(order) // 2):
        here, other = block_at(place), block_at(order.index(order[place] ^ 1))
        flip = odd if order[place] & 1 == 0 else ~odd
        pair = jnp.concatenate([jnp.where(flip, other, here), jnp.where(flip, here, other)], 1)
        first = pl.multiple_of(((me ^ order[place]) >> 1) * (2 * columns), 2 * columns)
        for slab in range(3):
            term = jnp.dot(pair, weight_ref[slab, pl.ds(first, 2 * columns), :], preferred_element_type=jnp.float32)
            total[slab] = term if total[slab] is None else total[slab] + term
    every = jnp.concatenate([part.astype(jnp.bfloat16) for part in total], 0)
    out_ref[...] = jnp.dot(pick_ref[...], every, preferred_element_type=jnp.float32).astype(jnp.bfloat16)


def head_rows(piece, own_rows):
    piece = piece.astype(jnp.float32)
    far = piece[3 * own_rows :]
    slabs = []
    for slab in range(3):
        shifted = far if slab == 0 else pltpu.roll(far, far.shape[0] - slab * FARS, 0)
        slabs.append(jnp.concatenate([piece[slab * own_rows : (slab + 1) * own_rows], shifted[:own_rows]], 0))
    return slabs


def head_factors(keys, gate_row, bias, size):
    logit = jnp.sum(keys * gate_row, axis=-1, keepdims=True) / math.sqrt(size) + bias
    decay = 1.0 / (1.0 + jnp.exp(-logit))
    return decay, lax.rsqrt(jnp.sum(keys * keys, axis=-1, keepdims=True) + 1e-06)


def lane_of(recv_order, me, head):
    return head if recv_order is None else place_in(recv_order, me ^ head)


def readout_kernel(recv_order, block, near_count, me_ref, bias_ref, place_ref, gate_ref, gain_ref, *refs):
    sources, parts, (out_ref, recv_ref, norm_ref) = refs[:near_count], refs[near_count:-3], refs[-3:]
    own_rows, heads, size = sources[0].shape[0], sources[0].shape[1], sources[0].shape[2]
    slots = place_ref.shape[0]
    for number, part in enumerate(parts):
        for within in range(part.shape[0]):
            recv_ref[within * len(parts) + number] = part[within]
    place = place_ref[:, 0:1]
    joint = math.gcd(block, 2)
    states = sum(ref.shape[0] if len(ref.shape) == 4 else 1 for ref in sources)

    def work(step, carry):
        for group in range(0, block, joint):
            first_head = step * block + group
            rows = [
                head_rows(recv_ref[lane_of(recv_order, me_ref[0], first_head + n)], own_rows) for n in range(joint)
            ]
            spread = [
                jnp.concatenate([jnp.where(place == float(p), row[0], 0.0).astype(jnp.bfloat16) for p in range(states)], 1)
                for row in rows
            ]
            priors = []
            for n in range(joint):
                head = first_head + n
                one = [
                    ref[:, pl.ds(head, 1)].reshape(ref.shape[0] * size, size) if len(ref.shape) == 4 else ref[head]
                    for ref in sources
                ]
                priors.append(jnp.concatenate(one, 0))
            product = jnp.dot(
                jnp.concatenate(spread, 0), jnp.concatenate(priors, 1), preferred_element_type=jnp.float32
            )
            for n in range(joint):
                head = first_head + n
                queries, keys, values = rows[n]
                decay, inverse = head_factors(keys, gate_ref[pl.ds(head, 1), :], bias_ref[head], size)
                overlap = jnp.sum(queries * keys, axis=-1, keepdims=True) * inverse
                readout = decay * product[n * slots : (n + 1) * slots, n * size : (n + 1) * size] + overlap * values
                scale = lax.rsqrt(jnp.mean(readout * readout, axis=-1, keepdims=True) + 1e-05)
                norm_ref[head] = readout * scale * gain_ref[pl.ds(head, 1), :]
        return carry

    lax.fori_loop(0, heads // block, work, 0)
    share = heads // own_rows
    columns = [norm_ref[h][:own_rows] for h in range(heads)]
    for number in range(own_rows, own_rows + FARS):
        lines = []
        for line in range(own_rows):
            span = range(line * share, (line + 1) * share)
            lines.append(jnp.concatenate([norm_ref[h][number : number + 1] for h in span], 1))
        columns.append(jnp.concatenate(lines, 0))
    out_ref[...] = jnp.concatenate(columns, 1).astype(jnp.bfloat16)


def output_kernel(own_rows, x_ref, weight_ref, pick_ref, *refs):
    parts, (out_ref, far_ref) = refs[:-2], refs[-2:]
    width = weight_ref.shape[0]
    share = width // own_rows
    gathered = jnp.concatenate([part[...] for part in parts], 0)
    count = gathered.shape[0] // own_rows
    lanes = far_ref.shape[2]
    for block in range(far_ref.shape[0]):
        far_ref[block] = gathered[:, width + block * lanes : width + (block + 1) * lanes].astype(jnp.float32)
    rows = [gathered[:, :width]]
    blocks = share // lanes
    for number in range(FARS):
        spans = range(number * blocks, (number + 1) * blocks)
        lines = [far_ref[block, pl.ds(line, count, stride=own_rows), :] for line in range(own_rows) for block in spans]
        rows.append(jnp.concatenate(lines, 1).astype(jnp.bfloat16))
    rest = jnp.dot(jnp.concatenate(rows, 0), weight_ref[...], preferred_element_type=jnp.float32)
    total = x_ref[...].astype(jnp.float32)
    terms = []
    for _ in range(3):
        terms.append(rest.astype(jnp.bfloat16))
        rest = rest - terms[-1].astype(jnp.float32)
    sums = jnp.dot(pick_ref[...], jnp.concatenate(terms, 1), preferred_element_type=jnp.float32)
    columns = x_ref.shape[1]
    for part in range(3):
        total = total + sums[:, part * columns : (part + 1) * columns]
    out_ref[...] = total.astype(jnp.bfloat16)


def near_update_kernel(
    recv_order, block, blocks, me_ref, parent_ref, bias_ref, recv_ref, gate_ref, states_ref,
    out_ref, turned_ref, values_ref, terms_ref, new_ref, out_sem,
):
    own_rows, heads, size = states_ref.shape[0], states_ref.shape[1], states_ref.shape[2]
    slots = values_ref.shape[1]
    user, member = split(me_ref[0], blocks)

    def prepare(step, carry):
        for part in range(block):
            head = step * block + part
            _, keys, values = head_rows(recv_ref[lane_of(recv_order, me_ref[0], head)], own_rows)
            decay, inverse = head_factors(keys, gate_ref[pl.ds(head, 1), :], bias_ref[head], size)
            turned_ref[head] = jnp.transpose(keys).astype(jnp.bfloat16)
            values_ref[head] = values
            terms_ref[0, head] = jnp.broadcast_to(decay, (slots, size))
            terms_ref[1, head] = jnp.broadcast_to(inverse, (slots, size))
        return carry

    lax.fori_loop(0, heads // block, prepare, 0)
    line = lax.broadcasted_iota(jnp.int32, (slots, size), 0)

    def save(row):
        return pltpu.make_async_copy(new_ref.at[row], out_ref.at[row], out_sem.at[row])

    def facts(row):
        parent_block, place = split(parent_ref[0, user, member * own_rows + row], own_rows)
        return parent_block ^ member, place

    def update(row, prior_of):
        for head in range(heads):
            value = jnp.where(line == row, values_ref[head], 0.0).astype(jnp.bfloat16)
            outer = jnp.dot(turned_ref[head], value, preferred_element_type=jnp.float32)
            fresh = terms_ref[0, head, pl.ds(row, 1), :] * prior_of(head).astype(jnp.float32)
            fresh = fresh + terms_ref[1, head, pl.ds(row, 1), :] * outer
            new_ref[row, head] = fresh.astype(jnp.bfloat16)
        save(row).start()

    def work(row, carry):
        away, place = facts(row)

        @pl.when(away == 0)
        def _():
            update(row, lambda head: states_ref[place, head])

        return carry

    lax.fori_loop(0, own_rows, work, 0)

    def finish(row, carry):
        @pl.when(facts(row)[0] == 0)
        def _():
            save(row).wait()

        return carry

    lax.fori_loop(0, own_rows, finish, 0)


def far_update_kernel(block, blocks, own_rows, entries, me_ref, parent_ref, turned_ref, values_ref, terms_ref, *refs):
    gots, (_, out_ref, new_ref, out_sem) = refs[:-4], refs[-4:]
    user, member = split(me_ref[0], blocks)
    children = [
        matching_children(parent_ref, user, member, member ^ partner, own_rows, -1)[0][rank] for partner, rank, *_ in entries
    ]
    line = lax.broadcasted_iota(jnp.int32, values_ref.shape[1:], 0)

    def save(entry, head):
        target = out_ref.at[jnp.maximum(children[entry], 0), pl.ds(head, block)]
        return pltpu.make_async_copy(new_ref.at[entry, pl.ds(head, block)], target, out_sem.at[entry, head // block])

    for entry, (_, _, array, start, heads) in enumerate(entries):
        got_ref, child = gots[array], children[entry]

        @pl.when(child >= 0)
        def _():
            for head in heads:
                value = jnp.where(line == child, values_ref[head], 0.0).astype(jnp.bfloat16)
                outer = jnp.dot(turned_ref[head], value, preferred_element_type=jnp.float32)
                prior = got_ref[start + head - heads[0]].astype(jnp.float32)
                fresh = terms_ref[0, head, pl.ds(child, 1), :] * prior
                fresh = fresh + terms_ref[1, head, pl.ds(child, 1), :] * outer
                new_ref[entry, head] = fresh.astype(jnp.bfloat16)
                if (head + 1) % block == 0:
                    save(entry, head + 1 - block).start()

    for entry, (_, _, _, _, heads) in enumerate(entries):

        @pl.when(children[entry] >= 0)
        def _():
            for head in heads[::block]:
                save(entry, head).wait()


def per_device(
    token_ids,
    parents,
    states,
    embed_table,
    qkv_weight,
    gate_weight,
    gate_bias,
    norm_gain,
    out_weight,
):
    own_rows, heads, size = states.shape[0], states.shape[1], states.shape[2]
    width = heads * size
    columns = embed_table.shape[1]
    row_total = token_ids.shape[1]
    users, beam = parents.shape[1], parents.shape[2]
    blocks = beam // own_rows
    count = lax.axis_size("rows")
    me = lax.axis_index("rows").astype(jnp.int32)
    user, member = me // blocks, me % blocks
    plan = stage_plan(count)
    steps = exchange_plan(plan)
    recv_order, normed_order = plan_order(steps), gather_order(plan)
    slots, piece = 2 * own_rows, 5 * own_rows
    one_state, two_states = (heads, size, size), (CAP, heads, size, size)
    normed_columns = width + FARS * width // own_rows
    bf16, int32 = jnp.bfloat16, jnp.int32
    mine = me[None]
    parent_row = jnp.broadcast_to(parents.reshape(1, row_total), (8, row_total))
    head_block = math.gcd(heads, 4)
    extra = heads // 4

    local_columns, first_out = pl.pallas_call(
        functools.partial(fetch_kernel, blocks),
        in_specs=[SCALARS, SCALARS, SCALARS, WHOLE, PLACED, PLACED],
        out_specs=[WHOLE] * 2,
        out_shape=[pltpu.VMEM((row_total, columns), bf16), pltpu.VMEM((heads + extra, size, size), bf16)],
        scratch_shapes=[
            pltpu.VMEM((row_total * TILE, columns), bf16),
            pltpu.SemaphoreType.DMA,
            pltpu.SemaphoreType.DMA((3,)),
        ],
        compiler_params=params(),
        name="fetch",
    )(mine, in_hbm(parents), in_hbm(token_ids), in_hbm(token_ids), in_hbm(embed_table), in_hbm(states))
    first_got = xor_permute(first_out, 2)

    send_pick, corner_out = pl.pallas_call(
        functools.partial(pick_kernel, blocks, piece, recv_order),
        in_specs=[SCALARS, SCALARS, WHOLE, PLACED],
        out_specs=[WHOLE] * 2,
        out_shape=[jax.ShapeDtypeStruct((count * piece, 3 * row_total), bf16), pltpu.VMEM(two_states, bf16)],
        scratch_shapes=[pltpu.SemaphoreType.DMA((CAP,))],
        compiler_params=params(),
        name="pick",
    )(mine, in_hbm(parents), parent_row, in_hbm(states))
    corner_got = xor_permute(corner_out, 3)

    *near_outs, last_out, place, out_pick = pl.pallas_call(
        functools.partial(stage_kernel, blocks, normed_order),
        in_specs=[SCALARS, SCALARS, WHOLE, PLACED],
        out_specs=[PLACED] * (CAP + 1) + [WHOLE] * 2,
        out_shape=[pltpu.HBM(one_state, bf16)] * CAP
        + [pltpu.HBM((heads - extra, size, size), bf16)]
        + [
            jax.ShapeDtypeStruct((slots, 128), jnp.float32),
            jax.ShapeDtypeStruct((row_total, row_total + FARS * count), bf16),
        ],
        scratch_shapes=[
            pltpu.VMEM((CAP + 1, heads, size, size), bf16),
            pltpu.SemaphoreType.DMA((CAP + 1,)),
            pltpu.SemaphoreType.DMA((CAP + 1,)),
        ],
        compiler_params=params(),
        name="stage",
    )(mine, in_hbm(parents), parent_row, in_hbm(states))
    near_gots = [xor_permute(block, 1) for block in near_outs]
    last_got = xor_permute(last_out, 2)

    held = pl.pallas_call(
        hold_kernel,
        in_specs=[PLACED],
        out_specs=WHOLE,
        out_shape=pltpu.VMEM(states.shape, bf16),
        scratch_shapes=[pltpu.SemaphoreType.DMA((own_rows,))],
        compiler_params=params(),
        name="hold",
    )(in_hbm(states))

    weight = jnp.transpose(qkv_weight, (1, 0, 2))
    tied = {}

    def in_inputs(stage, parts):
        if stage == 0:
            *parts, tied["weight"], tied["pick"] = lax.optimization_barrier((*parts, weight, send_pick))
        if stage == 1:
            *parts, tied["place"] = lax.optimization_barrier((*parts, place))
        if stage == len(plan) - 1:
            *parts, tied["first"] = lax.optimization_barrier((*parts, first_got))
        return parts

    every_input = gather_all(local_columns, plan, in_inputs)
    pieces = pl.pallas_call(
        functools.partial(project_kernel, normed_order),
        in_specs=[SCALARS] + [WHOLE] * (2 + len(every_input)),
        out_specs=WHOLE,
        out_shape=jax.ShapeDtypeStruct((count * piece, columns), bf16),
        compiler_params=params(),
        name="project",
    )(mine, tied["weight"], tied["pick"], *every_input)

    def in_exchange(stage, parts):
        if stage == 1:
            *parts, tied["near"], tied["nearer"] = lax.optimization_barrier((*parts, *near_gots))
        return parts

    received = exchange_all(pieces.reshape(count, piece, columns), steps, in_exchange)
    if columns != size:
        every_piece = jnp.stack(received, 1).reshape(count, piece, columns)
        places = jnp.array([recv_order.index(d) for d in range(count)], int32)[jnp.arange(count, dtype=int32) ^ me]
        every_piece = jnp.take(every_piece, places, axis=0).transpose(1, 0, 2).reshape(piece, heads, size)
        received = [every_piece.transpose(1, 0, 2)]
        recv_order = None

    held, near_gots = in_vmem(held), [tied["near"], tied["nearer"]]
    sources = [held, *near_gots, tied["first"]]
    normed, by_head = pl.pallas_call(
        functools.partial(readout_kernel, recv_order, heads, len(sources)),
        in_specs=[SCALARS] * 2 + [WHOLE] * (3 + len(sources) + len(received)),
        out_specs=[WHOLE] * 2,
        out_shape=[
            jax.ShapeDtypeStruct((own_rows, normed_columns), bf16),
            jax.ShapeDtypeStruct((heads, piece, size), bf16),
        ],
        scratch_shapes=[pltpu.VMEM((heads, slots, size), jnp.float32)],
        compiler_params=params(),
        name="readout",
    )(mine, gate_bias, tied["place"], gate_weight, norm_gain.reshape(heads, size), *sources, *received)

    near_done, turned, values, terms = pl.pallas_call(
        functools.partial(near_update_kernel, recv_order, head_block, blocks),
        in_specs=[SCALARS] * 3 + [WHOLE] * 3,
        out_specs=[PLACED] + [WHOLE] * 3,
        out_shape=[
            pltpu.HBM(states.shape, bf16),
            jax.ShapeDtypeStruct((heads, size, slots), bf16),
            jax.ShapeDtypeStruct((heads, slots, size), jnp.float32),
            jax.ShapeDtypeStruct((2, heads, slots, size), jnp.float32),
        ],
        scratch_shapes=[pltpu.VMEM(states.shape, bf16), pltpu.SemaphoreType.DMA((own_rows,))],
        compiler_params=params(),
        name="near_update",
    )(mine, parents, gate_bias, by_head, gate_weight, held)

    far_block = math.gcd(extra, 4)

    def far_update(before, gots, entries, name):
        return pl.pallas_call(
            functools.partial(far_update_kernel, far_block, blocks, own_rows, entries),
            in_specs=[SCALARS] * 2 + [WHOLE] * (3 + len(gots)) + [PLACED],
            out_specs=PLACED,
            out_shape=jax.ShapeDtypeStruct(states.shape, bf16),
            scratch_shapes=[
                pltpu.VMEM((len(entries),) + one_state, bf16),
                pltpu.SemaphoreType.DMA((len(entries), heads // far_block)),
            ],
            input_output_aliases={5 + len(gots): 0},
            compiler_params=params(),
            name=name,
        )(mine, parents, tied["turned"], values, terms, *gots, before)

    def in_normed(stage, parts):
        if stage == 0:
            *parts, tied["rows"], tied["turned"] = lax.optimization_barrier((*parts, near_done, turned))
        if stage == 1:
            every = range(heads)
            entries = [(2, 0, 0, 0, every), (2, 1, 0, heads, every[:extra])]
            entries += [(3, rank, 1, rank * heads, every) for rank in range(CAP)]
            gots = [tied["first"], corner_got.reshape(CAP * heads, size, size)]
            entries += [(1, rank, 2 + rank, 0, every) for rank in range(CAP)]
            far_done = far_update(tied["rows"], gots + near_gots, entries, "far_update")
            *parts, tied["done"] = lax.optimization_barrier((*parts, far_done))
        return parts

    every_normed = gather_all(normed, plan, in_normed)
    layer_out = pl.pallas_call(
        functools.partial(output_kernel, own_rows),
        in_specs=[WHOLE] * (3 + len(every_normed)),
        out_specs=WHOLE,
        out_shape=jax.ShapeDtypeStruct((row_total, columns), bf16),
        scratch_shapes=[pltpu.VMEM(((normed_columns - width) // size, row_total, size), jnp.float32)],
        compiler_params=params(),
        name="output",
    )(local_columns, out_weight, out_pick, *every_normed)
    layer_out, last_got = lax.optimization_barrier((layer_out, last_got))
    final = far_update(tied["done"], [last_got], [(2, 1, 0, 0, range(extra, heads))], "last_update")
    return (layer_out[None], final)


def solution(mesh):
    placed = (
        P(None, "groups"),
        P(None, "groups", None),
        P(("groups", "rows"), None, None, None),
        P(None, "rows"),
        P(None, None, "rows"),
        P(),
        P(),
        P(),
        P(None, "rows"),
    )
    return jax.shard_map(
        per_device,
        mesh=mesh,
        in_specs=placed,
        out_specs=(P(None, "groups", "rows"), P(("groups", "rows"), None, None, None)),
        check_vma=False,
    )
```

```python
import functools
import math

import jax
import jax.numpy as jnp
from jax import lax
from jax.experimental import pallas as pl
from jax.experimental.pallas import tpu as pltpu
from jax.sharding import PartitionSpec as P

CAP = 2
FARS = 2 * CAP - 1
TILE = 16
VMEM_BYTES = 24 * 1024 * 1024
WHOLE = pl.BlockSpec(memory_space=pltpu.VMEM)
SCALARS = pl.BlockSpec(memory_space=pltpu.SMEM)
PLACED = pl.BlockSpec(memory_space=pl.ANY)


def params():
    return pltpu.CompilerParams(vmem_limit_bytes=VMEM_BYTES)


def in_hbm(array):
    return pltpu.with_memory_space_constraint(array, pltpu.HBM)


def in_vmem(array):
    return pltpu.with_memory_space_constraint(array, pltpu.VMEM)


def xor_permute(block, distance):
    count = lax.axis_size("rows")
    return lax.ppermute(block, "rows", [(i, i ^ distance) for i in range(count)])


def stage_plan(count):
    if count == 1:
        return []
    if count == 2:
        return [[1]]
    if count == 4:
        return [[2], [1]]
    plan = [[6], [12, 8, 4] if count >= 16 else [4]]
    bit = 16
    while bit < count:
        plan.append([bit])
        bit *= 2
    return plan + [[1]]


def plan_order(plan):
    order = [0]
    for stage in plan:
        order = [near ^ far for near in order for far in [0] + stage]
    return order


def gather_order(plan):
    order = [0]
    for stage in plan:
        order = [near ^ far for far in [0] + stage for near in order]
    return order


def gather_all(block, plan, after=lambda stage, held: held):
    held = [block]
    for number, stage in enumerate(plan):
        held = held + [xor_permute(part, distance) for distance in stage for part in held]
        if len(held) == 2:
            held = [jnp.concatenate(held, 0)]
        held = after(number, held)
    return held


def exchange_plan(plan):
    return plan[-1:] + plan[:-1]


def exchange_all(pieces, plan, after=lambda stage, held: held):
    tail = pieces.shape[1:]
    held = [pieces.reshape(tuple(len(stage) + 1 for stage in plan) + tail)]
    for axis, stage in enumerate(plan):
        fresh = []
        for part in held:
            slabs = [lax.index_in_dim(part, place, axis, keepdims=True) for place in range(len(stage) + 1)]
            fresh.append(slabs[0])
            fresh += [xor_permute(slab, distance) for slab, distance in zip(slabs[1:], stage)]
        held = after(axis, fresh if axis == len(plan) - 1 else [jnp.concatenate(fresh, axis)])
    return [part.reshape((-1,) + tail) for part in held]


def split(number, size):
    if size & (size - 1) == 0:
        return lax.shift_right_logical(number, size.bit_length() - 1), number & (size - 1)
    return lax.div(number, size), lax.rem(number, size)


def place_in(order, distance):
    place, bit = distance & 0, 0
    while 1 << bit < len(order):
        place = place ^ ((lax.shift_right_logical(distance, bit) & 1) * order.index(1 << bit))
        bit += 1
    return place


def row_facts(parent_row, blocks, own_rows):
    lane = lax.broadcasted_iota(jnp.int32, parent_row.shape, 1)
    device, child = split(lane, own_rows)
    parent_block, parent_place = split(parent_row, own_rows)
    rank = jnp.zeros_like(lane)
    for earlier in range(1, own_rows):
        same = (pltpu.roll(parent_block, earlier, 1) == parent_block) & (child >= earlier)
        rank = rank + same.astype(jnp.int32)
    return device, child, parent_block ^ (device & (blocks - 1)), rank, parent_place


def far_number(away, rank):
    return (away == 3) | ((away == 2) & (rank > 0)), jnp.where(away == 3, rank, CAP + rank - 1)


def column_of(row):
    spread = jnp.broadcast_to(row[0:1].astype(jnp.float32), (8, row.shape[1]))
    return jnp.transpose(spread)[:, 0:1]


def chosen_rows(column, width):
    shape = (column.shape[0], width)
    return (lax.broadcasted_iota(jnp.int32, shape, 1).astype(jnp.float32) == column).astype(jnp.float32)


def matching_children(parent_ref, user, child_block, parent_block, own_rows, none):
    children, parents, found = [jnp.int32(none)] * CAP, [jnp.int32(0)] * CAP, jnp.int32(0)
    for child in range(own_rows):
        block, place = split(parent_ref[0, user, child_block * own_rows + child], own_rows)
        hit = block == parent_block
        for j in range(CAP):
            children[j] = jnp.where(hit & (found == j), child, children[j])
            parents[j] = jnp.where(hit & (found == j), place, parents[j])
        found = found + hit.astype(jnp.int32)
    return children, parents


def fetch_kernel(
    blocks, me_ref, parent_ref, token_ref, tokens_ref, table_ref, states_ref, x_ref, y_ref, rows_ref, row_sem, state_sem
):
    count, own_rows, heads = token_ref.shape[1], states_ref.shape[0], states_ref.shape[1]
    user, member = split(me_ref[0], blocks)

    def start_row(r, carry):
        first = pl.multiple_of(split(token_ref[0, r], TILE)[0] * TILE, TILE)
        pltpu.make_async_copy(
            table_ref.at[pl.ds(first, TILE)],
            rows_ref.at[pl.ds(pl.multiple_of(r * TILE, TILE), TILE)],
            row_sem,
        ).start()
        return carry

    lax.fori_loop(0, count, start_row, 0, unroll=8)
    copies = []
    wanted = matching_children(parent_ref, user, member ^ 2, member, own_rows, 0)[1]
    extra = y_ref.shape[0] - heads
    for part, (row, first, size) in enumerate(((wanted[0], 0, heads // 2), (wanted[0], heads // 2, heads // 2), (wanted[1], 0, extra))):
        span, target = pl.ds(first, size), y_ref.at[pl.ds(part * (heads // 2), size)]
        copies.append(pltpu.make_async_copy(states_ref.at[row, span], target, state_sem.at[part]))
        copies[-1].start()
    step = math.gcd(count, 128)
    picks = []
    for first in range(0, count, step):
        low = column_of(split(tokens_ref[:, first : first + step], TILE)[1])
        wanted = low + lax.broadcasted_iota(jnp.int32, (step, 1), 0).astype(jnp.float32) * TILE
        picks.append(chosen_rows(wanted, step * TILE).astype(jnp.bfloat16))
    pltpu.make_async_copy(table_ref.at[pl.ds(0, count * TILE)], rows_ref, row_sem).wait()
    for first, pick in zip(range(0, count, step), picks):
        x_ref[first : first + step, :] = jnp.dot(
            pick, rows_ref[first * TILE : (first + step) * TILE, :], preferred_element_type=jnp.float32
        ).astype(jnp.bfloat16)
    for copy in copies:
        copy.wait()


def pick_kernel(blocks, piece, send_order, me_ref, parent_ref, parents_ref, states_ref, pick_ref, corner_ref, sem):
    me, rows, own_rows = me_ref[0], parents_ref.shape[1], states_ref.shape[0]
    user, member = split(me, blocks)
    copies = []
    for slot, row in enumerate(matching_children(parent_ref, user, member ^ 3, member, own_rows, 0)[1]):
        copies.append(pltpu.make_async_copy(states_ref.at[row], corner_ref.at[slot], sem.at[slot]))
        copies[-1].start()
    device, child, away, rank, _ = row_facts(parents_ref[...], blocks, own_rows)
    is_far, number = far_number(away, rank)
    own = place_in(send_order, device ^ me) * piece + child
    far = place_in(send_order, device ^ away ^ me) * piece + 3 * own_rows + number
    line = lax.broadcasted_iota(jnp.int32, (len(send_order) * piece, rows), 0)
    for slab in range(3):
        far_line = jnp.where(is_far, far + slab * FARS, -1)
        chosen = (line == own[0:1] + slab * own_rows) | (line == far_line[0:1])
        pick_ref[:, slab * rows : (slab + 1) * rows] = chosen.astype(jnp.float32).astype(jnp.bfloat16)
    for copy in copies:
        copy.wait()


def stage_kernel(blocks, normed_order, me_ref, parent_ref, parents_ref, states_ref, *refs):
    outs, (place_ref, pick_ref, hold_ref, in_sem, out_sem) = refs[:-5], refs[-5:]
    me, own_rows = me_ref[0], states_ref.shape[0]
    user, member = split(me, blocks)
    wanted = matching_children(parent_ref, user, member ^ 1, member, own_rows, 0)[1]
    wanted += matching_children(parent_ref, user, member ^ 2, member, own_rows, 0)[1][1:]
    heads = states_ref.shape[1]
    loads, saves = [], []
    for place, (row, out) in enumerate(zip(wanted, outs)):
        span, kept = pl.ds(heads - out.shape[0], out.shape[0]), pl.ds(0, out.shape[0])
        loads.append(pltpu.make_async_copy(states_ref.at[row, span], hold_ref.at[place, kept], in_sem.at[place]))
        saves.append(pltpu.make_async_copy(hold_ref.at[place, kept], out, out_sem.at[place]))
        loads[-1].start()
    device, child, away, rank, parent_place = row_facts(parents_ref[...], blocks, own_rows)
    is_far, number = far_number(away, rank)
    line = lax.broadcasted_iota(jnp.int32, (place_ref.shape[0], parents_ref.shape[1]), 0)
    own = (line == jnp.where((device == me) & ~is_far, child, -1)[0:1]).astype(jnp.float32)
    far = (line == jnp.where((device ^ away == me) & is_far, own_rows + number, -1)[0:1]).astype(jnp.float32)
    came = own_rows + jnp.where(away == 1, rank, CAP + rank)
    own_place = jnp.where(away == 0, parent_place, came)
    place = own * (own_place[0:1] + 1).astype(jnp.float32) + far * (parent_place[0:1] + 1).astype(jnp.float32)
    place_ref[...] = jnp.broadcast_to(jnp.sum(place, axis=1, keepdims=True) - 1.0, place_ref.shape)
    for load, save in zip(loads, saves):
        load.wait()
        save.start()
    count = len(normed_order)
    holder = place_in(normed_order, jnp.where(is_far, device ^ away, device) ^ me)
    index = jnp.where(is_far, count * own_rows + number * count + holder, holder * own_rows + child)
    pick_ref[...] = chosen_rows(column_of(index), pick_ref.shape[1]).astype(jnp.bfloat16)
    for save in saves:
        save.wait()


def hold_kernel(states_ref, held_ref, sem):
    copies = [pltpu.make_async_copy(states_ref.at[row], held_ref.at[row], sem.at[row]) for row in range(states_ref.shape[0])]
    for copy in copies:
        copy.start()
    for copy in copies:
        copy.wait()


def project_kernel(order, me_ref, weight_ref, pick_ref, *refs):
    held, out_ref = refs[:-1], refs[-1]
    me, columns, parts = me_ref[0], held[0].shape[1], len(held)
    rows = pick_ref.shape[1] // 3
    total = [None] * 3

    def block_at(place):
        ref, within = held[place * parts // len(order)], place % (len(order) // parts)
        return ref[within * rows : (within + 1) * rows, :]

    odd = (me & 1) == 1
    for place in range(len(order) // 2):
        here, other = block_at(place), block_at(order.index(order[place] ^ 1))
        flip = odd if order[place] & 1 == 0 else ~odd
        pair = jnp.concatenate([jnp.where(flip, other, here), jnp.where(flip, here, other)], 1)
        first = pl.multiple_of(((me ^ order[place]) >> 1) * (2 * columns), 2 * columns)
        for slab in range(3):
            term = jnp.dot(pair, weight_ref[slab, pl.ds(first, 2 * columns), :], preferred_element_type=jnp.float32)
            total[slab] = term if total[slab] is None else total[slab] + term
    every = jnp.concatenate([part.astype(jnp.bfloat16) for part in total], 0)
    out_ref[...] = jnp.dot(pick_ref[...], every, preferred_element_type=jnp.float32).astype(jnp.bfloat16)


def head_rows(piece, own_rows):
    piece = piece.astype(jnp.float32)
    far = piece[3 * own_rows :]
    slabs = []
    for slab in range(3):
        shifted = far if slab == 0 else pltpu.roll(far, far.shape[0] - slab * FARS, 0)
        slabs.append(jnp.concatenate([piece[slab * own_rows : (slab + 1) * own_rows], shifted[:own_rows]], 0))
    return slabs


def head_factors(keys, gate_row, bias, size):
    logit = jnp.sum(keys * gate_row, axis=-1, keepdims=True) / math.sqrt(size) + bias
    decay = 1.0 / (1.0 + jnp.exp(-logit))
    return decay, lax.rsqrt(jnp.sum(keys * keys, axis=-1, keepdims=True) + 1e-06)


def lane_of(recv_order, me, head):
    return head if recv_order is None else place_in(recv_order, me ^ head)


def readout_kernel(recv_order, block, near_count, me_ref, bias_ref, place_ref, gate_ref, gain_ref, *refs):
    sources, parts, (out_ref, recv_ref, norm_ref) = refs[:near_count], refs[near_count:-3], refs[-3:]
    own_rows, heads, size = sources[0].shape[0], sources[0].shape[1], sources[0].shape[2]
    slots = place_ref.shape[0]
    for number, part in enumerate(parts):
        for within in range(part.shape[0]):
            recv_ref[within * len(parts) + number] = part[within]
    place = place_ref[:, 0:1]
    joint = math.gcd(block, 2)
    states = sum(ref.shape[0] if len(ref.shape) == 4 else 1 for ref in sources)

    def work(step, carry):
        for group in range(0, block, joint):
            first_head = step * block + group
            rows = [
                head_rows(recv_ref[lane_of(recv_order, me_ref[0], first_head + n)], own_rows) for n in range(joint)
            ]
            spread = [
                jnp.concatenate([jnp.where(place == float(p), row[0], 0.0).astype(jnp.bfloat16) for p in range(states)], 1)
                for row in rows
            ]
            priors = []
            for n in range(joint):
                head = first_head + n
                one = [
                    ref[:, pl.ds(head, 1)].reshape(ref.shape[0] * size, size) if len(ref.shape) == 4 else ref[head]
                    for ref in sources
                ]
                priors.append(jnp.concatenate(one, 0))
            product = jnp.dot(
                jnp.concatenate(spread, 0), jnp.concatenate(priors, 1), preferred_element_type=jnp.float32
            )
            for n in range(joint):
                head = first_head + n
                queries, keys, values = rows[n]
                decay, inverse = head_factors(keys, gate_ref[pl.ds(head, 1), :], bias_ref[head], size)
                overlap = jnp.sum(queries * keys, axis=-1, keepdims=True) * inverse
                readout = decay * product[n * slots : (n + 1) * slots, n * size : (n + 1) * size] + overlap * values
                scale = lax.rsqrt(jnp.mean(readout * readout, axis=-1, keepdims=True) + 1e-05)
                norm_ref[head] = readout * scale * gain_ref[pl.ds(head, 1), :]
        return carry

    lax.fori_loop(0, heads // block, work, 0)
    share = heads // own_rows
    columns = [norm_ref[h][:own_rows] for h in range(heads)]
    for number in range(own_rows, own_rows + FARS):
        lines = []
        for line in range(own_rows):
            span = range(line * share, (line + 1) * share)
            lines.append(jnp.concatenate([norm_ref[h][number : number + 1] for h in span], 1))
        columns.append(jnp.concatenate(lines, 0))
    out_ref[...] = jnp.concatenate(columns, 1).astype(jnp.bfloat16)


def output_kernel(own_rows, x_ref, weight_ref, pick_ref, *refs):
    parts, (out_ref, far_ref) = refs[:-2], refs[-2:]
    width = weight_ref.shape[0]
    share = width // own_rows
    gathered = jnp.concatenate([part[...] for part in parts], 0)
    count = gathered.shape[0] // own_rows
    lanes = far_ref.shape[2]
    for block in range(far_ref.shape[0]):
        far_ref[block] = gathered[:, width + block * lanes : width + (block + 1) * lanes].astype(jnp.float32)
    rows = [gathered[:, :width]]
    blocks = share // lanes
    for number in range(FARS):
        spans = range(number * blocks, (number + 1) * blocks)
        lines = [far_ref[block, pl.ds(line, count, stride=own_rows), :] for line in range(own_rows) for block in spans]
        rows.append(jnp.concatenate(lines, 1).astype(jnp.bfloat16))
    rest = jnp.dot(jnp.concatenate(rows, 0), weight_ref[...], preferred_element_type=jnp.float32)
    total = x_ref[...].astype(jnp.float32)
    terms = []
    for _ in range(3):
        terms.append(rest.astype(jnp.bfloat16))
        rest = rest - terms[-1].astype(jnp.float32)
    sums = jnp.dot(pick_ref[...], jnp.concatenate(terms, 1), preferred_element_type=jnp.float32)
    columns = x_ref.shape[1]
    for part in range(3):
        total = total + sums[:, part * columns : (part + 1) * columns]
    out_ref[...] = total.astype(jnp.bfloat16)


def near_update_kernel(
    recv_order, block, blocks, me_ref, parent_ref, bias_ref, recv_ref, gate_ref, states_ref,
    out_ref, turned_ref, values_ref, terms_ref, new_ref, out_sem,
):
    own_rows, heads, size = states_ref.shape[0], states_ref.shape[1], states_ref.shape[2]
    slots = values_ref.shape[1]
    user, member = split(me_ref[0], blocks)

    def prepare(step, carry):
        for part in range(block):
            head = step * block + part
            _, keys, values = head_rows(recv_ref[lane_of(recv_order, me_ref[0], head)], own_rows)
            decay, inverse = head_factors(keys, gate_ref[pl.ds(head, 1), :], bias_ref[head], size)
            turned_ref[head] = jnp.transpose(keys).astype(jnp.bfloat16)
            values_ref[head] = values
            terms_ref[0, head] = jnp.broadcast_to(decay, (slots, size))
            terms_ref[1, head] = jnp.broadcast_to(inverse, (slots, size))
        return carry

    lax.fori_loop(0, heads // block, prepare, 0)
    line = lax.broadcasted_iota(jnp.int32, (slots, size), 0)

    def save(row):
        return pltpu.make_async_copy(new_ref.at[row], out_ref.at[row], out_sem.at[row])

    def facts(row):
        parent_block, place = split(parent_ref[0, user, member * own_rows + row], own_rows)
        return parent_block ^ member, place

    def update(row, prior_of):
        for head in range(heads):
            value = jnp.where(line == row, values_ref[head], 0.0).astype(jnp.bfloat16)
            outer = jnp.dot(turned_ref[head], value, preferred_element_type=jnp.float32)
            fresh = terms_ref[0, head, pl.ds(row, 1), :] * prior_of(head).astype(jnp.float32)
            fresh = fresh + terms_ref[1, head, pl.ds(row, 1), :] * outer
            new_ref[row, head] = fresh.astype(jnp.bfloat16)
        save(row).start()

    def work(row, carry):
        away, place = facts(row)

        @pl.when(away == 0)
        def _():
            update(row, lambda head: states_ref[place, head])

        return carry

    lax.fori_loop(0, own_rows, work, 0)

    def finish(row, carry):
        @pl.when(facts(row)[0] == 0)
        def _():
            save(row).wait()

        return carry

    lax.fori_loop(0, own_rows, finish, 0)


def far_update_kernel(block, blocks, own_rows, entries, me_ref, parent_ref, turned_ref, values_ref, terms_ref, *refs):
    gots, (_, out_ref, new_ref, out_sem) = refs[:-4], refs[-4:]
    user, member = split(me_ref[0], blocks)
    children = [
        matching_children(parent_ref, user, member, member ^ partner, own_rows, -1)[0][rank] for partner, rank, *_ in entries
    ]
    line = lax.broadcasted_iota(jnp.int32, values_ref.shape[1:], 0)

    def save(entry, head):
        target = out_ref.at[jnp.maximum(children[entry], 0), pl.ds(head, block)]
        return pltpu.make_async_copy(new_ref.at[entry, pl.ds(head, block)], target, out_sem.at[entry, head // block])

    for entry, (_, _, array, start, heads) in enumerate(entries):
        got_ref, child = gots[array], children[entry]

        @pl.when(child >= 0)
        def _():
            for head in heads:
                value = jnp.where(line == child, values_ref[head], 0.0).astype(jnp.bfloat16)
                outer = jnp.dot(turned_ref[head], value, preferred_element_type=jnp.float32)
                prior = got_ref[start + head - heads[0]].astype(jnp.float32)
                fresh = terms_ref[0, head, pl.ds(child, 1), :] * prior
                fresh = fresh + terms_ref[1, head, pl.ds(child, 1), :] * outer
                new_ref[entry, head] = fresh.astype(jnp.bfloat16)
                if (head + 1) % block == 0:
                    save(entry, head + 1 - block).start()

    for entry, (_, _, _, _, heads) in enumerate(entries):

        @pl.when(children[entry] >= 0)
        def _():
            for head in heads[::block]:
                save(entry, head).wait()


def per_device(
    token_ids,
    parents,
    states,
    embed_table,
    qkv_weight,
    gate_weight,
    gate_bias,
    norm_gain,
    out_weight,
):
    own_rows, heads, size = states.shape[0], states.shape[1], states.shape[2]
    width = heads * size
    columns = embed_table.shape[1]
    row_total = token_ids.shape[1]
    users, beam = parents.shape[1], parents.shape[2]
    blocks = beam // own_rows
    count = lax.axis_size("rows")
    me = lax.axis_index("rows").astype(jnp.int32)
    user, member = me // blocks, me % blocks
    plan = stage_plan(count)
    steps = exchange_plan(plan)
    recv_order, normed_order = plan_order(steps), gather_order(plan)
    slots, piece = 2 * own_rows, 5 * own_rows
    one_state, two_states = (heads, size, size), (CAP, heads, size, size)
    normed_columns = width + FARS * width // own_rows
    bf16, int32 = jnp.bfloat16, jnp.int32
    mine = me[None]
    parent_row = jnp.broadcast_to(parents.reshape(1, row_total), (8, row_total))
    head_block = math.gcd(heads, 4)
    extra = heads // 4

    local_columns, first_out = pl.pallas_call(
        functools.partial(fetch_kernel, blocks),
        in_specs=[SCALARS, SCALARS, SCALARS, WHOLE, PLACED, PLACED],
        out_specs=[WHOLE] * 2,
        out_shape=[pltpu.VMEM((row_total, columns), bf16), pltpu.VMEM((heads + extra, size, size), bf16)],
        scratch_shapes=[
            pltpu.VMEM((row_total * TILE, columns), bf16),
            pltpu.SemaphoreType.DMA,
            pltpu.SemaphoreType.DMA((3,)),
        ],
        compiler_params=params(),
        name="fetch",
    )(mine, in_hbm(parents), in_hbm(token_ids), in_hbm(token_ids), in_hbm(embed_table), in_hbm(states))
    first_got = xor_permute(first_out, 2)

    send_pick, corner_out = pl.pallas_call(
        functools.partial(pick_kernel, blocks, piece, recv_order),
        in_specs=[SCALARS, SCALARS, WHOLE, PLACED],
        out_specs=[WHOLE] * 2,
        out_shape=[jax.ShapeDtypeStruct((count * piece, 3 * row_total), bf16), pltpu.VMEM(two_states, bf16)],
        scratch_shapes=[pltpu.SemaphoreType.DMA((CAP,))],
        compiler_params=params(),
        name="pick",
    )(mine, in_hbm(parents), parent_row, in_hbm(states))
    corner_got = xor_permute(corner_out, 3)

    *near_outs, last_out, place, out_pick = pl.pallas_call(
        functools.partial(stage_kernel, blocks, normed_order),
        in_specs=[SCALARS, SCALARS, WHOLE, PLACED],
        out_specs=[PLACED] * (CAP + 1) + [WHOLE] * 2,
        out_shape=[pltpu.HBM(one_state, bf16)] * CAP
        + [pltpu.HBM((heads - extra, size, size), bf16)]
        + [
            jax.ShapeDtypeStruct((slots, 128), jnp.float32),
            jax.ShapeDtypeStruct((row_total, row_total + FARS * count), bf16),
        ],
        scratch_shapes=[
            pltpu.VMEM((CAP + 1, heads, size, size), bf16),
            pltpu.SemaphoreType.DMA((CAP + 1,)),
            pltpu.SemaphoreType.DMA((CAP + 1,)),
        ],
        compiler_params=params(),
        name="stage",
    )(mine, in_hbm(parents), parent_row, in_hbm(states))
    near_gots = [xor_permute(block, 1) for block in near_outs]
    last_got = xor_permute(last_out, 2)

    held = pl.pallas_call(
        hold_kernel,
        in_specs=[PLACED],
        out_specs=WHOLE,
        out_shape=pltpu.VMEM(states.shape, bf16),
        scratch_shapes=[pltpu.SemaphoreType.DMA((own_rows,))],
        compiler_params=params(),
        name="hold",
    )(in_hbm(states))

    weight = jnp.transpose(qkv_weight, (1, 0, 2))
    tied = {}

    def in_inputs(stage, parts):
        if stage == 0:
            *parts, tied["weight"], tied["pick"] = lax.optimization_barrier((*parts, weight, send_pick))
        if stage == 1:
            *parts, tied["place"] = lax.optimization_barrier((*parts, place))
        if stage == len(plan) - 1:
            *parts, tied["first"] = lax.optimization_barrier((*parts, first_got))
        return parts

    every_input = gather_all(local_columns, plan, in_inputs)
    pieces = pl.pallas_call(
        functools.partial(project_kernel, normed_order),
        in_specs=[SCALARS] + [WHOLE] * (2 + len(every_input)),
        out_specs=WHOLE,
        out_shape=jax.ShapeDtypeStruct((count * piece, columns), bf16),
        compiler_params=params(),
        name="project",
    )(mine, tied["weight"], tied["pick"], *every_input)

    def in_exchange(stage, parts):
        if stage == 1:
            *parts, tied["near"], tied["nearer"] = lax.optimization_barrier((*parts, *near_gots))
        return parts

    received = exchange_all(pieces.reshape(count, piece, columns), steps, in_exchange)
    if columns != size:
        every_piece = jnp.stack(received, 1).reshape(count, piece, columns)
        places = jnp.array([recv_order.index(d) for d in range(count)], int32)[jnp.arange(count, dtype=int32) ^ me]
        every_piece = jnp.take(every_piece, places, axis=0).transpose(1, 0, 2).reshape(piece, heads, size)
        received = [every_piece.transpose(1, 0, 2)]
        recv_order = None

    held, near_gots = in_vmem(held), [tied["near"], tied["nearer"]]
    sources = [held, *near_gots, tied["first"]]
    normed, by_head = pl.pallas_call(
        functools.partial(readout_kernel, recv_order, heads, len(sources)),
        in_specs=[SCALARS] * 2 + [WHOLE] * (3 + len(sources) + len(received)),
        out_specs=[WHOLE] * 2,
        out_shape=[
            jax.ShapeDtypeStruct((own_rows, normed_columns), bf16),
            jax.ShapeDtypeStruct((heads, piece, size), bf16),
        ],
        scratch_shapes=[pltpu.VMEM((heads, slots, size), jnp.float32)],
        compiler_params=params(),
        name="readout",
    )(mine, gate_bias, tied["place"], gate_weight, norm_gain.reshape(heads, size), *sources, *received)

    near_done, turned, values, terms = pl.pallas_call(
        functools.partial(near_update_kernel, recv_order, head_block, blocks),
        in_specs=[SCALARS] * 3 + [WHOLE] * 3,
        out_specs=[PLACED] + [WHOLE] * 3,
        out_shape=[
            pltpu.HBM(states.shape, bf16),
            jax.ShapeDtypeStruct((heads, size, slots), bf16),
            jax.ShapeDtypeStruct((heads, slots, size), jnp.float32),
            jax.ShapeDtypeStruct((2, heads, slots, size), jnp.float32),
        ],
        scratch_shapes=[pltpu.VMEM(states.shape, bf16), pltpu.SemaphoreType.DMA((own_rows,))],
        compiler_params=params(),
        name="near_update",
    )(mine, parents, gate_bias, by_head, gate_weight, held)

    far_block = math.gcd(extra, 4)

    def far_update(before, gots, entries, name, far_block=far_block):
        return pl.pallas_call(
            functools.partial(far_update_kernel, far_block, blocks, own_rows, entries),
            in_specs=[SCALARS] * 2 + [WHOLE] * (3 + len(gots)) + [PLACED],
            out_specs=PLACED,
            out_shape=jax.ShapeDtypeStruct(states.shape, bf16),
            scratch_shapes=[
                pltpu.VMEM((len(entries),) + one_state, bf16),
                pltpu.SemaphoreType.DMA((len(entries), heads // far_block)),
            ],
            input_output_aliases={5 + len(gots): 0},
            compiler_params=params(),
            name=name,
        )(mine, parents, tied["turned"], values, terms, *gots, before)

    def in_normed(stage, parts):
        if stage == 0:
            *parts, tied["rows"], tied["turned"] = lax.optimization_barrier((*parts, near_done, turned))
        if stage == 1:
            every = range(heads)
            entries = [(2, 0, 0, 0, every), (2, 1, 0, heads, every[:extra])]
            entries += [(3, rank, 1, rank * heads, every) for rank in range(CAP)]
            gots = [tied["first"], corner_got.reshape(CAP * heads, size, size)]
            entries += [(1, rank, 2 + rank, 0, every) for rank in range(CAP)]
            far_done = far_update(tied["rows"], gots + near_gots, entries, "far_update")
            *parts, tied["done"] = lax.optimization_barrier((*parts, far_done))
        return parts

    every_normed = gather_all(normed, plan, in_normed)
    layer_out = pl.pallas_call(
        functools.partial(output_kernel, own_rows),
        in_specs=[WHOLE] * (3 + len(every_normed)),
        out_specs=WHOLE,
        out_shape=jax.ShapeDtypeStruct((row_total, columns), bf16),
        scratch_shapes=[pltpu.VMEM(((normed_columns - width) // size, row_total, size), jnp.float32)],
        compiler_params=params(),
        name="output",
    )(local_columns, out_weight, out_pick, *every_normed)
    layer_out, last_got = lax.optimization_barrier((layer_out, last_got))
    final = far_update(tied["done"], [last_got], [(2, 1, 0, 0, range(extra, heads))], "last_update", math.gcd(extra, 2))
    return (layer_out[None], final)


def solution(mesh):
    placed = (
        P(None, "groups"),
        P(None, "groups", None),
        P(("groups", "rows"), None, None, None),
        P(None, "rows"),
        P(None, None, "rows"),
        P(),
        P(),
        P(),
        P(None, "rows"),
    )
    return jax.shard_map(
        per_device,
        mesh=mesh,
        in_specs=placed,
        out_specs=(P(None, "groups", "rows"), P(("groups", "rows"), None, None, None)),
        check_vma=False,
    )
```
